32 devices in a mesh: section: 2 (over x), wide: 16 (over z, y, core).
Axes of the slice: x: 2, y: 2, z: 4, core: 2. Of those that a mesh axis runs over, the one named last changes fastest.
Arguments:
- tokens: bfloat16 [8192, 768], P('wide'), may hold values from -6 to 6
- cotangent: bfloat16 [8192, 768], P('wide'), may hold values from -6 to 6
- lengths: int32 [32], P('wide'), may hold values from 16 to 256, as said below
- buckets: int32 [3, 8192], P(None, 'wide'), may hold values from 0 to 31
- in_proj: bfloat16 [2, 768, 2304], P('section'), may hold values from -0.21875 to 0.21875
- out_proj: bfloat16 [2, 768, 768], P('section'), may hold values from -0.625 to 0.625
- up_proj: bfloat16 [2, 768, 3072], P('section'), may hold values from -0.21875 to 0.21875
- down_proj: bfloat16 [2, 3072, 768], P('section'), may hold values from -0.109375 to 0.109375
- layout_tables: bfloat16 [2, 3, 12, 1024], P('section'), may hold values from -3 to 3
- norm_gains: float32 [2, 2, 768], P('section'), may hold values from 0.5 to 1.5
- offsets: float32 [2, 6, 768], P('section'), may hold values from -2 to 2
- hidden_bias: float32 [2, 3072], P('section'), may hold values from -2 to 2
Outputs:
- section_outputs: bfloat16 [2, 8192, 768], P('section', 'wide')
- section_input_grads: float32 [2, 8192, 768], P('section', 'wide')
- grad_in_proj: float32 [2, 768, 2304], P('section', 'wide')
- grad_out_proj: float32 [2, 768, 768], P('section', 'wide')
- grad_up_proj: float32 [2, 768, 3072], P('section', 'wide')
- grad_down_proj: float32 [2, 3072, 768], P('section', 'wide')
- grad_layout_tables: float32 [2, 3, 12, 1024], P('section', None, None, 'wide')
- grad_norm_gains: float32 [2, 2, 768], P('section', None, 'wide')
- grad_offsets: float32 [2, 6, 768], P('section', None, 'wide')
- grad_hidden_bias: float32 [2, 3072], P('section', 'wide')
The draws below stay inside these ranges and needn't reach their ends.
Inputs may be any that keep to these rules, and one draw needn't show every extreme that they name: `lengths`: page positions below a page's length hold real tokens; some page has exactly 256.
All inputs are finite; a program needn't handle non-finite values.
Results may differ from the reference program's by a relative error of at most 0.023.
Values may be sent and summed in bfloat16 or wider, within the bound.
A program may use at most 448 MiB of HBM per device.

```python
import jax
import jax.numpy as jnp
from jax import lax

D = 768
HEADS = 12
FF = 3072
LEN = 256
BUCKETS = 32
PAGES = 32
TOKENS = 8192


def draw_lengths(key, part):
    key = jax.random.fold_in(key, 11)
    first_key, second_key, third_key = jax.random.split(key, 3)
    starting = jax.random.randint(first_key, (PAGES,), LEN // 16, LEN // 4 + 1)
    doubling = jax.random.randint(second_key, (PAGES,), 0, 4)
    widened = jnp.minimum(jnp.left_shift(starting, doubling), LEN)
    chosen = jax.random.randint(third_key, (), 0, PAGES)
    return jnp.where(jnp.arange(PAGES) == chosen, LEN, widened).astype(jnp.int32)


def set_ends(drawn, rng, least, high):
    index_at = [jax.random.randint(jax.random.fold_in(rng, axis), (), 0, length) for axis, length in enumerate(drawn.shape)]
    longest = drawn.shape.index(max(drawn.shape))
    neighbour = index_at[:longest] + [(index_at[longest] + 1) % drawn.shape[longest]] + index_at[longest + 1:]
    return drawn.at[tuple(index_at)].set(least).at[tuple(neighbour)].set(high)


def with_spikes(values, rng, source, target, blocks, factor):
    def block_of(axis_at):
        return (jnp.arange(values.shape[axis_at]) // (values.shape[axis_at] // blocks)).reshape((-1,) + (1,) * (values.ndim - 1 - axis_at))

    one_side = jax.random.permutation(rng, blocks)[block_of(target)]
    second = (block_of(target) + blocks // 2) % blocks
    return jnp.where((block_of(source) == one_side) | (block_of(source) == second), factor * values, values)


def steps_of(own_key, dims, pieces, least, largest):
    loudness = 1.0
    for dim, blocks in pieces:
        heights = jax.random.uniform(jax.random.fold_in(jax.random.fold_in(own_key, 6), dim), (blocks,), jnp.float32, least / len(pieces), largest / len(pieces))
        loudness = loudness * jnp.repeat(jnp.exp(heights), dims[dim] // blocks).reshape((-1,) + (1,) * (len(dims) - 1 - dim))
    return loudness


def gaussian(key, extent, deviation, most, cuts=(), held_as=jnp.bfloat16):
    drawn = jax.random.normal(key, extent, jnp.float32) * deviation
    if len(cuts) > 0:
        drawn = steps_of(key, extent, cuts, -0.22, 0.18) * drawn
    return jnp.clip(drawn, min=-most, max=most).astype(held_as)


def heavy_noise(key, shape, scale, limit, cuts, heavy, kind=jnp.bfloat16):
    values = scale * jax.random.normal(key, shape, jnp.float32)
    if cuts:
        values = values * steps_of(key, shape, cuts, -0.22, 0.18)
    return jnp.clip(with_spikes(values, jax.random.fold_in(key, 3), *heavy), -limit, limit).astype(kind)


def setup_inputs(seed: int = 0) -> dict:
    key_of = jax.random.split(jax.random.key(seed), 13)
    return {
        "tokens": heavy_noise(key_of[0], (TOKENS, D), 1.0, 6.0, ((0, 16),), (0, 1, 16, 2.0)),
        "cotangent": heavy_noise(key_of[1], (TOKENS, D), 1.0, 6.0, ((0, 16),), (0, 1, 16, 2.0)),
        "lengths": draw_lengths(jax.random.fold_in(key_of[12], 71), 0),
        "buckets": set_ends(jax.random.randint(key_of[3], (3, TOKENS), 0, BUCKETS), jax.random.fold_in(key_of[3], 1), 0, BUCKETS - 1).astype(jnp.int32),
        "in_proj": gaussian(key_of[4], (2, D, 3 * D), D ** -0.5, 0.21875, ((0, 2),)),
        "out_proj": gaussian(key_of[5], (2, D, D), (D // 8) ** -0.5, 0.625, ((0, 2),)),
        "up_proj": gaussian(key_of[6], (2, D, FF), D ** -0.5, 0.21875, ((0, 2),)),
        "down_proj": gaussian(key_of[7], (2, FF, D), FF ** -0.5, 0.109375, ((0, 2),)),
        "layout_tables": gaussian(key_of[8], (2, 3, HEADS, BUCKETS * BUCKETS), 0.5, 3.0, ((0, 2),)),
        "norm_gains": jnp.clip(1.0 + 0.1 * jax.random.normal(key_of[9], (2, 2, D), jnp.float32), 0.5, 1.5),
        "offsets": gaussian(key_of[10], (2, 6, D), 0.3, 2.0, ((0, 2),), jnp.float32),
        "hidden_bias": gaussian(key_of[11], (2, FF), 0.3, 2.0, ((0, 2),), jnp.float32),
    }


@jax.custom_vjp
def low(v):
    return lax.optimization_barrier(v.astype(jnp.bfloat16)).astype(jnp.float32)

@jax.custom_vjp
def low_back(v):
    return v

def low_keep(v):
    return (low(v), None)

def low_pass(kept, grad):
    return (grad,)

def back_keep(v):
    return (v, None)

def back_low(kept, grad):
    return (low(grad),)
low.defvjp(low_keep, low_pass)
low_back.defvjp(back_keep, back_low)
epsilon = 1e-05
masked_score = -1000000000.0
highest = lax.Precision.HIGHEST

def product(left, right):
    return jnp.dot(left, right, precision=highest)

def normalize(values, gain, offset):
    centered = values - lax.optimization_barrier(jnp.mean(values, axis=-1, keepdims=True))
    spread = lax.optimization_barrier(jnp.mean(centered * centered, axis=-1, keepdims=True))
    return centered * lax.rsqrt(spread + epsilon) * gain + offset

def layer(inputs, key_live, bucket_ids, in_proj, out_proj, up_proj, down_proj, tables, gains, offsets, hidden_bias):
    page_count = key_live.shape[0]
    width = inputs.shape[1]
    head_count = tables.shape[1]
    head_size = width // head_count
    blank = jnp.zeros((width,), jnp.float32)
    projected = product(inputs, in_proj) + jnp.concatenate([offsets[0], blank, offsets[1]])
    projected = low_back(low(projected)).reshape(page_count, LEN, 3, head_count, head_size)
    query = projected[:, :, 0]
    keyed = projected[:, :, 1]
    valued = projected[:, :, 2]
    scores = jnp.einsum('gqhe,gkhe->ghqk', query, keyed, precision=highest) * head_size ** (-0.5)
    marks = bucket_ids.reshape(3, page_count, LEN)
    for axis_id in range(3):
        cells = marks[axis_id][:, :, None] * BUCKETS + marks[axis_id][:, None, :]
        scores = scores + jnp.moveaxis(tables[axis_id][:, cells], 0, 1)
    scores = low_back(scores)
    scores = jnp.where(key_live[:, None, None, :], scores, masked_score)
    peak = lax.optimization_barrier(jnp.max(scores, axis=-1, keepdims=True))
    raised = jnp.exp(scores - peak)
    attention = low(raised / lax.optimization_barrier(jnp.sum(raised, axis=-1, keepdims=True)))
    context = jnp.einsum('ghqk,gkhe->gqhe', attention, valued, precision=highest)
    context = low_back(low(context.reshape(page_count * LEN, width)))
    attended = low_back(product(context, out_proj) + offsets[2])
    normed = normalize(inputs + attended, gains[0], offsets[3])
    before = low_back(product(low(normed), up_proj) + hidden_bias)
    hidden = low(jax.nn.gelu(before, approximate=False))
    branch = low_back(product(hidden, down_proj) + offsets[4])
    return normalize(normed + branch, gains[1], offsets[5])

def both_layers(inputs, probe, key_live, bucket_ids, stacked):
    first = [array[0] for array in stacked]
    second = [array[1] for array in stacked]
    boundary = low_back(low(layer(inputs, key_live, bucket_ids, *first)) + probe)
    final = layer(boundary, key_live, bucket_ids, *second)
    return (boundary, final)

def reference(tokens, cotangent, lengths, buckets, in_proj, out_proj, up_proj, down_proj, layout_tables, norm_gains, offsets, hidden_bias):
    page_total = lengths.shape[0]
    width = tokens.shape[1]
    group = 1
    while group * 2 * LEN <= 4096 and page_total % (group * 2) == 0:
        group = group * 2
    rounds = page_total // group
    positions = jnp.arange(LEN, dtype=jnp.int32)
    key_live = positions[None, :] < lengths[:, None]
    live_groups = key_live.reshape(rounds, group, LEN)
    mark_groups = jnp.moveaxis(buckets.reshape(3, rounds, group * LEN), 1, 0)
    stacked = [array.astype(jnp.float32) for array in (in_proj, out_proj, up_proj, down_proj, layout_tables, norm_gains, offsets, hidden_bias)]
    inputs = tokens.astype(jnp.float32).reshape(rounds, group * LEN, width)
    probe = jnp.zeros((rounds, group * LEN, width), jnp.float32)

    def whole(inputs, probe, params):

        def visit(carry, items):
            return (carry, jax.checkpoint(both_layers)(items[0], items[1], items[2], items[3], params))
        _, outcome = lax.scan(visit, jnp.zeros((), jnp.float32), (inputs, probe, live_groups, mark_groups))
        return outcome
    outcome, pullback = jax.vjp(whole, inputs, probe, stacked)
    upstream = cotangent.astype(jnp.float32).reshape(rounds, group * LEN, width)
    grads = pullback((jnp.zeros_like(outcome[0]), upstream))
    sectioned = jnp.stack([outcome[0], outcome[1]]).reshape(2, page_total * LEN, width).astype(jnp.bfloat16)
    input_grads = jnp.stack([grads[0], grads[1]]).reshape(2, page_total * LEN, width)
    weight_grads = grads[2]
    return (sectioned, input_grads, weight_grads[0], weight_grads[1], weight_grads[2], weight_grads[3], weight_grads[4], weight_grads[5], weight_grads[6], weight_grads[7])
```

```python
import functools

import jax
import jax.numpy as jnp
from jax import lax
from jax.experimental import pallas as pl
from jax.experimental.pallas import tpu as pltpu
from jax.sharding import PartitionSpec as P

MESH = pl.DeviceIdType.MESH
BUCKETS = 32
LANES = 128
epsilon = 1e-05
masked_score = -1000000000.0
low = jnp.bfloat16
high = jnp.float32


def dot_nn(left, right):
    return jnp.dot(left, right, preferred_element_type=high)


def dot_nt(left, right):
    return lax.dot_general(left, right, (((1,), (1,)), ((), ())), preferred_element_type=high)


def normal_terms(values):
    below = 0.5 + 0.5 * lax.erf(values * 0.7071067811865476)
    return below, values * (0.3989422804014327 * jnp.exp(-0.5 * values * values))


def norm_rows(values):
    centered = values - jnp.mean(values, axis=-1, keepdims=True)
    spread = jnp.mean(centered * centered, axis=-1, keepdims=True)
    scale = lax.rsqrt(spread + epsilon)
    return centered * scale, scale


def norm_back(upstream, gain, normal, scale):
    scaled = upstream * gain
    middle = jnp.mean(scaled, axis=-1, keepdims=True)
    along = jnp.mean(scaled * normal, axis=-1, keepdims=True)
    return scale * (scaled - middle - normal * along)


def column_sum(values):
    return jnp.sum(values.astype(high), axis=0, keepdims=True)


def main_kernel(
    sizes,
    lengths, tokens, cotangent, onehot, spread, gains, offsets, bias,
    in_hbm, out_hbm, up_hbm, down_hbm,
    result, input_grads, left_hbm, right_hbm, tables, vectors, bias_grad,
    w_in, w_out, w_up, w_down, arrive, arrive_grad, sent_grad,
    qkv, chance, context, normal_one, scale_one, normed, normed_low, slope, hidden,
    normal_two, scale_two, picked, work, square, square_low, left, d_proj, d_att, d_before, d_branch,
    turned, turned_grad, back, d_context, d_first,
    load_sem, page_sem, left_sem, right_sem, send_sem, recv_sem,
):
    rows, width, heads, ff, pages = sizes
    size = width // heads
    pairs = heads // 2
    section = lax.axis_index("section")
    first = section == 0
    block = 64
    chunk = 512

    def peer_copy(src, dst, slot):
        return pltpu.make_async_remote_copy(
            src_ref=src, dst_ref=dst, send_sem=send_sem.at[slot], recv_sem=recv_sem.at[slot],
            device_id={"section": 1 - section}, device_id_type=MESH)

    def page_rows(page):
        return pl.ds(pl.multiple_of(page * rows, rows), rows)

    loads = [pltpu.make_async_copy(src, dst, load_sem.at[at]) for at, (src, dst) in enumerate(
        ((in_hbm, w_in), (out_hbm, w_out), (up_hbm, w_up), (down_hbm, w_down)))]

    def own_copy(page):
        return pltpu.make_async_copy(tokens.at[page_rows(page)], arrive.at[page], page_sem.at[page])

    def own_grad_copy(page):
        return pltpu.make_async_copy(cotangent.at[page_rows(page)], arrive_grad.at[page], page_sem.at[page])

    @pl.when(first)
    def _():
        for page in range(pages):
            own_copy(page).start()

    for load in loads:
        load.start()

    @pl.when(section == 1)
    def _():
        for page in range(pages):
            own_grad_copy(page).start()

    barrier = pltpu.get_barrier_semaphore()
    pl.semaphore_signal(barrier, inc=1, device_id={"section": 1 - section}, device_id_type=MESH)
    pl.semaphore_wait(barrier, 1)

    tables[...] = jnp.zeros_like(tables)
    vectors[...] = jnp.zeros_like(vectors)
    bias_grad[...] = jnp.zeros_like(bias_grad)

    def left_copy(page):
        return pltpu.make_async_copy(
            left, left_hbm.at[:, pl.ds(pl.multiple_of(page * rows, rows), rows)], left_sem)

    def right_copies(page):
        found, at = [], 0
        for slot, piece in enumerate((d_proj, d_att, d_before, d_branch)):
            cols = piece.shape[1]
            found.append(pltpu.make_async_copy(
                piece, right_hbm.at[page_rows(page), pl.ds(at, cols)], right_sem.at[slot]))
            at += cols
        return found

    lane = lax.broadcasted_iota(jnp.int32, (rows, LANES), 1)
    side = lane < size

    def result_copy(page):
        return peer_copy(result.at[page_rows(page)], arrive.at[page], page)

    def grad_copy(page):
        return peer_copy(sent_grad.at[page], arrive_grad.at[page], pages + page)

    def forward(page, carry):
        @pl.when(first)
        def _():
            own_copy(page).wait()

        @pl.when(section == 1)
        def _():
            result_copy(page).wait_recv()

        @pl.when(page == 0)
        def _():
            loads[0].wait()

        @pl.when(page > 0)
        def _():
            left_copy(page - 1).wait()

        layer_in = arrive[page]
        for part in range(3):
            cols = slice(part * width, (part + 1) * width)
            found = dot_nn(layer_in, w_in[:, cols])
            if part != 1:
                found = found + offsets[part // 2 : part // 2 + 1, :]
            qkv[page, :, cols] = found.astype(low)
        left[0:width, :] = layer_in.T
        mark = onehot[page_rows(page), :]
        picked[...] = dot_nn(mark, spread[...]).astype(low)
        live = lax.broadcasted_iota(jnp.int32, (1, rows), 1) < lengths[page]
        zero = jnp.zeros((rows, LANES), low)
        for pair in range(pairs):
            cols = slice(pair * LANES, (pair + 1) * LANES)
            query = qkv[page, :, cols] * jnp.asarray(size**-0.5, low)
            keyed = jnp.concatenate([qkv[page, :, width + pair * LANES : width + (pair + 1) * LANES], mark], axis=1)
            valued = qkv[page, :, 2 * width + pair * LANES : 2 * width + (pair + 1) * LANES]
            found = []
            for half in range(2):
                head = 2 * pair + half
                mine = jnp.where(side if half == 0 else ~side, query, zero)
                full = jnp.concatenate([mine, picked[:, head * LANES : (head + 1) * LANES]], axis=1)
                square[half] = dot_nt(full, keyed)
            for half in range(2):
                head = 2 * pair + half
                for at in range(0, rows, block):
                    scores = jnp.where(live, square[half, at : at + block], masked_score)
                    raised = jnp.exp(scores - jnp.max(scores, axis=-1, keepdims=True))
                    share = raised * (1.0 / jnp.sum(raised, axis=-1, keepdims=True))
                    chance[page, head, at : at + block] = share
                    square_low[half, at : at + block] = share.astype(low)
            for half in range(2):
                found.append(dot_nn(square_low[half], valued))
            context[:, cols] = jnp.where(side, found[0], found[1]).astype(low)
        left[width : 2 * width, :] = context[...].T

        @pl.when(page == 0)
        def _():
            loads[1].wait()

        work[...] = dot_nn(context[...], w_out[...])
        for at in range(0, rows, block):
            here = slice(at, at + block)
            summed = arrive[page, here].astype(high) + (work[here] + offsets[2:3])
            normal, scale = norm_rows(summed)
            normal_one[page, here] = normal
            scale_one[page, here] = scale
            shifted = normal * gains[0:1] + offsets[3:4]
            normed[here] = shifted
            normed_low[here] = shifted.astype(low)
        left[2 * width : 3 * width, :] = normed_low[...].T

        @pl.when(page == 0)
        def _():
            loads[2].wait()
            loads[3].wait()

        for at in range(0, ff, chunk):
            cols = slice(at, at + chunk)
            before = dot_nn(normed_low[...], w_up[:, cols]) + bias[:, cols]
            below, density = normal_terms(before)
            hidden[:, cols] = (before * below).astype(low)
            slope[page, :, cols] = (below + density).astype(slope.dtype)
        share = width // 16
        deep = ff // width
        spun = hidden[...].T
        for at in range(16):
            for part in range(deep):
                left[3 * width + part * width + at * share : 3 * width + part * width + (at + 1) * share] = (
                    spun[(at * deep + part) * share : (at * deep + part + 1) * share])
        work[...] = dot_nn(hidden[...], w_down[...])
        for at in range(0, rows, block):
            here = slice(at, at + block)
            normal, scale = norm_rows(normed[here] + (work[here] + offsets[4:5]))
            normal_two[page, here] = normal
            scale_two[page, here] = scale
            result[pl.ds(pl.multiple_of(page * rows + at, block), block), :] = (
                normal * gains[1:2] + offsets[5:6]).astype(low)

        @pl.when(first)
        def _():
            result_copy(page).start()

        left_copy(page).start()
        return carry

    lax.fori_loop(0, pages, forward, 0)

    def backward(page, carry):
        @pl.when(first)
        def _():
            grad_copy(page).wait_recv()

        @pl.when(section == 1)
        def _():
            own_grad_copy(page).wait()

        @pl.when(page > 0)
        def _():
            for copy in right_copies(page - 1):
                copy.wait()

        sums = [jnp.zeros((1, width), high) for _ in range(8)]
        for at in range(0, rows, block):
            here = slice(at, at + block)
            upstream = arrive_grad[page, here].astype(high)
            normal = normal_two[page, here]
            sums[1] += column_sum(upstream * normal)
            sums[7] += column_sum(upstream)
            d_second = norm_back(upstream, gains[1:2], normal, scale_two[page, here])
            d_first[here] = d_second
            branch = d_second.astype(low)
            sums[6] += column_sum(branch)
            d_branch[here] = branch
        for at in range(0, ff, chunk):
            cols = slice(at, at + chunk)
            d_hidden = dot_nt(d_branch[...], w_down[cols, :])
            d_chunk = (d_hidden * slope[page, :, cols].astype(high)).astype(low)
            d_before[:, cols] = d_chunk
            bias_grad[:, cols] += column_sum(d_chunk)
        work[...] = dot_nt(d_before[...], w_up[...])
        for at in range(0, rows, block):
            here = slice(at, at + block)
            d_normed = d_first[here] + work[here]
            normal = normal_one[page, here]
            sums[0] += column_sum(d_normed * normal)
            sums[5] += column_sum(d_normed)
            found = norm_back(d_normed, gains[0:1], normal, scale_one[page, here])
            d_first[here] = found
            attended = found.astype(low)
            sums[4] += column_sum(attended)
            d_att[here] = attended
        d_context[...] = dot_nt(d_att[...], w_out[...]).astype(low)
        turned[...] = qkv[page, :, 0:width].T
        turned_grad[...] = d_context[...].T
        mark = onehot[page_rows(page), :]
        mark_turned = mark.T
        zero = jnp.zeros((rows, LANES), low)
        scaling = size**-0.5
        for pair in range(pairs):
            cols = slice(pair * LANES, (pair + 1) * LANES)
            keyed = jnp.concatenate([qkv[page, :, width + pair * LANES : width + (pair + 1) * LANES], mark], axis=1)
            valued = qkv[page, :, 2 * width + pair * LANES : 2 * width + (pair + 1) * LANES]
            given = d_context[:, cols]
            for half in range(2):
                mine = jnp.where(side if half == 0 else ~side, given, zero)
                square[half] = dot_nt(mine, valued)
            found = []
            for half in range(2):
                head = 2 * pair + half
                for at in range(0, rows, block):
                    share = chance[page, head, at : at + block]
                    both = share * square[half, at : at + block]
                    d_scores = both - share * jnp.sum(both, axis=-1, keepdims=True)
                    square_low[half, at : at + block] = d_scores.astype(low)
            for half in range(2):
                head = 2 * pair + half
                slim = slice(head * size, (head + 1) * size)
                both = dot_nn(square_low[half], keyed)
                found.append(both[:, :LANES])
                rest = both[:, LANES:]
                upper = rest.astype(low)
                lower = (rest - upper.astype(high)).astype(low)
                crossed = dot_nn(mark_turned, jnp.concatenate([upper, lower], axis=1))
                crossed = crossed[:, :LANES] + crossed[:, LANES:]
                place = lax.broadcasted_iota(jnp.int32, (BUCKETS, LANES), 1)
                tables[head] += jnp.where(
                    place < BUCKETS, crossed[:BUCKETS],
                    jnp.where(place < 2 * BUCKETS, crossed[BUCKETS : 2 * BUCKETS], crossed[2 * BUCKETS : 3 * BUCKETS]))
                back[slim, :] = dot_nn(turned[slim, :], square_low[half]) * scaling
                back[slice(width + head * size, width + (head + 1) * size), :] = dot_nn(
                    turned_grad[slim, :], chance[page, head].astype(low))
            d_proj[:, cols] = (jnp.where(side, found[0], found[1]) * scaling).astype(low)
        d_proj[:, width:] = back[...].astype(low).T
        sums[2] += column_sum(d_proj[:, 0:width])
        sums[3] += column_sum(d_proj[:, 2 * width :])
        for row, value in enumerate(sums):
            vectors[row : row + 1, :] += value
        work[...] = dot_nt(d_proj[...], w_in[...])
        for at in range(0, rows, block):
            here = slice(at, at + block)
            d_in = d_first[here] + work[here]
            narrow = d_in.astype(low)
            sent_grad[page, here] = narrow
            input_grads[pl.ds(pl.multiple_of(page * rows + at, block), block), :] = jnp.where(
                first, d_in, narrow.astype(high))

        @pl.when(section == 1)
        def _():
            grad_copy(page).start()

        for copy in right_copies(page):
            copy.start()
        return carry

    lax.fori_loop(0, pages, backward, 0)
    left_copy(pages - 1).wait()
    for copy in right_copies(pages - 1):
        copy.wait()
    for page in range(pages):
        @pl.when(first)
        def _():
            result_copy(page).wait_send()

        @pl.when(section == 1)
        def _():
            grad_copy(page).wait_send()


def both_passes(tokens, cotangent, lengths, onehot, spread, params):
    in_proj, out_proj, up_proj, down_proj, gains, offsets, bias, heads = params
    pages = lengths.shape[0]
    rows = tokens.shape[0] // pages
    width, ff = up_proj.shape
    sizes = (rows, width, heads, ff, pages)
    VM = pltpu.VMEM
    here, there = pl.BlockSpec(memory_space=pltpu.VMEM), pl.BlockSpec(memory_space=pl.ANY)
    scratch = [
        VM(in_proj.shape, low), VM(out_proj.shape, low), VM(up_proj.shape, low), VM(down_proj.shape, low),
        VM((pages, rows, width), low), VM((pages, rows, width), low), VM((pages, rows, width), low),
        VM((pages, rows, 3 * width), low),
        VM((pages, heads, rows, rows), high),
        VM((rows, width), low),
        VM((pages, rows, width), high), VM((pages, rows, 1), high),
        VM((rows, width), high), VM((rows, width), low),
        VM((pages, rows, ff), high),
        VM((rows, ff), low),
        VM((pages, rows, width), high), VM((pages, rows, 1), high),
        VM((rows, heads * LANES), low),
        VM((rows, width), high),
        VM((2, rows, rows), high), VM((2, rows, rows), low),
        VM((3 * width + ff, rows), low),
        VM((rows, 3 * width), low), VM((rows, width), low), VM((rows, ff), low), VM((rows, width), low),
        VM((width, rows), low), VM((width, rows), low), VM((2 * width, rows), high),
        VM((rows, width), low), VM((rows, width), high),
        pltpu.SemaphoreType.DMA((4,)), pltpu.SemaphoreType.DMA((pages,)), pltpu.SemaphoreType.DMA,
        pltpu.SemaphoreType.DMA((4,)), pltpu.SemaphoreType.DMA((2 * pages,)), pltpu.SemaphoreType.DMA((2 * pages,)),
    ]
    return pl.pallas_call(
        functools.partial(main_kernel, sizes),
        out_shape=(
            jax.ShapeDtypeStruct(tokens.shape, low),
            jax.ShapeDtypeStruct(tokens.shape, high),
            jax.ShapeDtypeStruct((3 * width + ff, pages * rows), low),
            jax.ShapeDtypeStruct((pages * rows, 5 * width + ff), low),
            jax.ShapeDtypeStruct((heads, BUCKETS, LANES), high),
            jax.ShapeDtypeStruct((8, width), high),
            jax.ShapeDtypeStruct((1, ff), high),
        ),
        in_specs=[pl.BlockSpec(memory_space=pltpu.SMEM), there, there, here, here, here, here, here] + [there] * 4,
        out_specs=(here, here, there, there, here, here, here),
        scratch_shapes=scratch,
        compiler_params=pltpu.CompilerParams(
            collective_id=0, has_side_effects=True, vmem_limit_bytes=63 * 2**20),
    )(lengths, tokens, cotangent, onehot, spread, gains, offsets, bias[None], in_proj, out_proj, up_proj, down_proj)


def marks_of(buckets):
    levels = jnp.arange(LANES, dtype=jnp.int32)
    own = jnp.where(levels < BUCKETS, buckets[0][:, None], jnp.where(levels < 2 * BUCKETS, buckets[1][:, None], buckets[2][:, None]))
    return jnp.logical_and(own == levels % BUCKETS, levels < 3 * BUCKETS).astype(low)


def spread_of(layout):
    axes, heads, _ = layout.shape
    grid = layout.reshape(axes, heads, BUCKETS, BUCKETS)
    placed = [
        jnp.pad(grid[a].transpose(1, 0, 2), ((0, 0), (0, 0), (a * BUCKETS, LANES - (a + 1) * BUCKETS)))
        for a in range(axes)
    ]
    placed.append(jnp.zeros_like(placed[0]))
    return jnp.concatenate(placed, axis=0).reshape(LANES, heads * LANES)


LAGS = (0, 1, 7, 10, 13)


def left_of(at):
    return jnp.where(at < 9, 0, jnp.where(at < 12, 1, jnp.where(at < 24, 2, 3 + (at - 24) // 3)))


def right_of(at):
    return jnp.where(at < 24, at, 24 + at % 3)


def rs_kernel(
    count, levels, rows, cols, lags, compute,
    xt_ref, dy_ref, small_ref, out_ref, small_out_ref,
    dw, k1, k2, k3, s0, s1, s2, s3, r0, r1, r2, r3, ssem, rsem,
    ks0, ks1, ks2, ss0, ss1, ss2, ss3, sr0, sr1, sr2, sr3, sssem, srsem,
):
    me = lax.axis_index("wide")
    keeps, sends, recvs = (dw, k1, k2, k3), (s0, s1, s2, s3), (r0, r1, r2, r3)
    skeeps, ssends, srecvs = (small_ref, ks0, ks1, ks2), (ss0, ss1, ss2, ss3), (sr0, sr1, sr2, sr3)
    bits = [(me // 2**level) % 2 for level in range(levels)]
    partners = [me + 2**level * (1 - 2 * bits[level]) for level in range(levels)]

    barrier = pltpu.get_barrier_semaphore()
    for partner in partners:
        pl.semaphore_signal(barrier, inc=1, device_id={"wide": partner}, device_id_type=MESH)
    pl.semaphore_wait(barrier, levels)

    def copy(level, at):
        return pltpu.make_async_remote_copy(
            src_ref=sends[level].at[at], dst_ref=recvs[level].at[at],
            send_sem=ssem.at[level, at], recv_sem=rsem.at[level, at],
            device_id={"wide": partners[level]}, device_id_type=MESH)

    def small_copy(level):
        return pltpu.make_async_remote_copy(
            src_ref=ssends[level], dst_ref=srecvs[level],
            send_sem=sssem.at[level], recv_sem=srsem.at[level],
            device_id={"wide": partners[level]}, device_id_type=MESH)

    def start(at):
        slot = at % keeps[0].shape[0]
        if compute:
            dw[slot] = jnp.dot(xt_ref[left_of(at)], dy_ref[right_of(at)],
                               preferred_element_type=jnp.float32).reshape(dw.shape[1:])
        half = 2 ** (levels - 1)
        for j in range(half):
            s0[at, j] = dw[slot, 2 * j + 1 - bits[0]].astype(s0.dtype)
        copy(0, at).start()

    def middle(level, at):
        copy(level - 1, at).wait_recv()
        half = 2 ** (levels - 1 - level)
        old = at % keeps[level - 1].shape[0]
        new = at % keeps[level].shape[0]
        before = bits[level - 1]
        for j in range(half):
            pick = 2 * j + 1 - bits[level]
            total = keeps[level - 1][old, 2 * pick + before] if level == 1 else keeps[level - 1][old, pick]
            sends[level][at, j] = (total + recvs[level - 1][at, pick].astype(jnp.float32)).astype(sends[level].dtype)
        copy(level, at).start()
        for j in range(half):
            pick = 2 * j + bits[level]
            total = keeps[level - 1][old, 2 * pick + before] if level == 1 else keeps[level - 1][old, pick]
            keeps[level][new, j] = total + recvs[level - 1][at, pick].astype(jnp.float32)

    def finish(at):
        copy(levels - 1, at).wait_recv()
        old = at % keeps[levels - 1].shape[0]
        columns = pl.ds(pl.multiple_of(at * cols, cols), cols)
        out_ref[:, columns] = keeps[levels - 1][old, 0] + recvs[levels - 1][at, 0].astype(jnp.float32)

    def small_stage(level):
        if level:
            small_copy(level - 1).wait_recv()
        if level == levels:
            small_out_ref[...] = skeeps[levels - 1][0] + srecvs[levels - 1][0]
            return
        half = 2 ** (levels - 1 - level)
        for kept in (0, 1):
            for j in range(half):
                pick = 2 * j + (bits[level] if kept else 1 - bits[level])
                if level == 0:
                    value = small_ref[pick]
                else:
                    at = 2 * pick + bits[0] if level == 1 else pick
                    value = skeeps[level - 1][at] + srecvs[level - 1][pick]
                if not kept:
                    ssends[level][j] = value
                elif level:
                    skeeps[level][j] = value
            if not kept:
                small_copy(level).start()

    def step(moment, carry):
        for level in range(levels + 1):
            due = moment - lags[level]

            @pl.when(jnp.logical_and(due >= 0, due < count))
            def _():
                at = count - 1 - due
                if level == 0:
                    start(at)
                elif level < levels:
                    middle(level, at)
                else:
                    finish(at)
        return carry

    lax.fori_loop(0, count // 2, step, 0)
    small_stage(0)
    small_stage(1)
    lax.fori_loop(count // 2, count, step, 0)
    small_stage(2)
    small_stage(3)
    small_stage(4)
    lax.fori_loop(count, count + lags[levels], step, 0)

    def drain(at, carry):
        for level in range(levels):
            copy(level, at).wait_send()
        return carry

    lax.fori_loop(0, count, drain, 0)
    for level in range(levels):
        small_copy(level).wait_send()


def reduce_grads(xt, dy, small, lags=LAGS, compute=True, count=36, levels=4, wire=jnp.bfloat16, cid=1):
    n = 2**levels
    deep = dy.shape[0]
    cols = dy.shape[1] // 27
    rows = 3 * cols // n
    xt = xt.reshape(7, 3 * cols, deep)
    dy = dy.reshape(deep, 27, cols).transpose(1, 0, 2)
    def ring(level):
        return lags[level + 1] - lags[level] + 1
    VM = pltpu.VMEM
    scratch = [VM((ring(0), n, rows, cols), jnp.float32)]
    scratch += [VM((ring(l), n >> (l + 1), rows, cols), jnp.float32) for l in (1, 2, 3)]
    scratch += [VM((count, n >> (l + 1), rows, cols), wire) for l in range(4)]
    scratch += [VM((count, n >> (l + 1), rows, cols), wire) for l in range(4)]
    scratch += [pltpu.SemaphoreType.DMA((levels, count))] * 2
    sm = small.shape[1:]
    scratch += [VM((n >> (l + 1),) + sm, jnp.float32) for l in (1, 2, 3)]
    scratch += [VM((n >> (l + 1),) + sm, jnp.float32) for l in range(4)] * 2
    scratch += [pltpu.SemaphoreType.DMA((levels,))] * 2
    return pl.pallas_call(
        functools.partial(rs_kernel, count, levels, rows, cols, lags, compute),
        out_shape=(jax.ShapeDtypeStruct((rows, count * cols), jnp.float32),
                   jax.ShapeDtypeStruct(sm, jnp.float32)),
        in_specs=[pl.BlockSpec(memory_space=pltpu.VMEM)] * 3,
        out_specs=(pl.BlockSpec(memory_space=pltpu.VMEM),) * 2,
        scratch_shapes=scratch,
        compiler_params=pltpu.CompilerParams(collective_id=cid, has_side_effects=True, vmem_limit_bytes=63 * 2**20),
    )(xt, dy, small)


def local(tokens, cotangent, lengths, buckets, in_proj, out_proj, up_proj, down_proj, layout_tables, norm_gains, offsets, hidden_bias):
    heads = layout_tables.shape[2]
    width, ff = up_proj.shape[1:]
    params = (in_proj[0], out_proj[0], up_proj[0], down_proj[0], norm_gains[0], offsets[0], hidden_bias[0], heads)
    result, input_grads, left, right, tables, vectors, bias_grad = both_passes(
        tokens, cotangent, lengths, marks_of(buckets), spread_of(layout_tables[0]), params)
    wide_count = lax.axis_size("wide")
    share, deep = width // wide_count, ff // width
    tables = tables[:, :, : 3 * BUCKETS].reshape(heads, BUCKETS, 3, BUCKETS).transpose(2, 0, 1, 3).reshape(3 * heads, -1)
    if wide_count == 16 and share % 16 == 0:
        small = jnp.concatenate(
            [
                tables.reshape(3 * heads, wide_count, -1).transpose(1, 0, 2).reshape(wide_count, -1),
                vectors.reshape(8, wide_count, -1).transpose(1, 0, 2).reshape(wide_count, -1),
                bias_grad.reshape(wide_count, -1),
            ],
            axis=1,
        )
        filled = small.shape[1]
        small = jnp.pad(small, ((0, 0), (0, -filled % 1024))).reshape(wide_count, -1, 128)
        grads, few = reduce_grads(left, right, small)
        few = few.reshape(-1)
        tables_size = 3 * heads * BUCKETS * BUCKETS // wide_count
        grad_tables = few[:tables_size].reshape(1, 3, heads, -1)
        vectors = few[tables_size : tables_size + 8 * share].reshape(1, 8, share)
        grad_hidden = few[tables_size + 8 * share : filled].reshape(1, -1)
        grad_in = grads[None, :, : 3 * width]
        grad_out = grads[None, :, 3 * width : 4 * width]
        grad_up = grads[None, :, 4 * width : 4 * width + ff]
        grad_down = grads[:, 4 * width + ff :].reshape(share, deep, width)
        grad_down = grad_down.transpose(1, 0, 2).reshape(1, deep * share, width)
    else:

        def scattered(value, dim):
            return lax.psum_scatter(value[None], "wide", scatter_dimension=dim, tiled=True)

        def product(rows_from, cols_from, cols):
            return dot_nn(left[rows_from : rows_from + width], right[:, cols_from : cols_from + cols])

        slim = width // 16
        grad_in = scattered(product(0, 0, 3 * width), 1)
        grad_out = scattered(product(width, 3 * width, width), 1)
        grad_up = scattered(product(2 * width, 4 * width, ff), 1)
        grad_down = dot_nn(left[3 * width :], right[:, 4 * width + ff :])
        grad_down = grad_down.reshape(deep, 16, slim, width).transpose(1, 0, 2, 3).reshape(ff, width)
        grad_down = scattered(grad_down, 1)
        grad_hidden = scattered(bias_grad[0], 1)
        grad_tables = scattered(tables.reshape(3, heads, -1), 3)
        vectors = scattered(vectors, 2)
    return (
        result[None],
        input_grads[None],
        grad_in,
        grad_out,
        grad_up,
        grad_down,
        grad_tables,
        vectors[:, :2],
        vectors[:, 2:],
        grad_hidden,
    )


def solution(mesh):
    placed = (
        P("wide", None),
        P("wide", None),
        P("wide"),
        P(None, "wide"),
        P("section", None, None),
        P("section", None, None),
        P("section", None, None),
        P("section", None, None),
        P("section", None, None, None),
        P("section", None, None),
        P("section", None, None),
        P("section", None),
    )
    return jax.shard_map(
        local,
        mesh=mesh,
        in_specs=placed,
        out_specs=(
            P("section", "wide", None),
            P("section", "wide", None),
            P("section", "wide", None),
            P("section", "wide", None),
            P("section", "wide", None),
            P("section", "wide", None),
            P("section", None, None, "wide"),
            P("section", None, "wide"),
            P("section", None, "wide"),
            P("section", "wide"),
        ),
        check_vma=False,
    )
```

```python
import functools

import jax
import jax.numpy as jnp
from jax import lax
from jax.experimental import pallas as pl
from jax.experimental.pallas import tpu as pltpu
from jax.sharding import PartitionSpec as P

MESH = pl.DeviceIdType.MESH
BUCKETS = 32
LANES = 128
epsilon = 1e-05
masked_score = -1000000000.0
low = jnp.bfloat16
high = jnp.float32


def dot_nn(left, right):
    return jnp.dot(left, right, preferred_element_type=high)


def dot_nt(left, right):
    return lax.dot_general(left, right, (((1,), (1,)), ((), ())), preferred_element_type=high)


def normal_terms(values):
    below = 0.5 + 0.5 * lax.erf(values * 0.7071067811865476)
    return below, values * (0.3989422804014327 * jnp.exp(-0.5 * values * values))


def norm_rows(values):
    centered = values - jnp.mean(values, axis=-1, keepdims=True)
    spread = jnp.mean(centered * centered, axis=-1, keepdims=True)
    scale = lax.rsqrt(spread + epsilon)
    return centered * scale, scale


def norm_back(upstream, gain, normal, scale):
    scaled = upstream * gain
    middle = jnp.mean(scaled, axis=-1, keepdims=True)
    along = jnp.mean(scaled * normal, axis=-1, keepdims=True)
    return scale * (scaled - middle - normal * along)


def column_sum(values):
    return jnp.sum(values.astype(high), axis=0, keepdims=True)


def main_kernel(
    sizes, exchange,
    lengths, tokens, cotangent, buckets, layout, gains, offsets, bias,
    in_hbm, out_hbm, up_hbm, down_hbm,
    result, input_grads, plain_hbm, pair_hbm, full_hbm, right_hbm, cross_hbm, vectors, bias_grad, near_branch,
    w_in, w_out, w_up, w_down, arrive, arrive_grad, sent_grad,
    qkv, chance, context, normal_one, scale_one, normed, normed_low, slope, hidden,
    normal_two, scale_two, picked, work, square, square_low, cross, d_proj, d_att, d_before, d_branch,
    turned, turned_grad, back, d_context, d_first, onehot, spread, near_hidden, spun,
    load_sem, page_sem, spun_sem, right_sem, send_sem, recv_sem, near_send, near_recv,
):
    rows, width, heads, ff, pages = sizes
    size = width // heads
    pairs = heads // 2
    section = lax.axis_index("section")
    first = section == 0
    block = 64
    chunk = 512
    me = lax.axis_index("wide")
    side_bit = (me // 2) % 2
    near = me + 2 - 4 * side_bit
    slim = width // 2

    def near_copies(page):
        found = []
        for slot in range(ff // width):
            at = pl.multiple_of(slot * width + (1 - side_bit) * slim, LANES)
            found.append((hidden.at[page, :, pl.ds(at, slim)], near_hidden.at[page, :, pl.ds(slot * slim, slim)]))
        found.append((d_branch.at[page], near_branch.at[page_rows(page)]))
        return [
            pltpu.make_async_remote_copy(
                src_ref=src, dst_ref=dst, send_sem=near_send.at[page, slot], recv_sem=near_recv.at[page, slot],
                device_id={"wide": near}, device_id_type=MESH)
            for slot, (src, dst) in enumerate(found)
        ]

    def peer_copy(src, dst, slot):
        return pltpu.make_async_remote_copy(
            src_ref=src, dst_ref=dst, send_sem=send_sem.at[slot], recv_sem=recv_sem.at[slot],
            device_id={"section": 1 - section}, device_id_type=MESH)

    def page_rows(page):
        return pl.ds(pl.multiple_of(page * rows, rows), rows)

    loads = [pltpu.make_async_copy(src, dst, load_sem.at[at]) for at, (src, dst) in enumerate(
        ((in_hbm, w_in), (out_hbm, w_out), (up_hbm, w_up), (down_hbm, w_down)))]

    def own_copy(page):
        return pltpu.make_async_copy(tokens.at[page_rows(page)], arrive.at[page], page_sem.at[page])

    def own_grad_copy(page):
        return pltpu.make_async_copy(cotangent.at[page_rows(page)], arrive_grad.at[page], page_sem.at[page])

    @pl.when(first)
    def _():
        for page in range(pages):
            own_copy(page).start()

    for load in loads:
        load.start()

    @pl.when(section == 1)
    def _():
        for page in range(pages):
            own_grad_copy(page).start()

    barrier = pltpu.get_barrier_semaphore()
    pl.semaphore_signal(barrier, inc=1, device_id={"section": 1 - section}, device_id_type=MESH)
    if exchange:
        pl.semaphore_signal(barrier, inc=1, device_id={"wide": near}, device_id_type=MESH)
    pl.semaphore_wait(barrier, 2 if exchange else 1)

    onehot[...] = marks_of(buckets).T
    spread_tables(layout, spread)
    vectors[...] = jnp.zeros_like(vectors)
    bias_grad[...] = jnp.zeros_like(bias_grad)

    share = width // 16
    pieces = ff // width
    both = pages * rows

    def plain_copy(block):
        return pltpu.make_async_copy(
            spun.at[block % 2], plain_hbm.at[pl.ds(block * width, width)], spun_sem.at[block % 2, 0])

    def turn_plain():
        for block, source in enumerate((arrive, context, normed_low)):
            if block > 1:
                plain_copy(block - 2).wait()
            for page in range(pages):
                spun[block % 2, :, page * rows : (page + 1) * rows] = source[page].T
            plain_copy(block).start()
        for block in (1, 2):
            plain_copy(block).wait()

    def slab_copies(block, slot, pair, far):
        found = []
        for core in range(2):
            for piece in range(pieces):
                source = spun.at[slot, pl.ds((core * pieces + piece) * share, share)]
                row = pl.multiple_of((2 * block + core) * share, share)
                if pair:
                    target = pair_hbm.at[piece, pl.ds(row, share), pl.ds(far * both, both)]
                else:
                    target = full_hbm.at[piece, pl.ds(row, share)]
                found.append(pltpu.make_async_copy(source, target, spun_sem.at[slot, core * pieces + piece]))
        return found

    def turn_slabs(count, pair, far):
        def one(block, carry):
            slot = block % 2

            @pl.when(block > 1)
            def _():
                for copy in slab_copies(block - 2, slot, pair, far):
                    copy.wait()

            for page in range(pages):
                if far:
                    slab = near_hidden[page, :, pl.ds(pl.multiple_of(block * slim, LANES), slim)]
                elif pair:
                    slab = hidden[page, :, pl.ds(pl.multiple_of(block * width + side_bit * slim, LANES), slim)]
                else:
                    slab = hidden[page, :, pl.ds(pl.multiple_of(block * slim, LANES), slim)]
                spun[slot, 0:slim, page * rows : (page + 1) * rows] = slab.T
            for copy in slab_copies(block, slot, pair, far):
                copy.start()
            return carry

        lax.fori_loop(0, count, one, 0)
        for block in (count - 2, count - 1):
            for copy in slab_copies(block, block % 2, pair, far):
                copy.wait()

    def right_copies(page):
        found, at = [], 0
        for slot, piece in enumerate((d_proj, d_att, d_before, d_branch.at[page])):
            cols = piece.shape[-1]
            found.append(pltpu.make_async_copy(
                piece, right_hbm.at[page_rows(page), pl.ds(at, cols)], right_sem.at[page if slot == 3 else pages + slot]))
            at += cols
        found.append(pltpu.make_async_copy(cross, cross_hbm.at[page_rows(page)], right_sem.at[pages + 4]))
        return found

    lane = lax.broadcasted_iota(jnp.int32, (rows, LANES), 1)
    side = lane < size

    def result_copy(page):
        return peer_copy(result.at[page_rows(page)], arrive.at[page], page)

    def grad_copy(page):
        return peer_copy(sent_grad.at[page], arrive_grad.at[page], pages + page)

    def forward(page, carry):
        @pl.when(first)
        def _():
            own_copy(page).wait()

        @pl.when(section == 1)
        def _():
            result_copy(page).wait_recv()

        @pl.when(page == 0)
        def _():
            loads[0].wait()

        layer_in = arrive[page]
        for part in range(3):
            cols = slice(part * width, (part + 1) * width)
            found = dot_nn(layer_in, w_in[:, cols])
            if part != 1:
                found = found + offsets[part // 2]
            qkv[page, :, cols] = found.astype(low)
        mark = onehot[page_rows(page), :]
        for head in range(heads):
            picked[:, head * LANES : (head + 1) * LANES] = dot_nn(mark, spread[head]).astype(low)
        live = lax.broadcasted_iota(jnp.int32, (1, rows), 1) < lengths[page]
        zero = jnp.zeros((rows, LANES), low)
        for pair in range(pairs):
            cols = slice(pair * LANES, (pair + 1) * LANES)
            query = qkv[page, :, cols] * jnp.asarray(size**-0.5, low)
            keyed = jnp.concatenate([qkv[page, :, width + pair * LANES : width + (pair + 1) * LANES], mark], axis=1)
            valued = qkv[page, :, 2 * width + pair * LANES : 2 * width + (pair + 1) * LANES]
            found = []
            for half in range(2):
                head = 2 * pair + half
                mine = jnp.where(side if half == 0 else ~side, query, zero)
                full = jnp.concatenate([mine, picked[:, head * LANES : (head + 1) * LANES]], axis=1)
                square[half] = dot_nt(full, keyed)
            for half in range(2):
                head = 2 * pair + half
                for at in range(0, rows, block):
                    scores = jnp.where(live, square[half, at : at + block], masked_score)
                    raised = jnp.exp(scores - jnp.max(scores, axis=-1, keepdims=True))
                    share = raised * (1.0 / jnp.sum(raised, axis=-1, keepdims=True))
                    chance[page, head, at : at + block] = share
                    square_low[half, at : at + block] = share.astype(low)
            for half in range(2):
                found.append(dot_nn(square_low[half], valued))
            context[page, :, cols] = jnp.where(side, found[0], found[1]).astype(low)

        @pl.when(page == 0)
        def _():
            loads[1].wait()

        work[...] = dot_nn(context[page], w_out[...])

        for at in range(0, rows, block):
            here = slice(at, at + block)
            summed = arrive[page, here].astype(high) + (work[here] + offsets[2])
            normal, scale = norm_rows(summed)
            normal_one[page, here] = normal
            scale_one[page, here] = scale
            shifted = normal * gains[0:1] + offsets[3]
            normed[here] = shifted
            normed_low[page, here] = shifted.astype(low)

        @pl.when(page == 0)
        def _():
            loads[2].wait()
            loads[3].wait()

        for at in range(0, ff, chunk):
            cols = slice(at, at + chunk)
            before = dot_nn(normed_low[page], w_up[:, cols]) + bias[:, cols]
            below, density = normal_terms(before)
            hidden[page, :, cols] = (before * below).astype(low)
            slope[page, :, cols] = (below + density).astype(slope.dtype)
        if exchange:
            @pl.when(first)
            def _():
                for copy in near_copies(page)[:-1]:
                    copy.start()

        work[...] = dot_nn(hidden[page], w_down[...])
        for at in range(0, rows, block):
            here = slice(at, at + block)
            normal, scale = norm_rows(normed[here] + (work[here] + offsets[4]))
            normal_two[page, here] = normal
            scale_two[page, here] = scale
            result[pl.ds(pl.multiple_of(page * rows + at, block), block), :] = (
                normal * gains[1:2] + offsets[5]).astype(low)

        @pl.when(first)
        def _():
            result_copy(page).start()

        return carry

    lax.fori_loop(0, pages, forward, 0)

    @pl.when(first)
    def _():
        turn_plain()
        if exchange:
            turn_slabs(ff // width, True, 0)
            for page in range(pages):
                for copy in near_copies(page)[:-1]:
                    copy.wait()
            turn_slabs(ff // width, True, 1)
        else:
            turn_slabs(2 * ff // width, False, 0)

    def backward(page, carry):
        @pl.when(first)
        def _():
            grad_copy(page).wait_recv()

        @pl.when(section == 1)
        def _():
            own_grad_copy(page).wait()

        sums = [jnp.zeros((1, width), high) for _ in range(8)]
        for at in range(0, rows, block):
            here = slice(at, at + block)
            upstream = arrive_grad[page, here].astype(high)
            normal = normal_two[page, here]
            sums[1] += column_sum(upstream * normal)
            sums[7] += column_sum(upstream)
            d_second = norm_back(upstream, gains[1:2], normal, scale_two[page, here])
            d_first[here] = d_second
            branch = d_second.astype(low)
            sums[6] += column_sum(branch)
            d_branch[page, here] = branch
        right_copies(page)[3].start()
        if exchange:
            @pl.when(first)
            def _():
                near_copies(page)[-1].start()


        @pl.when(page > 0)
        def _():
            right_copies(page - 1)[2].wait()

        for at in range(0, ff, chunk):
            cols = slice(at, at + chunk)
            d_hidden = dot_nt(d_branch[page], w_down[cols, :])
            d_chunk = (d_hidden * slope[page, :, cols].astype(high)).astype(low)
            d_before[:, cols] = d_chunk
            bias_grad[:, cols] += column_sum(d_chunk)
        right_copies(page)[2].start()
        work[...] = dot_nt(d_before[...], w_up[...])

        @pl.when(page > 0)
        def _():
            right_copies(page - 1)[1].wait()

        for at in range(0, rows, block):
            here = slice(at, at + block)
            d_normed = d_first[here] + work[here]
            normal = normal_one[page, here]
            sums[0] += column_sum(d_normed * normal)
            sums[5] += column_sum(d_normed)
            found = norm_back(d_normed, gains[0:1], normal, scale_one[page, here])
            d_first[here] = found
            attended = found.astype(low)
            sums[4] += column_sum(attended)
            d_att[here] = attended
        right_copies(page)[1].start()
        d_context[...] = dot_nt(d_att[...], w_out[...]).astype(low)
        turned[...] = qkv[page, :, 0:width].T
        turned_grad[...] = d_context[...].T
        mark = onehot[page_rows(page), :]
        zero = jnp.zeros((rows, LANES), low)
        scaling = size**-0.5

        @pl.when(page > 0)
        def _():
            right_copies(page - 1)[0].wait()

        @pl.when(page > 0)
        def _():
            right_copies(page - 1)[4].wait()

        for pair in range(pairs):
            cols = slice(pair * LANES, (pair + 1) * LANES)
            keyed = jnp.concatenate([qkv[page, :, width + pair * LANES : width + (pair + 1) * LANES], mark], axis=1)
            valued = qkv[page, :, 2 * width + pair * LANES : 2 * width + (pair + 1) * LANES]
            given = d_context[:, cols]
            for half in range(2):
                mine = jnp.where(side if half == 0 else ~side, given, zero)
                square[half] = dot_nt(mine, valued)
            found = []
            for half in range(2):
                head = 2 * pair + half
                for at in range(0, rows, block):
                    share = chance[page, head, at : at + block]
                    both = share * square[half, at : at + block]
                    d_scores = both - share * jnp.sum(both, axis=-1, keepdims=True)
                    square_low[half, at : at + block] = d_scores.astype(low)
            for half in range(2):
                head = 2 * pair + half
                slim = slice(head * size, (head + 1) * size)
                both = dot_nn(square_low[half], keyed)
                found.append(both[:, :LANES])
                rest = both[:, LANES:]
                upper = rest.astype(low)
                lower = (rest - upper.astype(high)).astype(low)
                cross[:, 2 * head * LANES : (2 * head + 1) * LANES] = upper
                cross[:, (2 * head + 1) * LANES : (2 * head + 2) * LANES] = lower
                back[slim, :] = dot_nn(turned[slim, :], square_low[half]) * scaling
                back[slice(width + head * size, width + (head + 1) * size), :] = dot_nn(
                    turned_grad[slim, :], chance[page, head].astype(low))
            d_proj[:, cols] = (jnp.where(side, found[0], found[1]) * scaling).astype(low)
        d_proj[:, width:] = back[...].astype(low).T
        sums[2] += column_sum(d_proj[:, 0:width])
        sums[3] += column_sum(d_proj[:, 2 * width :])
        for row, value in enumerate(sums):
            vectors[row : row + 1, :] += value
        right_copies(page)[0].start()
        right_copies(page)[4].start()
        work[...] = dot_nt(d_proj[...], w_in[...])
        for at in range(0, rows, block):
            here = slice(at, at + block)
            d_in = d_first[here] + work[here]
            narrow = d_in.astype(low)
            sent_grad[page, here] = narrow
            input_grads[pl.ds(pl.multiple_of(page * rows + at, block), block), :] = jnp.where(
                first, d_in, narrow.astype(high))

        @pl.when(section == 1)
        def _():
            grad_copy(page).start()

        return carry

    lax.fori_loop(0, pages, backward, 0)

    @pl.when(section == 1)
    def _():
        turn_plain()
        turn_slabs(2 * ff // width, False, 0)

    for page in range(pages):
        right_copies(page)[3].wait()
        if exchange:
            @pl.when(first)
            def _():
                near_copies(page)[-1].wait()

    for slot in (0, 1, 2, 4):
        right_copies(pages - 1)[slot].wait()
    for page in range(pages):
        @pl.when(first)
        def _():
            result_copy(page).wait_send()

        @pl.when(section == 1)
        def _():
            grad_copy(page).wait_send()


def both_passes(tokens, cotangent, lengths, buckets, layout, params, exchange):
    in_proj, out_proj, up_proj, down_proj, gains, offsets, bias, heads = params
    pages = lengths.shape[0]
    rows = tokens.shape[0] // pages
    width, ff = up_proj.shape
    sizes = (rows, width, heads, ff, pages)
    VM = pltpu.VMEM
    here, there = pl.BlockSpec(memory_space=pltpu.VMEM), pl.BlockSpec(memory_space=pl.ANY)
    scratch = [
        VM(in_proj.shape, low), VM(out_proj.shape, low), VM(up_proj.shape, low), VM(down_proj.shape, low),
        VM((pages, rows, width), low), VM((pages, rows, width), low), VM((pages, rows, width), low),
        VM((pages, rows, 3 * width), low),
        VM((pages, heads, rows, rows), high),
        VM((pages, rows, width), low),
        VM((pages, rows, width), high), VM((pages, rows, 1), high),
        VM((rows, width), high), VM((pages, rows, width), low),
        VM((pages, rows, ff), high),
        VM((pages, rows, ff), low),
        VM((pages, rows, width), high), VM((pages, rows, 1), high),
        VM((rows, heads * LANES), low),
        VM((rows, width), high),
        VM((2, rows, rows), high), VM((2, rows, rows), low),
        VM((rows, 2 * heads * LANES), low),
        VM((rows, 3 * width), low), VM((rows, width), low), VM((rows, ff), low), VM((pages, rows, width), low),
        VM((width, rows), low), VM((width, rows), low), VM((2 * width, rows), high),
        VM((rows, width), low), VM((rows, width), high),
        VM((pages * rows, LANES), low), VM((heads, LANES, LANES), low),
        VM((pages, rows, ff // 2), low), VM((2, width, pages * rows), low),
        pltpu.SemaphoreType.DMA((4,)), pltpu.SemaphoreType.DMA((pages,)), pltpu.SemaphoreType.DMA((2, 2 * ff // width)),
        pltpu.SemaphoreType.DMA((pages + 5,)), pltpu.SemaphoreType.DMA((2 * pages,)), pltpu.SemaphoreType.DMA((2 * pages,)),
        pltpu.SemaphoreType.DMA((pages, ff // width + 1)), pltpu.SemaphoreType.DMA((pages, ff // width + 1)),
    ]
    return pl.pallas_call(
        functools.partial(main_kernel, sizes, exchange),
        out_shape=(
            jax.ShapeDtypeStruct(tokens.shape, low),
            jax.ShapeDtypeStruct(tokens.shape, high),
            jax.ShapeDtypeStruct((3 * width, pages * rows), low),
            jax.ShapeDtypeStruct((ff // width, width // 2, 2 * pages * rows), low),
            jax.ShapeDtypeStruct((ff // width, width, pages * rows), low),
            jax.ShapeDtypeStruct((pages * rows, 5 * width + ff), low),
            jax.ShapeDtypeStruct((pages * rows, 2 * heads * LANES), low),
            jax.ShapeDtypeStruct((8, width), high),
            jax.ShapeDtypeStruct((1, ff), high),
            jax.ShapeDtypeStruct((pages * rows, width), low),
        ),
        in_specs=[pl.BlockSpec(memory_space=pltpu.SMEM), there, there, here, here, here, here, here] + [there] * 4,
        out_specs=(here, here, there, there, there, there, there, here, here, there),
        scratch_shapes=scratch,
        compiler_params=pltpu.CompilerParams(
            collective_id=0, has_side_effects=True, vmem_limit_bytes=63 * 2**20),
    )(lengths, tokens, cotangent, buckets, layout, gains, offsets, bias, in_proj, out_proj, up_proj, down_proj)


def marks_of(buckets):
    tokens = buckets.shape[1]
    level = lax.broadcasted_iota(jnp.int32, (BUCKETS, tokens), 0)
    rows = [jnp.where(buckets[axis : axis + 1, :] == level, 1.0, 0.0) for axis in range(3)]
    return jnp.concatenate(rows + [jnp.zeros((BUCKETS, tokens), high)], axis=0).astype(low)


def spread_tables(layout, spread):
    cells = BUCKETS * BUCKETS
    row = lax.broadcasted_iota(jnp.int32, (BUCKETS, cells), 0)
    own = lax.broadcasted_iota(jnp.int32, (BUCKETS, cells), 1) // BUCKETS == row
    cell = lax.broadcasted_iota(jnp.int32, (cells, LANES), 0) % BUCKETS
    place = lax.broadcasted_iota(jnp.int32, (cells, LANES), 1)
    heads = layout.shape[1]
    for axis in range(3):
        cellwise = layout[axis].astype(high)
        target = jnp.where(cell + axis * BUCKETS == place, 1.0, 0.0).astype(low)
        for head in range(heads):
            grid = jnp.where(own, cellwise[head : head + 1], 0.0).astype(low)
            spread[head, axis * BUCKETS : (axis + 1) * BUCKETS] = dot_nn(grid, target).astype(low)
    spread[:, 3 * BUCKETS :] = jnp.zeros((heads, LANES - 3 * BUCKETS, LANES), low)


def cross_tables(turned, cross):
    found = dot_nn(turned, cross)
    found = found[:, :LANES] + found[:, LANES:]
    place = lax.broadcasted_iota(jnp.int32, (BUCKETS, LANES), 1)
    return jnp.where(
        place < BUCKETS, found[:BUCKETS],
        jnp.where(place < 2 * BUCKETS, found[BUCKETS : 2 * BUCKETS], found[2 * BUCKETS : 3 * BUCKETS]))


LAGS = ((0, 2, 7, 12, 17), (0, 1, 3, 8, 13))


def down_turn(turn):
    return jnp.logical_or(turn == 35, jnp.logical_and(turn < 33, turn % 3 == 0))


def down_of(turn):
    return jnp.where(turn == 35, 11, turn // 3)


def place_of(turn):
    other = jnp.where(turn < 33, 2 * (turn // 3) + turn % 3 - 1, turn - 11)
    other = jnp.where(other < 12, other + 12, jnp.where(other < 15, other - 3, other - 15))
    return jnp.where(down_turn(turn), 24 + down_of(turn), other)


def left_of(at):
    return jnp.where(at < 9, 0, jnp.where(at < 12, 1, 2))


def rs_kernel(
    count, levels, rows, cols, lags,
    plain_hbm, pair_hbm, full_hbm, right_hbm, cross_hbm, near_branch, buckets, vectors, bias_grad,
    out_in, out_out, out_up, out_down, out_tables, out_gains, out_offsets, out_bias,
    left, left_pair, left_full, right, right_down, cross, tables, dw, k1, k2, k3, s0, s1, s2, s3, r0, r1, r2, r3, ssem, rsem, left_sem, right_sem, left_down_sem, right_down_sem, cross_sem,
    ks, ks0, ks1, ks2, ss0, ss1, ss2, ss3, sr0, sr1, sr2, sr3, sssem, srsem,
):
    me = lax.axis_index("wide")
    keeps, sends, recvs = (dw, k1, k2, k3), (s0, s1, s2, s3), (r0, r1, r2, r3)
    skeeps, ssends, srecvs = (ks, ks0, ks1, ks2), (ss0, ss1, ss2, ss3), (sr0, sr1, sr2, sr3)
    bits = [(me // 2**level) % 2 for level in range(levels)]
    partners = [me + 2**level * (1 - 2 * bits[level]) for level in range(levels)]
    width = rows * 2**levels

    section = lax.axis_index("section")
    first = section == 0
    depth = right.shape[1]

    def left_load(block):
        return pltpu.make_async_copy(
            plain_hbm.at[pl.ds(pl.multiple_of(block * width, width), width)], left.at[block], left_sem.at[block])

    def right_load(block):
        return pltpu.make_async_copy(
            right_hbm.at[:, pl.ds(pl.multiple_of(block * cols, cols), cols)], right.at[block], right_sem.at[block])

    def pair_load(piece):
        return pltpu.make_async_copy(pair_hbm.at[piece], left_pair.at[piece], left_down_sem.at[piece])

    def full_load(piece):
        return pltpu.make_async_copy(full_hbm.at[piece], left_full.at[piece], left_down_sem.at[piece])

    def right_down_load(col):
        here = pl.ds(pl.multiple_of((right.shape[0] + col) * cols, cols), cols)
        return pltpu.make_async_copy(right_hbm.at[:, here], right_down.at[col, pl.ds(0, depth)], right_down_sem.at[0, col])

    def near_load(col):
        there = pl.ds(pl.multiple_of(col * cols, cols), cols)
        return pltpu.make_async_copy(near_branch.at[:, there], right_down.at[col, pl.ds(depth, depth)], right_down_sem.at[1, col])

    cross_load = pltpu.make_async_copy(cross_hbm, cross, cross_sem)
    barrier = pltpu.get_barrier_semaphore()
    for partner in partners:
        pl.semaphore_signal(barrier, inc=1, device_id={"wide": partner}, device_id_type=MESH)

    @pl.when(first)
    def _():
        pair_load(0).start()
        near_load(0).start()

    @pl.when(section == 1)
    def _():
        full_load(0).start()

    right_down_load(0).start()
    left_load(2).start()
    for block in range(12, 16):
        right_load(block).start()
    for col in (1, 2):
        right_down_load(col).start()

    @pl.when(first)
    def _():
        for col in (1, 2):
            near_load(col).start()
        for piece in (1, 2, 3):
            pair_load(piece).start()

    @pl.when(section == 1)
    def _():
        for piece in (1, 2, 3):
            full_load(piece).start()

    for block in range(16, 24):
        right_load(block).start()
    cross_load.start()
    for block in (1, 0):
        left_load(block).start()
    for block in range(0, 12):
        right_load(block).start()
    pl.semaphore_wait(barrier, levels)

    def copy(step, at, partner):
        return pltpu.make_async_remote_copy(
            src_ref=sends[step].at[at], dst_ref=recvs[step].at[at],
            send_sem=ssem.at[step, at], recv_sem=rsem.at[step, at],
            device_id={"wide": partners[partner]}, device_id_type=MESH)

    def small_copy(step):
        return pltpu.make_async_remote_copy(
            src_ref=ssends[step], dst_ref=srecvs[step],
            send_sem=sssem.at[step], recv_sem=srsem.at[step],
            device_id={"wide": partners[step]}, device_id_type=MESH)

    def cross_head(head):
        here = pl.ds(pl.multiple_of(head * 2 * LANES, 2 * LANES), 2 * LANES)
        tables[head] = cross_tables(marks_of(buckets), cross[:, here])

    def paired(turn):
        return jnp.logical_and(first, down_turn(turn))

    def far_first(turn):
        return jnp.logical_and(section == 1, turn % 6 == 0)

    def start(turn):
        at = place_of(turn)
        slot = turn % dw.shape[0]
        down = down_of(turn)
        piece, col = down // 3, down % 3

        def take(value):
            dw[slot] = value.reshape(dw.shape[1:])
            for j in range(2 ** (levels - 1)):
                s0[turn, j] = dw[slot, 2 * j + 1 - bits[0]].astype(low)
            copy(0, turn, 0).start()

        @pl.when(jnp.logical_and(down_turn(turn), down < 3))
        def _():
            right_down_load(down).wait()

        @pl.when(paired(turn))
        def _():
            @pl.when(down < 3)
            def _():
                near_load(down).wait()

            @pl.when(col == 0)
            def _():
                pair_load(piece).wait()

            found = dot_nn(left_pair[piece], right_down[col])
            dw[slot, 0 : 2 ** (levels - 1)] = found.reshape((2 ** (levels - 1),) + dw.shape[2:])

        @pl.when(jnp.logical_and(section == 1, down_turn(turn)))
        def _():
            @pl.when(col == 0)
            def _():
                full_load(piece).wait()

            take(dot_nn(left_full[piece], right_down[col, 0:depth]))

        @pl.when(jnp.logical_not(down_turn(turn)))
        def _():
            right_load(at).wait()

            @pl.when(jnp.logical_or(at == 12, jnp.logical_or(at == 9, at == 0)))
            def _():
                left_load(left_of(at)).wait()

            take(dot_nn(left[left_of(at)], right[at]))

    def pass_on(step, at, partner, place, total):
        half = 2 ** (levels - 1 - step)
        new = at % keeps[step].shape[0]
        bit = bits[partner]

        def pick(j, value):
            return (j >> place << (place + 1)) + (j & (2**place - 1)) + value * 2**place

        for j in range(half):
            sends[step][at, j] = total(pick(j, 1 - bit)).astype(low)
        copy(step, at, partner).start()
        for j in range(half):
            keeps[step][new, j] = total(pick(j, bit))

    def second(at, kind):
        old = at % dw.shape[0]
        if kind == "paired":
            pass_on(1, at, 0, 0, lambda pick: dw[old, pick])
            return
        copy(0, at, 0).wait_recv()
        partner, place = (2, 1) if kind == "far" else (1, 0)
        pass_on(1, at, partner, place, lambda pick: dw[old, 2 * pick + bits[0]] + r0[at, pick].astype(high))

    def later(step, at, kind):
        copy(step - 1, at, 0).wait_recv()
        old = at % keeps[step - 1].shape[0]
        partner, place = ((3, 1) if step == 2 else (1, 0)) if kind == "far" else (step, 0)
        pass_on(step, at, partner, place, lambda pick: keeps[step - 1][old, pick] + recvs[step - 1][at, pick].astype(high))

    def finish(turn):
        copy(levels - 1, turn, levels - 1).wait_recv()
        old = turn % keeps[levels - 1].shape[0]
        value = keeps[levels - 1][old, 0] + recvs[levels - 1][turn, 0].astype(high)
        at = place_of(turn)

        def columns(first):
            return pl.ds(pl.multiple_of((at - first) * cols, cols), cols)

        @pl.when(at < 9)
        def _():
            out_in[0, :, columns(0)] = value

        @pl.when(jnp.logical_and(at >= 9, at < 12))
        def _():
            out_out[0, :, columns(9)] = value

        @pl.when(jnp.logical_and(at >= 12, at < 24))
        def _():
            out_up[0, :, columns(12)] = value

        @pl.when(at >= 24)
        def _():
            part, col = (at - 24) // 3, at % 3
            out_down[0, pl.ds(pl.multiple_of(part * rows, rows), rows), pl.ds(pl.multiple_of(col * cols, cols), cols)] = value

    def small_fill():
        heads = tables.shape[0]
        for part in range(2**levels):
            for head in range(heads):
                ks[part, 2 * head : 2 * head + 2] = tables[head, 2 * part : 2 * part + 2]
            ks[part, 2 * heads : 2 * heads + 8, 0:rows] = vectors[:, part * rows : (part + 1) * rows]
            for piece in range(4):
                at = (4 * part + piece) * rows
                ks[part, 2 * heads + piece : 2 * heads + piece + 1, rows : 2 * rows] = bias_grad[:, at : at + rows]

    def small_stage(step):
        if step:
            small_copy(step - 1).wait_recv()
        if step == levels:
            heads = tables.shape[0]
            ks[0] = skeeps[levels - 1][0] + srecvs[levels - 1][0]
            for axis in range(3):
                for i in range(2):
                    got = ks[0, pl.ds(i, heads, 2), :]
                    out_tables[axis, :, 0, i * BUCKETS : (i + 1) * BUCKETS] = got[:, axis * BUCKETS : (axis + 1) * BUCKETS]
            out_gains[0] = ks[0, 2 * heads : 2 * heads + 2, 0:rows]
            out_offsets[:, 0] = ks[0, 2 * heads + 2 : 2 * heads + 8, 0:rows]
            for piece in range(4):
                out_bias[:, piece * rows : (piece + 1) * rows] = ks[0, 2 * heads + piece : 2 * heads + piece + 1, rows : 2 * rows]
            return
        half = 2 ** (levels - 1 - step)

        def total(pick):
            if step == 0:
                return ks[pick]
            return skeeps[step - 1][2 * pick + bits[0] if step == 1 else pick] + srecvs[step - 1][pick]

        for j in range(half):
            ssends[step][j] = total(2 * j + 1 - bits[step])
        small_copy(step).start()
        if step:
            for j in range(half):
                skeeps[step][j] = total(2 * j + bits[step])

    def step_at(moment, carry):
        @pl.when(moment == 5)
        def _():
            cross_load.wait()

        @pl.when(jnp.logical_and(moment >= 5, moment < 5 + tables.shape[0]))
        def _():
            cross_head(moment - 5)

        def due(at):
            return jnp.logical_and(at >= 0, at < count)

        @pl.when(due(moment))
        def _():
            start(moment)

        for step in range(1, levels + 1):
            near_at, pair_at = moment - lags[0][step], moment - lags[1][step]
            plain_due = jnp.logical_and(due(near_at), jnp.logical_not(paired(near_at)))
            pair_due = jnp.logical_and(due(pair_at), paired(pair_at))
            if step == 1:
                @pl.when(pair_due)
                def _():
                    second(pair_at, "paired")
            elif step < levels:
                @pl.when(pair_due)
                def _():
                    later(step, pair_at, "paired")
            else:
                @pl.when(pair_due)
                def _():
                    finish(pair_at)

                @pl.when(plain_due)
                def _():
                    finish(near_at)
                continue
            for kind in ("plain", "far"):
                chosen = far_first(near_at) if kind == "far" else jnp.logical_not(far_first(near_at))

                @pl.when(jnp.logical_and(plain_due, chosen))
                def _():
                    second(near_at, kind) if step == 1 else later(step, near_at, kind)
        return carry

    ks[...] = jnp.zeros_like(ks)
    lax.fori_loop(0, 19, step_at, 0)
    small_fill()
    small_stage(0)
    lax.fori_loop(19, 22, step_at, 0)
    small_stage(1)
    lax.fori_loop(22, count, step_at, 0)
    small_stage(2)
    small_stage(3)
    small_stage(4)
    lax.fori_loop(count, count + lags[0][levels], step_at, 0)

    def drain(at, carry):
        @pl.when(jnp.logical_not(paired(at)))
        def _():
            copy(0, at, 0).wait_send()

        for step in range(1, levels):
            copy(step, at, step).wait_send()
        return carry

    lax.fori_loop(0, count, drain, 0)
    for step in range(levels):
        small_copy(step).wait_send()


def reduce_grads(plain, pair, full, right, cross, near_branch, buckets, vectors, bias_grad, count=36, levels=4, lags=LAGS):
    n = 2**levels
    depth, total = right.shape
    width = vectors.shape[1]
    cols, rows = 256, width // n
    heads = cross.shape[1] // (2 * LANES)
    ff = bias_grad.shape[1]
    others = total // cols - width // cols

    def ring(step):
        return max(lag[step + 1] for lag in lags) - min(lag[step] for lag in lags) + 1

    VM = pltpu.VMEM
    scratch = [VM((3, width, depth), low), VM(pair.shape, low), VM(full.shape, low)]
    scratch += [VM((others, depth, cols), low), VM((width // cols, 2 * depth, cols), low)]
    scratch += [VM(cross.shape, low), VM((heads, BUCKETS, LANES), high)]
    scratch += [VM((ring(0), n, rows, cols), high)]
    scratch += [VM((ring(step), n >> (step + 1), rows, cols), high) for step in (1, 2, 3)]
    scratch += [VM((count, n >> (step + 1), rows, cols), low) for step in range(4)] * 2
    scratch += [pltpu.SemaphoreType.DMA((levels, count))] * 2
    scratch += [pltpu.SemaphoreType.DMA((3,)), pltpu.SemaphoreType.DMA((others,))]
    scratch += [pltpu.SemaphoreType.DMA((ff // width,)), pltpu.SemaphoreType.DMA((2, width // cols)), pltpu.SemaphoreType.DMA]
    few = (2 * heads + 8, LANES)
    scratch += [VM((n,) + few, high)]
    scratch += [VM((n >> (step + 1),) + few, high) for step in (1, 2, 3)]
    scratch += [VM((n >> (step + 1),) + few, high) for step in range(4)] * 2
    scratch += [pltpu.SemaphoreType.DMA((levels,))] * 2
    here, there = pl.BlockSpec(memory_space=pltpu.VMEM), pl.BlockSpec(memory_space=pl.ANY)
    shapes = (
        (1, rows, 3 * width), (1, rows, width), (1, rows, ff), (1, ff // n, width),
        (3, heads, 1, 2 * BUCKETS), (1, 2, rows), (6, 1, rows), (1, ff // n),
    )
    return pl.pallas_call(
        functools.partial(rs_kernel, count, levels, rows, cols, lags),
        out_shape=tuple(jax.ShapeDtypeStruct(shape, high) for shape in shapes),
        in_specs=[there] * 6 + [here] * 3,
        out_specs=(here,) * len(shapes),
        scratch_shapes=scratch,
        compiler_params=pltpu.CompilerParams(
            collective_id=1, has_side_effects=True, vmem_limit_bytes=63 * 2**20),
    )(plain, pair, full, right, cross, near_branch, buckets, vectors, bias_grad)


def settle_kernel(count, *refs):
    sources, targets, held, sem = refs[:count], refs[count : 2 * count], refs[2 * count : 3 * count], refs[3 * count]
    copies = [
        (pltpu.make_async_copy(sources[at], held[at], sem.at[0, at]), pltpu.make_async_copy(held[at], targets[at], sem.at[1, at]))
        for at in range(count)
    ]
    for fetch, _ in copies:
        fetch.start()
    for fetch, put in copies:
        fetch.wait()
        put.start()
    for _, put in copies:
        put.wait()


def settle(arrays):
    there = pl.BlockSpec(memory_space=pl.ANY)
    return pl.pallas_call(
        functools.partial(settle_kernel, len(arrays)),
        out_shape=tuple(jax.ShapeDtypeStruct(array.shape, array.dtype) for array in arrays),
        in_specs=[there] * len(arrays),
        out_specs=(there,) * len(arrays),
        scratch_shapes=[pltpu.VMEM(array.shape, array.dtype) for array in arrays] + [pltpu.SemaphoreType.DMA((2, len(arrays)))],
        compiler_params=pltpu.CompilerParams(vmem_limit_bytes=63 * 2**20),
    )(*arrays)


def local(tokens, cotangent, lengths, buckets, in_proj, out_proj, up_proj, down_proj, layout_tables, norm_gains, offsets, hidden_bias):
    heads = layout_tables.shape[2]
    width, ff = up_proj.shape[1:]
    shifts = jnp.transpose(offsets, (1, 0, 2))
    params = (in_proj[0], out_proj[0], up_proj[0], down_proj[0], norm_gains[0], shifts, hidden_bias, heads)
    wide_count = lax.axis_size("wide")
    result, input_grads, plain, pair, full, right, cross, vectors, bias_grad, near_branch = both_passes(
        tokens, cotangent, lengths, buckets, layout_tables[0], params, wide_count == 16)
    share = width // wide_count
    if wide_count == 16 and share % 16 == 0:
        found = reduce_grads(plain, pair, full, right, cross, near_branch, buckets, vectors, bias_grad)
        found = settle((result[None], input_grads[None]) + found)
        return found[:6] + (jnp.transpose(found[6], (2, 0, 1, 3)), found[7], jnp.transpose(found[8], (1, 0, 2)), found[9])
    else:

        def scattered(value, dim):
            return lax.psum_scatter(value[None], "wide", scatter_dimension=dim, tiled=True)

        def product(rows_from, cols_from, cols):
            return dot_nn(plain[rows_from : rows_from + width], right[:, cols_from : cols_from + cols])

        grad_in = scattered(product(0, 0, 3 * width), 1)
        grad_out = scattered(product(width, 3 * width, width), 1)
        grad_up = scattered(product(2 * width, 4 * width, ff), 1)
        grad_down = dot_nn(full.reshape(ff, -1), right[:, 4 * width + ff :])
        grad_down = grad_down.reshape(ff // width, 16, -1, width).transpose(1, 0, 2, 3).reshape(ff, width)
        grad_down = scattered(grad_down, 1)
        grad_hidden = scattered(bias_grad[0], 1)
        turned = marks_of(buckets)
        tables = jnp.stack([
            cross_tables(turned, cross[:, 2 * head * LANES : 2 * (head + 1) * LANES]) for head in range(heads)])
        tables = tables[:, :, : 3 * BUCKETS].reshape(heads, BUCKETS, 3, BUCKETS).transpose(2, 0, 1, 3)
        grad_tables = scattered(tables.reshape(3, heads, -1), 3)
        vectors = scattered(vectors, 2)
        grad_gains, grad_offsets = vectors[:, :2], vectors[:, 2:]
    return (
        result[None],
        input_grads[None],
        grad_in,
        grad_out,
        grad_up,
        grad_down,
        grad_tables,
        grad_gains,
        grad_offsets,
        grad_hidden,
    )


def solution(mesh):
    placed = (
        P("wide", None),
        P("wide", None),
        P("wide"),
        P(None, "wide"),
        P("section", None, None),
        P("section", None, None),
        P("section", None, None),
        P("section", None, None),
        P("section", None, None, None),
        P("section", None, None),
        P("section", None, None),
        P("section", None),
    )
    return jax.shard_map(
        local,
        mesh=mesh,
        in_specs=placed,
        out_specs=(
            P("section", "wide", None),
            P("section", "wide", None),
            P("section", "wide", None),
            P("section", "wide", None),
            P("section", "wide", None),
            P("section", "wide", None),
            P("section", None, None, "wide"),
            P("section", None, "wide"),
            P("section", None, "wide"),
            P("section", "wide"),
        ),
        check_vma=False,
    )
```

```python
import functools

import jax
import jax.numpy as jnp
from jax import lax
from jax.experimental import pallas as pl
from jax.experimental.pallas import tpu as pltpu
from jax.sharding import PartitionSpec as P

MESH = pl.DeviceIdType.MESH
BUCKETS = 32
LANES = 128
epsilon = 1e-05
masked_score = -1000000000.0
low = jnp.bfloat16
high = jnp.float32


def dot_nn(left, right):
    return jnp.dot(left, right, preferred_element_type=high)


def dot_nt(left, right):
    return lax.dot_general(left, right, (((1,), (1,)), ((), ())), preferred_element_type=high)


def normal_terms(values):
    below = 0.5 + 0.5 * lax.erf(values * 0.7071067811865476)
    return below, values * (0.3989422804014327 * jnp.exp(-0.5 * values * values))


def norm_rows(values):
    centered = values - jnp.mean(values, axis=-1, keepdims=True)
    spread = jnp.mean(centered * centered, axis=-1, keepdims=True)
    scale = lax.rsqrt(spread + epsilon)
    return centered * scale, scale


def norm_back(upstream, gain, normal, scale):
    scaled = upstream * gain
    middle = jnp.mean(scaled, axis=-1, keepdims=True)
    along = jnp.mean(scaled * normal, axis=-1, keepdims=True)
    return scale * (scaled - middle - normal * along)


def column_sum(values):
    return jnp.sum(values.astype(high), axis=0, keepdims=True)


def main_kernel(
    sizes, exchange,
    lengths, tokens, cotangent, buckets, layout, gains, offsets, bias,
    in_hbm, out_hbm, up_hbm, down_hbm,
    result, input_grads, plain_hbm, pair_hbm, full_hbm, right_hbm, cross_hbm, vectors, bias_grad, near_branch,
    w_in, w_out, w_up, w_down, arrive, arrive_grad, sent_grad,
    qkv, chance, context, normal_one, scale_one, normed, normed_low, slope, hidden,
    normal_two, scale_two, picked, work, square, square_low, cross, d_proj, d_att, d_before, d_branch,
    turned, turned_grad, back, d_context, d_first, onehot, spread, near_hidden, spun,
    load_sem, page_sem, spun_sem, right_sem, send_sem, recv_sem, near_send, near_recv,
):
    rows, width, heads, ff, pages = sizes
    size = width // heads
    pairs = heads // 2
    section = lax.axis_index("section")
    first = section == 0
    block = 64
    chunk = 512
    me = lax.axis_index("wide")
    side_bit = (me // 2) % 2
    near = me + 2 - 4 * side_bit
    slim = width // 2

    def near_copies(page):
        found = []
        for slot in range(ff // width):
            at = pl.multiple_of(slot * width + (1 - side_bit) * slim, LANES)
            found.append((hidden.at[page, :, pl.ds(at, slim)], near_hidden.at[page, :, pl.ds(slot * slim, slim)]))
        found.append((d_branch.at[page], near_branch.at[page_rows(page)]))
        return [
            pltpu.make_async_remote_copy(
                src_ref=src, dst_ref=dst, send_sem=near_send.at[page, slot], recv_sem=near_recv.at[page, slot],
                device_id={"wide": near}, device_id_type=MESH)
            for slot, (src, dst) in enumerate(found)
        ]

    def peer_copy(src, dst, slot):
        return pltpu.make_async_remote_copy(
            src_ref=src, dst_ref=dst, send_sem=send_sem.at[slot], recv_sem=recv_sem.at[slot],
            device_id={"section": 1 - section}, device_id_type=MESH)

    def page_rows(page):
        return pl.ds(pl.multiple_of(page * rows, rows), rows)

    loads = [pltpu.make_async_copy(src, dst, load_sem.at[at]) for at, (src, dst) in enumerate(
        ((in_hbm, w_in), (out_hbm, w_out), (up_hbm, w_up), (down_hbm, w_down)))]

    def own_copy(page):
        return pltpu.make_async_copy(tokens.at[page_rows(page)], arrive.at[page], page_sem.at[page])

    def own_grad_copy(page):
        return pltpu.make_async_copy(cotangent.at[page_rows(page)], arrive_grad.at[page], page_sem.at[page])

    @pl.when(first)
    def _():
        for page in range(pages):
            own_copy(page).start()

    for load in loads:
        load.start()

    @pl.when(section == 1)
    def _():
        for page in range(pages):
            own_grad_copy(page).start()

    barrier = pltpu.get_barrier_semaphore()
    pl.semaphore_signal(barrier, inc=1, device_id={"section": 1 - section}, device_id_type=MESH)
    if exchange:
        pl.semaphore_signal(barrier, inc=1, device_id={"wide": near}, device_id_type=MESH)
    pl.semaphore_wait(barrier, 2 if exchange else 1)

    onehot[...] = marks_of(buckets).T
    spread_tables(layout, spread)
    vectors[...] = jnp.zeros_like(vectors)
    bias_grad[...] = jnp.zeros_like(bias_grad)

    share = width // 16
    pieces = ff // width
    both = pages * rows

    def plain_copy(block):
        return pltpu.make_async_copy(
            spun.at[block % 2], plain_hbm.at[pl.ds(block * width, width)], spun_sem.at[block % 2, 0])

    def turn_plain():
        for block, source in enumerate((arrive, context, normed_low)):
            if block > 1:
                plain_copy(block - 2).wait()
            for page in range(pages):
                spun[block % 2, :, page * rows : (page + 1) * rows] = source[page].T
            plain_copy(block).start()
        for block in (1, 2):
            plain_copy(block).wait()

    def slab_copies(block, slot, pair, far):
        found = []
        for core in range(2):
            for piece in range(pieces):
                source = spun.at[slot, pl.ds((core * pieces + piece) * share, share)]
                row = pl.multiple_of((2 * block + core) * share, share)
                if pair:
                    target = pair_hbm.at[piece, pl.ds(row, share), pl.ds(far * both, both)]
                else:
                    target = full_hbm.at[piece, pl.ds(row, share)]
                found.append(pltpu.make_async_copy(source, target, spun_sem.at[slot, core * pieces + piece]))
        return found

    def turn_slabs(count, pair, far):
        def one(block, carry):
            slot = block % 2

            @pl.when(block > 1)
            def _():
                for copy in slab_copies(block - 2, slot, pair, far):
                    copy.wait()

            for page in range(pages):
                if far:
                    slab = near_hidden[page, :, pl.ds(pl.multiple_of(block * slim, LANES), slim)]
                elif pair:
                    slab = hidden[page, :, pl.ds(pl.multiple_of(block * width + side_bit * slim, LANES), slim)]
                else:
                    slab = hidden[page, :, pl.ds(pl.multiple_of(block * slim, LANES), slim)]
                spun[slot, 0:slim, page * rows : (page + 1) * rows] = slab.T
            for copy in slab_copies(block, slot, pair, far):
                copy.start()
            return carry

        lax.fori_loop(0, count, one, 0)
        for block in (count - 2, count - 1):
            for copy in slab_copies(block, block % 2, pair, far):
                copy.wait()

    def right_copies(page):
        found, at = [], 0
        for slot, piece in enumerate((d_proj, d_att, d_before, d_branch.at[page])):
            cols = piece.shape[-1]
            found.append(pltpu.make_async_copy(
                piece, right_hbm.at[page_rows(page), pl.ds(at, cols)], right_sem.at[page if slot == 3 else pages + slot]))
            at += cols
        found.append(pltpu.make_async_copy(cross, cross_hbm.at[page_rows(page)], right_sem.at[pages + 4]))
        return found

    lane = lax.broadcasted_iota(jnp.int32, (rows, LANES), 1)
    side = lane < size

    tall = rows // 2

    def result_copy(page, part):
        here = pl.ds(pl.multiple_of(page * rows + part * tall, tall), tall)
        return peer_copy(result.at[here], arrive.at[page, pl.ds(part * tall, tall)], 2 * page + part)

    def grad_copy(page):
        return peer_copy(sent_grad.at[page], arrive_grad.at[page], 2 * pages + page)

    def forward(page, carry):
        @pl.when(first)
        def _():
            own_copy(page).wait()

        @pl.when(section == 1)
        def _():
            for part in range(2):
                result_copy(page, part).wait_recv()

        @pl.when(page == 0)
        def _():
            loads[0].wait()

        layer_in = arrive[page]
        for part in range(3):
            cols = slice(part * width, (part + 1) * width)
            found = dot_nn(layer_in, w_in[:, cols])
            if part != 1:
                found = found + offsets[part // 2]
            qkv[page, :, cols] = found.astype(low)
        mark = onehot[page_rows(page), :]
        for head in range(heads):
            picked[:, head * LANES : (head + 1) * LANES] = dot_nn(mark, spread[head]).astype(low)
        live = lax.broadcasted_iota(jnp.int32, (1, rows), 1) < lengths[page]
        zero = jnp.zeros((rows, LANES), low)

        def scores_of(pair):
            cols = slice(pair * LANES, (pair + 1) * LANES)
            query = qkv[page, :, cols] * jnp.asarray(size**-0.5, low)
            keyed = jnp.concatenate([qkv[page, :, width + pair * LANES : width + (pair + 1) * LANES], mark], axis=1)
            parts = []
            for half in range(2):
                head = 2 * pair + half
                mine = jnp.where(side if half == 0 else ~side, query, zero)
                parts.append(jnp.concatenate([mine, picked[:, head * LANES : (head + 1) * LANES]], axis=1))
            square[pair % 2] = dot_nt(jnp.concatenate(parts, axis=0), keyed)

        def attend(pair):
            cols = slice(pair * LANES, (pair + 1) * LANES)
            valued = qkv[page, :, 2 * width + pair * LANES : 2 * width + (pair + 1) * LANES]
            got = dot_nn(square_low[pair % 2], valued)
            context[page, :, cols] = jnp.where(side, got[:rows], got[rows:]).astype(low)

        scores_of(0)
        for pair in range(pairs):
            if pair + 1 < pairs:
                scores_of(pair + 1)
            for at in range(0, 2 * rows, block):
                scores = jnp.where(live, square[pair % 2, at : at + block], masked_score)
                raised = jnp.exp(scores - jnp.max(scores, axis=-1, keepdims=True))
                share = raised * (1.0 / jnp.sum(raised, axis=-1, keepdims=True))
                chance[page, 2 * pair + at // rows, at % rows : at % rows + block] = share
                square_low[pair % 2, at : at + block] = share.astype(low)
            if pair > 0:
                attend(pair - 1)
        attend(pairs - 1)

        @pl.when(page == 0)
        def _():
            loads[1].wait()

        work[...] = dot_nn(context[page], w_out[...])

        for at in range(0, rows, block):
            here = slice(at, at + block)
            summed = arrive[page, here].astype(high) + (work[here] + offsets[2])
            normal, scale = norm_rows(summed)
            normal_one[page, here] = normal
            scale_one[page, here] = scale
            shifted = normal * gains[0:1] + offsets[3]
            normed[here] = shifted
            normed_low[page, here] = shifted.astype(low)

        @pl.when(page == 0)
        def _():
            loads[2].wait()
            loads[3].wait()

        for part in range(2):
            mine = slice(part * tall, (part + 1) * tall)
            for at in range(0, ff, chunk):
                cols = slice(at, at + chunk)
                before = dot_nn(normed_low[page, mine], w_up[:, cols]) + bias[:, cols]
                below, density = normal_terms(before)
                hidden[page, mine, cols] = (before * below).astype(low)
                slope[page, mine, cols] = (below + density).astype(slope.dtype)
            work[mine] = dot_nn(hidden[page, mine], w_down[...])
            for at in range(part * tall, (part + 1) * tall, block):
                here = slice(at, at + block)
                normal, scale = norm_rows(normed[here] + (work[here] + offsets[4]))
                normal_two[page, here] = normal
                scale_two[page, here] = scale
                result[pl.ds(pl.multiple_of(page * rows + at, block), block), :] = (
                    normal * gains[1:2] + offsets[5]).astype(low)

            @pl.when(first)
            def _():
                result_copy(page, part).start()

        if exchange:
            @pl.when(first)
            def _():
                for copy in near_copies(page)[:-1]:
                    copy.start()

        return carry

    lax.fori_loop(0, pages, forward, 0)

    @pl.when(first)
    def _():
        turn_plain()
        if exchange:
            turn_slabs(ff // width, True, 0)
            for page in range(pages):
                for copy in near_copies(page)[:-1]:
                    copy.wait()
            turn_slabs(ff // width, True, 1)
        else:
            turn_slabs(2 * ff // width, False, 0)

    def backward(page, carry):
        @pl.when(first)
        def _():
            grad_copy(page).wait_recv()

        @pl.when(section == 1)
        def _():
            own_grad_copy(page).wait()

        sums = [jnp.zeros((1, width), high) for _ in range(8)]
        for at in range(0, rows, block):
            here = slice(at, at + block)
            upstream = arrive_grad[page, here].astype(high)
            normal = normal_two[page, here]
            sums[1] += column_sum(upstream * normal)
            sums[7] += column_sum(upstream)
            d_second = norm_back(upstream, gains[1:2], normal, scale_two[page, here])
            d_first[here] = d_second
            branch = d_second.astype(low)
            sums[6] += column_sum(branch)
            d_branch[page, here] = branch
        right_copies(page)[3].start()
        if exchange:
            @pl.when(first)
            def _():
                near_copies(page)[-1].start()


        @pl.when(page > 0)
        def _():
            right_copies(page - 1)[2].wait()

        for at in range(0, ff, chunk):
            cols = slice(at, at + chunk)
            d_hidden = dot_nt(d_branch[page], w_down[cols, :])
            d_chunk = (d_hidden * slope[page, :, cols].astype(high)).astype(low)
            d_before[:, cols] = d_chunk
            bias_grad[:, cols] += column_sum(d_chunk)
        right_copies(page)[2].start()
        work[...] = dot_nt(d_before[...], w_up[...])

        @pl.when(page > 0)
        def _():
            right_copies(page - 1)[1].wait()

        for at in range(0, rows, block):
            here = slice(at, at + block)
            d_normed = d_first[here] + work[here]
            normal = normal_one[page, here]
            sums[0] += column_sum(d_normed * normal)
            sums[5] += column_sum(d_normed)
            found = norm_back(d_normed, gains[0:1], normal, scale_one[page, here])
            d_first[here] = found
            attended = found.astype(low)
            sums[4] += column_sum(attended)
            d_att[here] = attended
        right_copies(page)[1].start()
        d_context[...] = dot_nt(d_att[...], w_out[...]).astype(low)
        turned[...] = qkv[page, :, 0:width].T
        turned_grad[...] = d_context[...].T
        mark = onehot[page_rows(page), :]
        zero = jnp.zeros((rows, LANES), low)
        scaling = size**-0.5

        @pl.when(page > 0)
        def _():
            right_copies(page - 1)[0].wait()

        @pl.when(page > 0)
        def _():
            right_copies(page - 1)[4].wait()

        def upstream_of(pair):
            valued = qkv[page, :, 2 * width + pair * LANES : 2 * width + (pair + 1) * LANES]
            given = d_context[:, pair * LANES : (pair + 1) * LANES]
            parts = [jnp.where(side, given, zero), jnp.where(side, zero, given)]
            square[pair % 2] = dot_nt(jnp.concatenate(parts, axis=0), valued)

        def consume(pair):
            cols = slice(pair * LANES, (pair + 1) * LANES)
            keyed = jnp.concatenate([qkv[page, :, width + pair * LANES : width + (pair + 1) * LANES], mark], axis=1)
            found = []
            joined = dot_nn(square_low[pair % 2], keyed)
            for half in range(2):
                head = 2 * pair + half
                slim_rows = slice(head * size, (head + 1) * size)
                both = joined[half * rows : (half + 1) * rows]
                found.append(both[:, :LANES])
                rest = both[:, LANES:]
                upper = rest.astype(low)
                lower = (rest - upper.astype(high)).astype(low)
                cross[:, 2 * head * LANES : (2 * head + 1) * LANES] = upper
                cross[:, (2 * head + 1) * LANES : (2 * head + 2) * LANES] = lower
                back[slim_rows, :] = dot_nn(turned[slim_rows, :], square_low[pair % 2, half * rows : (half + 1) * rows]) * scaling
                back[slice(width + head * size, width + (head + 1) * size), :] = dot_nn(
                    turned_grad[slim_rows, :], chance[page, head].astype(low))
            d_proj[:, cols] = (jnp.where(side, found[0], found[1]) * scaling).astype(low)

        upstream_of(0)
        for pair in range(pairs):
            if pair + 1 < pairs:
                upstream_of(pair + 1)
            for half in range(2):
                head = 2 * pair + half
                for at in range(0, rows, block):
                    here = slice(half * rows + at, half * rows + at + block)
                    share = chance[page, head, at : at + block]
                    both = share * square[pair % 2, here]
                    d_scores = both - share * jnp.sum(both, axis=-1, keepdims=True)
                    square_low[pair % 2, here] = d_scores.astype(low)
            if pair > 0:
                consume(pair - 1)
        consume(pairs - 1)
        d_proj[:, width:] = back[...].astype(low).T
        sums[2] += column_sum(d_proj[:, 0:width])
        sums[3] += column_sum(d_proj[:, 2 * width :])
        for row, value in enumerate(sums):
            vectors[row : row + 1, :] += value
        right_copies(page)[0].start()
        right_copies(page)[4].start()
        work[...] = dot_nt(d_proj[...], w_in[...])
        for at in range(0, rows, block):
            here = slice(at, at + block)
            d_in = d_first[here] + work[here]
            narrow = d_in.astype(low)
            sent_grad[page, here] = narrow
            input_grads[pl.ds(pl.multiple_of(page * rows + at, block), block), :] = jnp.where(
                first, d_in, narrow.astype(high))

        @pl.when(section == 1)
        def _():
            grad_copy(page).start()

        return carry

    lax.fori_loop(0, pages, backward, 0)

    @pl.when(section == 1)
    def _():
        turn_plain()
        turn_slabs(2 * ff // width, False, 0)

    for page in range(pages):
        right_copies(page)[3].wait()
        if exchange:
            @pl.when(first)
            def _():
                near_copies(page)[-1].wait()

    for slot in (0, 1, 2, 4):
        right_copies(pages - 1)[slot].wait()
    for page in range(pages):
        @pl.when(first)
        def _():
            for part in range(2):
                result_copy(page, part).wait_send()

        @pl.when(section == 1)
        def _():
            grad_copy(page).wait_send()


def both_passes(tokens, cotangent, lengths, buckets, layout, params, exchange):
    in_proj, out_proj, up_proj, down_proj, gains, offsets, bias, heads = params
    pages = lengths.shape[0]
    rows = tokens.shape[0] // pages
    width, ff = up_proj.shape
    sizes = (rows, width, heads, ff, pages)
    VM = pltpu.VMEM
    here, there = pl.BlockSpec(memory_space=pltpu.VMEM), pl.BlockSpec(memory_space=pl.ANY)
    scratch = [
        VM(in_proj.shape, low), VM(out_proj.shape, low), VM(up_proj.shape, low), VM(down_proj.shape, low),
        VM((pages, rows, width), low), VM((pages, rows, width), low), VM((pages, rows, width), low),
        VM((pages, rows, 3 * width), low),
        VM((pages, heads, rows, rows), high),
        VM((pages, rows, width), low),
        VM((pages, rows, width), high), VM((pages, rows, 1), high),
        VM((rows, width), high), VM((pages, rows, width), low),
        VM((pages, rows, ff), high),
        VM((pages, rows, ff), low),
        VM((pages, rows, width), high), VM((pages, rows, 1), high),
        VM((rows, heads * LANES), low),
        VM((rows, width), high),
        VM((2, 2 * rows, rows), high), VM((2, 2 * rows, rows), low),
        VM((rows, 2 * heads * LANES), low),
        VM((rows, 3 * width), low), VM((rows, width), low), VM((rows, ff), low), VM((pages, rows, width), low),
        VM((width, rows), low), VM((width, rows), low), VM((2 * width, rows), high),
        VM((rows, width), low), VM((rows, width), high),
        VM((pages * rows, LANES), low), VM((heads, LANES, LANES), low),
        VM((pages, rows, ff // 2), low), VM((2, width, pages * rows), low),
        pltpu.SemaphoreType.DMA((4,)), pltpu.SemaphoreType.DMA((pages,)), pltpu.SemaphoreType.DMA((2, 2 * ff // width)),
        pltpu.SemaphoreType.DMA((pages + 5,)), pltpu.SemaphoreType.DMA((3 * pages,)), pltpu.SemaphoreType.DMA((3 * pages,)),
        pltpu.SemaphoreType.DMA((pages, ff // width + 1)), pltpu.SemaphoreType.DMA((pages, ff // width + 1)),
    ]
    return pl.pallas_call(
        functools.partial(main_kernel, sizes, exchange),
        out_shape=(
            jax.ShapeDtypeStruct(tokens.shape, low),
            jax.ShapeDtypeStruct(tokens.shape, high),
            jax.ShapeDtypeStruct((3 * width, pages * rows), low),
            jax.ShapeDtypeStruct((ff // width, width // 2, 2 * pages * rows), low),
            jax.ShapeDtypeStruct((ff // width, width, pages * rows), low),
            jax.ShapeDtypeStruct((pages * rows, 5 * width + ff), low),
            jax.ShapeDtypeStruct((pages * rows, 2 * heads * LANES), low),
            jax.ShapeDtypeStruct((8, width), high),
            jax.ShapeDtypeStruct((1, ff), high),
            jax.ShapeDtypeStruct((pages * rows, width), low),
        ),
        in_specs=[pl.BlockSpec(memory_space=pltpu.SMEM), there, there, here, here, here, here, here] + [there] * 4,
        out_specs=(here, here, there, there, there, there, there, here, here, there),
        scratch_shapes=scratch,
        compiler_params=pltpu.CompilerParams(
            collective_id=0, has_side_effects=True, vmem_limit_bytes=63 * 2**20),
    )(lengths, tokens, cotangent, buckets, layout, gains, offsets, bias, in_proj, out_proj, up_proj, down_proj)


def marks_of(buckets):
    tokens = buckets.shape[1]
    level = lax.broadcasted_iota(jnp.int32, (BUCKETS, tokens), 0)
    rows = [jnp.where(buckets[axis : axis + 1, :] == level, 1.0, 0.0) for axis in range(3)]
    return jnp.concatenate(rows + [jnp.zeros((BUCKETS, tokens), high)], axis=0).astype(low)


def spread_tables(layout, spread):
    cells = BUCKETS * BUCKETS
    row = lax.broadcasted_iota(jnp.int32, (BUCKETS, cells), 0)
    own = lax.broadcasted_iota(jnp.int32, (BUCKETS, cells), 1) // BUCKETS == row
    cell = lax.broadcasted_iota(jnp.int32, (cells, LANES), 0) % BUCKETS
    place = lax.broadcasted_iota(jnp.int32, (cells, LANES), 1)
    heads = layout.shape[1]
    for axis in range(3):
        cellwise = layout[axis].astype(high)
        target = jnp.where(cell + axis * BUCKETS == place, 1.0, 0.0).astype(low)
        for head in range(heads):
            grid = jnp.where(own, cellwise[head : head + 1], 0.0).astype(low)
            spread[head, axis * BUCKETS : (axis + 1) * BUCKETS] = dot_nn(grid, target).astype(low)
    spread[:, 3 * BUCKETS :] = jnp.zeros((heads, LANES - 3 * BUCKETS, LANES), low)


def cross_tables(turned, cross):
    found = dot_nn(turned, cross)
    found = found[:, :LANES] + found[:, LANES:]
    place = lax.broadcasted_iota(jnp.int32, (BUCKETS, LANES), 1)
    return jnp.where(
        place < BUCKETS, found[:BUCKETS],
        jnp.where(place < 2 * BUCKETS, found[BUCKETS : 2 * BUCKETS], found[2 * BUCKETS : 3 * BUCKETS]))


LAGS = ((0, 2, 7, 12, 17), (0, 1, 3, 8, 13))


def down_turn(turn):
    return jnp.logical_or(turn == 35, jnp.logical_and(turn < 33, turn % 3 == 0))


def down_of(turn):
    return jnp.where(turn == 35, 11, turn // 3)


def place_of(turn):
    other = jnp.where(turn < 33, 2 * (turn // 3) + turn % 3 - 1, turn - 11)
    other = jnp.where(other < 12, other + 12, jnp.where(other < 15, other - 3, other - 15))
    return jnp.where(down_turn(turn), 24 + down_of(turn), other)


def left_of(at):
    return jnp.where(at < 9, 0, jnp.where(at < 12, 1, 2))


def rs_kernel(
    count, levels, rows, cols, lags,
    plain_hbm, pair_hbm, full_hbm, right_hbm, cross_hbm, near_branch, buckets, vectors, bias_grad,
    out_in, out_out, out_up, out_down, out_tables, out_gains, out_offsets, out_bias,
    left, left_pair, left_full, right, right_down, cross, tables, dw, k1, k2, k3, s0, s1, s2, s3, r0, r1, r2, r3, ssem, rsem, left_sem, right_sem, left_down_sem, right_down_sem, cross_sem,
    ks, ks0, ks1, ks2, ss0, ss1, ss2, ss3, sr0, sr1, sr2, sr3, sssem, srsem,
):
    me = lax.axis_index("wide")
    keeps, sends, recvs = (dw, k1, k2, k3), (s0, s1, s2, s3), (r0, r1, r2, r3)
    skeeps, ssends, srecvs = (ks, ks0, ks1, ks2), (ss0, ss1, ss2, ss3), (sr0, sr1, sr2, sr3)
    bits = [(me // 2**level) % 2 for level in range(levels)]
    partners = [me + 2**level * (1 - 2 * bits[level]) for level in range(levels)]
    width = rows * 2**levels

    section = lax.axis_index("section")
    first = section == 0
    depth = right.shape[1]

    def left_load(block):
        return pltpu.make_async_copy(
            plain_hbm.at[pl.ds(pl.multiple_of(block * width, width), width)], left.at[block], left_sem.at[block])

    def right_load(block):
        return pltpu.make_async_copy(
            right_hbm.at[:, pl.ds(pl.multiple_of(block * cols, cols), cols)], right.at[block], right_sem.at[block])

    def pair_load(piece):
        return pltpu.make_async_copy(pair_hbm.at[piece], left_pair.at[piece], left_down_sem.at[piece])

    def full_load(piece):
        return pltpu.make_async_copy(full_hbm.at[piece], left_full.at[piece], left_down_sem.at[piece])

    def right_down_load(col):
        here = pl.ds(pl.multiple_of((right.shape[0] + col) * cols, cols), cols)
        return pltpu.make_async_copy(right_hbm.at[:, here], right_down.at[col, pl.ds(0, depth)], right_down_sem.at[0, col])

    def near_load(col):
        there = pl.ds(pl.multiple_of(col * cols, cols), cols)
        return pltpu.make_async_copy(near_branch.at[:, there], right_down.at[col, pl.ds(depth, depth)], right_down_sem.at[1, col])

    cross_load = pltpu.make_async_copy(cross_hbm, cross, cross_sem)
    barrier = pltpu.get_barrier_semaphore()
    for partner in partners:
        pl.semaphore_signal(barrier, inc=1, device_id={"wide": partner}, device_id_type=MESH)

    @pl.when(first)
    def _():
        pair_load(0).start()
        near_load(0).start()

    @pl.when(section == 1)
    def _():
        full_load(0).start()

    right_down_load(0).start()
    left_load(2).start()
    for block in range(12, 16):
        right_load(block).start()
    for col in (1, 2):
        right_down_load(col).start()

    @pl.when(first)
    def _():
        for col in (1, 2):
            near_load(col).start()
        for piece in (1, 2, 3):
            pair_load(piece).start()

    @pl.when(section == 1)
    def _():
        for piece in (1, 2, 3):
            full_load(piece).start()

    for block in range(16, 24):
        right_load(block).start()
    cross_load.start()
    for block in (1, 0):
        left_load(block).start()
    for block in range(0, 12):
        right_load(block).start()
    pl.semaphore_wait(barrier, levels)

    def copy(step, at, partner):
        return pltpu.make_async_remote_copy(
            src_ref=sends[step].at[at], dst_ref=recvs[step].at[at],
            send_sem=ssem.at[step, at], recv_sem=rsem.at[step, at],
            device_id={"wide": partners[partner]}, device_id_type=MESH)

    def small_copy(step):
        return pltpu.make_async_remote_copy(
            src_ref=ssends[step], dst_ref=srecvs[step],
            send_sem=sssem.at[step], recv_sem=srsem.at[step],
            device_id={"wide": partners[step]}, device_id_type=MESH)

    def cross_head(head):
        here = pl.ds(pl.multiple_of(head * 2 * LANES, 2 * LANES), 2 * LANES)
        tables[head] = cross_tables(marks_of(buckets), cross[:, here])

    def paired(turn):
        return jnp.logical_and(first, down_turn(turn))

    def far_first(turn):
        return jnp.logical_and(section == 1, turn % 6 == 0)

    def start(turn):
        at = place_of(turn)
        slot = turn % dw.shape[0]
        down = down_of(turn)
        piece, col = down // 3, down % 3

        def take(value):
            dw[slot] = value.reshape(dw.shape[1:])
            for j in range(2 ** (levels - 1)):
                s0[turn, j] = dw[slot, 2 * j + 1 - bits[0]].astype(low)
            copy(0, turn, 0).start()

        @pl.when(jnp.logical_and(down_turn(turn), down < 3))
        def _():
            right_down_load(down).wait()

        @pl.when(paired(turn))
        def _():
            @pl.when(down < 3)
            def _():
                near_load(down).wait()

            @pl.when(col == 0)
            def _():
                pair_load(piece).wait()

            found = dot_nn(left_pair[piece], right_down[col])
            dw[slot, 0 : 2 ** (levels - 1)] = found.reshape((2 ** (levels - 1),) + dw.shape[2:])

        @pl.when(jnp.logical_and(section == 1, down_turn(turn)))
        def _():
            @pl.when(col == 0)
            def _():
                full_load(piece).wait()

            take(dot_nn(left_full[piece], right_down[col, 0:depth]))

        @pl.when(jnp.logical_not(down_turn(turn)))
        def _():
            right_load(at).wait()

            @pl.when(jnp.logical_or(at == 12, jnp.logical_or(at == 9, at == 0)))
            def _():
                left_load(left_of(at)).wait()

            take(dot_nn(left[left_of(at)], right[at]))

    def pass_on(step, at, partner, place, total):
        half = 2 ** (levels - 1 - step)
        new = at % keeps[step].shape[0]
        bit = bits[partner]

        def pick(j, value):
            return (j >> place << (place + 1)) + (j & (2**place - 1)) + value * 2**place

        for j in range(half):
            sends[step][at, j] = total(pick(j, 1 - bit)).astype(low)
        copy(step, at, partner).start()
        for j in range(half):
            keeps[step][new, j] = total(pick(j, bit))

    def second(at, kind):
        old = at % dw.shape[0]
        if kind == "paired":
            pass_on(1, at, 0, 0, lambda pick: dw[old, pick])
            return
        copy(0, at, 0).wait_recv()
        partner, place = (2, 1) if kind == "far" else (1, 0)
        pass_on(1, at, partner, place, lambda pick: dw[old, 2 * pick + bits[0]] + r0[at, pick].astype(high))

    def later(step, at, kind):
        copy(step - 1, at, 0).wait_recv()
        old = at % keeps[step - 1].shape[0]
        partner, place = ((3, 1) if step == 2 else (1, 0)) if kind == "far" else (step, 0)
        pass_on(step, at, partner, place, lambda pick: keeps[step - 1][old, pick] + recvs[step - 1][at, pick].astype(high))

    def finish(turn):
        copy(levels - 1, turn, levels - 1).wait_recv()
        old = turn % keeps[levels - 1].shape[0]
        value = keeps[levels - 1][old, 0] + recvs[levels - 1][turn, 0].astype(high)
        at = place_of(turn)

        def columns(first):
            return pl.ds(pl.multiple_of((at - first) * cols, cols), cols)

        @pl.when(at < 9)
        def _():
            out_in[0, :, columns(0)] = value

        @pl.when(jnp.logical_and(at >= 9, at < 12))
        def _():
            out_out[0, :, columns(9)] = value

        @pl.when(jnp.logical_and(at >= 12, at < 24))
        def _():
            out_up[0, :, columns(12)] = value

        @pl.when(at >= 24)
        def _():
            part, col = (at - 24) // 3, at % 3
            out_down[0, pl.ds(pl.multiple_of(part * rows, rows), rows), pl.ds(pl.multiple_of(col * cols, cols), cols)] = value

    def small_fill():
        heads = tables.shape[0]
        for part in range(2**levels):
            for head in range(heads):
                ks[part, 2 * head : 2 * head + 2] = tables[head, 2 * part : 2 * part + 2]
            ks[part, 2 * heads : 2 * heads + 8, 0:rows] = vectors[:, part * rows : (part + 1) * rows]
            for piece in range(4):
                at = (4 * part + piece) * rows
                ks[part, 2 * heads + piece : 2 * heads + piece + 1, rows : 2 * rows] = bias_grad[:, at : at + rows]

    def small_stage(step):
        if step:
            small_copy(step - 1).wait_recv()
        if step == levels:
            heads = tables.shape[0]
            ks[0] = skeeps[levels - 1][0] + srecvs[levels - 1][0]
            for axis in range(3):
                for i in range(2):
                    got = ks[0, pl.ds(i, heads, 2), :]
                    out_tables[axis, :, 0, i * BUCKETS : (i + 1) * BUCKETS] = got[:, axis * BUCKETS : (axis + 1) * BUCKETS]
            out_gains[0] = ks[0, 2 * heads : 2 * heads + 2, 0:rows]
            out_offsets[:, 0] = ks[0, 2 * heads + 2 : 2 * heads + 8, 0:rows]
            for piece in range(4):
                out_bias[:, piece * rows : (piece + 1) * rows] = ks[0, 2 * heads + piece : 2 * heads + piece + 1, rows : 2 * rows]
            return
        half = 2 ** (levels - 1 - step)

        def total(pick):
            if step == 0:
                return ks[pick]
            return skeeps[step - 1][2 * pick + bits[0] if step == 1 else pick] + srecvs[step - 1][pick]

        for j in range(half):
            ssends[step][j] = total(2 * j + 1 - bits[step])
        small_copy(step).start()
        if step:
            for j in range(half):
                skeeps[step][j] = total(2 * j + bits[step])

    def step_at(moment, carry):
        @pl.when(moment == 5)
        def _():
            cross_load.wait()

        @pl.when(jnp.logical_and(moment >= 5, moment < 5 + tables.shape[0]))
        def _():
            cross_head(moment - 5)

        def due(at):
            return jnp.logical_and(at >= 0, at < count)

        @pl.when(due(moment))
        def _():
            start(moment)

        for step in range(1, levels + 1):
            near_at, pair_at = moment - lags[0][step], moment - lags[1][step]
            plain_due = jnp.logical_and(due(near_at), jnp.logical_not(paired(near_at)))
            pair_due = jnp.logical_and(due(pair_at), paired(pair_at))
            if step == 1:
                @pl.when(pair_due)
                def _():
                    second(pair_at, "paired")
            elif step < levels:
                @pl.when(pair_due)
                def _():
                    later(step, pair_at, "paired")
            else:
                @pl.when(pair_due)
                def _():
                    finish(pair_at)

                @pl.when(plain_due)
                def _():
                    finish(near_at)
                continue
            for kind in ("plain", "far"):
                chosen = far_first(near_at) if kind == "far" else jnp.logical_not(far_first(near_at))

                @pl.when(jnp.logical_and(plain_due, chosen))
                def _():
                    second(near_at, kind) if step == 1 else later(step, near_at, kind)
        return carry

    ks[...] = jnp.zeros_like(ks)
    lax.fori_loop(0, 19, step_at, 0)
    small_fill()
    small_stage(0)
    lax.fori_loop(19, 22, step_at, 0)
    small_stage(1)
    lax.fori_loop(22, count, step_at, 0)
    small_stage(2)
    small_stage(3)
    small_stage(4)
    lax.fori_loop(count, count + lags[0][levels], step_at, 0)

    def drain(at, carry):
        @pl.when(jnp.logical_not(paired(at)))
        def _():
            copy(0, at, 0).wait_send()

        for step in range(1, levels):
            copy(step, at, step).wait_send()
        return carry

    lax.fori_loop(0, count, drain, 0)
    for step in range(levels):
        small_copy(step).wait_send()


def reduce_grads(plain, pair, full, right, cross, near_branch, buckets, vectors, bias_grad, count=36, levels=4, lags=LAGS):
    n = 2**levels
    depth, total = right.shape
    width = vectors.shape[1]
    cols, rows = 256, width // n
    heads = cross.shape[1] // (2 * LANES)
    ff = bias_grad.shape[1]
    others = total // cols - width // cols

    def ring(step):
        return max(lag[step + 1] for lag in lags) - min(lag[step] for lag in lags) + 1

    VM = pltpu.VMEM
    scratch = [VM((3, width, depth), low), VM(pair.shape, low), VM(full.shape, low)]
    scratch += [VM((others, depth, cols), low), VM((width // cols, 2 * depth, cols), low)]
    scratch += [VM(cross.shape, low), VM((heads, BUCKETS, LANES), high)]
    scratch += [VM((ring(0), n, rows, cols), high)]
    scratch += [VM((ring(step), n >> (step + 1), rows, cols), high) for step in (1, 2, 3)]
    scratch += [VM((count, n >> (step + 1), rows, cols), low) for step in range(4)] * 2
    scratch += [pltpu.SemaphoreType.DMA((levels, count))] * 2
    scratch += [pltpu.SemaphoreType.DMA((3,)), pltpu.SemaphoreType.DMA((others,))]
    scratch += [pltpu.SemaphoreType.DMA((ff // width,)), pltpu.SemaphoreType.DMA((2, width // cols)), pltpu.SemaphoreType.DMA]
    few = (2 * heads + 8, LANES)
    scratch += [VM((n,) + few, high)]
    scratch += [VM((n >> (step + 1),) + few, high) for step in (1, 2, 3)]
    scratch += [VM((n >> (step + 1),) + few, high) for step in range(4)] * 2
    scratch += [pltpu.SemaphoreType.DMA((levels,))] * 2
    here, there = pl.BlockSpec(memory_space=pltpu.VMEM), pl.BlockSpec(memory_space=pl.ANY)
    shapes = (
        (1, rows, 3 * width), (1, rows, width), (1, rows, ff), (1, ff // n, width),
        (3, heads, 1, 2 * BUCKETS), (1, 2, rows), (6, 1, rows), (1, ff // n),
    )
    return pl.pallas_call(
        functools.partial(rs_kernel, count, levels, rows, cols, lags),
        out_shape=tuple(jax.ShapeDtypeStruct(shape, high) for shape in shapes),
        in_specs=[there] * 6 + [here] * 3,
        out_specs=(here,) * len(shapes),
        scratch_shapes=scratch,
        compiler_params=pltpu.CompilerParams(
            collective_id=1, has_side_effects=True, vmem_limit_bytes=63 * 2**20),
    )(plain, pair, full, right, cross, near_branch, buckets, vectors, bias_grad)


def settle_kernel(count, *refs):
    sources, targets, held, sem = refs[:count], refs[count : 2 * count], refs[2 * count : 3 * count], refs[3 * count]
    copies = [
        (pltpu.make_async_copy(sources[at], held[at], sem.at[0, at]), pltpu.make_async_copy(held[at], targets[at], sem.at[1, at]))
        for at in range(count)
    ]
    for fetch, _ in copies:
        fetch.start()
    for fetch, put in copies:
        fetch.wait()
        put.start()
    for _, put in copies:
        put.wait()


def settle(arrays):
    there = pl.BlockSpec(memory_space=pl.ANY)
    return pl.pallas_call(
        functools.partial(settle_kernel, len(arrays)),
        out_shape=tuple(jax.ShapeDtypeStruct(array.shape, array.dtype) for array in arrays),
        in_specs=[there] * len(arrays),
        out_specs=(there,) * len(arrays),
        scratch_shapes=[pltpu.VMEM(array.shape, array.dtype) for array in arrays] + [pltpu.SemaphoreType.DMA((2, len(arrays)))],
        compiler_params=pltpu.CompilerParams(vmem_limit_bytes=63 * 2**20),
    )(*arrays)


def local(tokens, cotangent, lengths, buckets, in_proj, out_proj, up_proj, down_proj, layout_tables, norm_gains, offsets, hidden_bias):
    heads = layout_tables.shape[2]
    width, ff = up_proj.shape[1:]
    shifts = jnp.transpose(offsets, (1, 0, 2))
    params = (in_proj[0], out_proj[0], up_proj[0], down_proj[0], norm_gains[0], shifts, hidden_bias, heads)
    wide_count = lax.axis_size("wide")
    result, input_grads, plain, pair, full, right, cross, vectors, bias_grad, near_branch = both_passes(
        tokens, cotangent, lengths, buckets, layout_tables[0], params, wide_count == 16)
    share = width // wide_count
    if wide_count == 16 and share % 16 == 0:
        found = reduce_grads(plain, pair, full, right, cross, near_branch, buckets, vectors, bias_grad)
        found = settle((result[None], input_grads[None]) + found)
        return found[:6] + (jnp.transpose(found[6], (2, 0, 1, 3)), found[7], jnp.transpose(found[8], (1, 0, 2)), found[9])
    else:

        def scattered(value, dim):
            return lax.psum_scatter(value[None], "wide", scatter_dimension=dim, tiled=True)

        def product(rows_from, cols_from, cols):
            return dot_nn(plain[rows_from : rows_from + width], right[:, cols_from : cols_from + cols])

        grad_in = scattered(product(0, 0, 3 * width), 1)
        grad_out = scattered(product(width, 3 * width, width), 1)
        grad_up = scattered(product(2 * width, 4 * width, ff), 1)
        grad_down = dot_nn(full.reshape(ff, -1), right[:, 4 * width + ff :])
        grad_down = grad_down.reshape(ff // width, 16, -1, width).transpose(1, 0, 2, 3).reshape(ff, width)
        grad_down = scattered(grad_down, 1)
        grad_hidden = scattered(bias_grad[0], 1)
        turned = marks_of(buckets)
        tables = jnp.stack([
            cross_tables(turned, cross[:, 2 * head * LANES : 2 * (head + 1) * LANES]) for head in range(heads)])
        tables = tables[:, :, : 3 * BUCKETS].reshape(heads, BUCKETS, 3, BUCKETS).transpose(2, 0, 1, 3)
        grad_tables = scattered(tables.reshape(3, heads, -1), 3)
        vectors = scattered(vectors, 2)
        grad_gains, grad_offsets = vectors[:, :2], vectors[:, 2:]
    return (
        result[None],
        input_grads[None],
        grad_in,
        grad_out,
        grad_up,
        grad_down,
        grad_tables,
        grad_gains,
        grad_offsets,
        grad_hidden,
    )


def solution(mesh):
    placed = (
        P("wide", None),
        P("wide", None),
        P("wide"),
        P(None, "wide"),
        P("section", None, None),
        P("section", None, None),
        P("section", None, None),
        P("section", None, None),
        P("section", None, None, None),
        P("section", None, None),
        P("section", None, None),
        P("section", None),
    )
    return jax.shard_map(
        local,
        mesh=mesh,
        in_specs=placed,
        out_specs=(
            P("section", "wide", None),
            P("section", "wide", None),
            P("section", "wide", None),
            P("section", "wide", None),
            P("section", "wide", None),
            P("section", "wide", None),
            P("section", None, None, "wide"),
            P("section", None, "wide"),
            P("section", None, "wide"),
            P("section", "wide"),
        ),
        check_vma=False,
    )
```

```python
import functools

import jax
import jax.numpy as jnp
from jax import lax
from jax.experimental import pallas as pl
from jax.experimental.pallas import tpu as pltpu
from jax.sharding import PartitionSpec as P

MESH = pl.DeviceIdType.MESH
BUCKETS = 32
LANES = 128
epsilon = 1e-05
masked_score = -1000000000.0
low = jnp.bfloat16
high = jnp.float32


def dot_nn(left, right):
    return jnp.dot(left, right, preferred_element_type=high)


def dot_nt(left, right):
    return lax.dot_general(left, right, (((1,), (1,)), ((), ())), preferred_element_type=high)


def normal_terms(values):
    below = 0.5 + 0.5 * lax.erf(values * 0.7071067811865476)
    return below, values * (0.3989422804014327 * jnp.exp(-0.5 * values * values))


def norm_rows(values):
    centered = values - jnp.mean(values, axis=-1, keepdims=True)
    spread = jnp.mean(centered * centered, axis=-1, keepdims=True)
    scale = lax.rsqrt(spread + epsilon)
    return centered * scale, scale


def norm_back(upstream, gain, normal, scale):
    scaled = upstream * gain
    middle = jnp.mean(scaled, axis=-1, keepdims=True)
    along = jnp.mean(scaled * normal, axis=-1, keepdims=True)
    return scale * (scaled - middle - normal * along)


def column_sum(values):
    return jnp.sum(values.astype(high), axis=0, keepdims=True)


def main_kernel(
    sizes, exchange,
    lengths, tokens, cotangent, buckets, layout, gains, offsets, bias,
    in_hbm, out_hbm, up_hbm, down_hbm,
    result, input_grads, plain_hbm, pair_hbm, full_hbm, right_hbm, cross_hbm, vectors, bias_grad, near_branch,
    w_in, w_out, w_up, w_down, arrive, arrive_grad, sent_grad,
    qkv, chance, context, normal_one, scale_one, normed, normed_low, slope, hidden,
    normal_two, scale_two, picked, work, square, square_low, cross, d_proj, d_att, d_before, d_branch,
    turned, turned_grad, back, d_context, d_first, onehot, spread, near_hidden, spun,
    load_sem, page_sem, spun_sem, right_sem, send_sem, recv_sem, near_send, near_recv,
):
    rows, width, heads, ff, pages = sizes
    size = width // heads
    pairs = heads // 2
    section = lax.axis_index("section")
    first = section == 0
    block = 64
    chunk = 512
    me = lax.axis_index("wide")
    side_bit = (me // 2) % 2
    near = me + 2 - 4 * side_bit
    slim = width // 2

    def near_copies(page):
        found = []
        for slot in range(ff // width):
            at = pl.multiple_of(slot * width + (1 - side_bit) * slim, LANES)
            found.append((hidden.at[page, :, pl.ds(at, slim)], near_hidden.at[page, :, pl.ds(slot * slim, slim)]))
        found.append((d_branch.at[page], near_branch.at[page_rows(page)]))
        return [
            pltpu.make_async_remote_copy(
                src_ref=src, dst_ref=dst, send_sem=near_send.at[page, slot], recv_sem=near_recv.at[page, slot],
                device_id={"wide": near}, device_id_type=MESH)
            for slot, (src, dst) in enumerate(found)
        ]

    def peer_copy(src, dst, slot):
        return pltpu.make_async_remote_copy(
            src_ref=src, dst_ref=dst, send_sem=send_sem.at[slot], recv_sem=recv_sem.at[slot],
            device_id={"section": 1 - section}, device_id_type=MESH)

    def page_rows(page):
        return pl.ds(pl.multiple_of(page * rows, rows), rows)

    loads = [pltpu.make_async_copy(src, dst, load_sem.at[at]) for at, (src, dst) in enumerate(
        ((in_hbm, w_in), (out_hbm, w_out), (up_hbm, w_up), (down_hbm, w_down)))]

    def own_copy(page):
        return pltpu.make_async_copy(tokens.at[page_rows(page)], arrive.at[page], page_sem.at[page])

    def own_grad_copy(page):
        return pltpu.make_async_copy(cotangent.at[page_rows(page)], arrive_grad.at[page], page_sem.at[page])

    @pl.when(first)
    def _():
        for page in range(pages):
            own_copy(page).start()

    for load in loads:
        load.start()

    @pl.when(section == 1)
    def _():
        for page in range(pages):
            own_grad_copy(page).start()

    barrier = pltpu.get_barrier_semaphore()
    pl.semaphore_signal(barrier, inc=1, device_id={"section": 1 - section}, device_id_type=MESH)
    if exchange:
        pl.semaphore_signal(barrier, inc=1, device_id={"wide": near}, device_id_type=MESH)
    pl.semaphore_wait(barrier, 2 if exchange else 1)

    onehot[...] = marks_of(buckets).T
    spread_tables(layout, spread)
    vectors[...] = jnp.zeros_like(vectors)
    bias_grad[...] = jnp.zeros_like(bias_grad)

    share = width // 16
    pieces = ff // width
    both = pages * rows

    def plain_copy(block):
        return pltpu.make_async_copy(
            spun.at[block % 2], plain_hbm.at[pl.ds(block * width, width)], spun_sem.at[block % 2, 0])

    def turn_plain():
        for block, source in enumerate((arrive, context, normed_low)):
            if block > 1:
                plain_copy(block - 2).wait()
            for page in range(pages):
                spun[block % 2, :, page * rows : (page + 1) * rows] = source[page].T
            plain_copy(block).start()
        for block in (1, 2):
            plain_copy(block).wait()

    def slab_copies(block, slot, pair, far):
        found = []
        for core in range(2):
            for piece in range(pieces):
                source = spun.at[slot, pl.ds((core * pieces + piece) * share, share)]
                row = pl.multiple_of((2 * block + core) * share, share)
                if pair:
                    target = pair_hbm.at[piece, pl.ds(row, share), pl.ds(far * both, both)]
                else:
                    target = full_hbm.at[piece, pl.ds(row, share)]
                found.append(pltpu.make_async_copy(source, target, spun_sem.at[slot, core * pieces + piece]))
        return found

    def turn_slabs(count, pair, far):
        def one(block, carry):
            slot = block % 2

            @pl.when(block > 1)
            def _():
                for copy in slab_copies(block - 2, slot, pair, far):
                    copy.wait()

            for page in range(pages):
                if far:
                    slab = near_hidden[page, :, pl.ds(pl.multiple_of(block * slim, LANES), slim)]
                elif pair:
                    slab = hidden[page, :, pl.ds(pl.multiple_of(block * width + side_bit * slim, LANES), slim)]
                else:
                    slab = hidden[page, :, pl.ds(pl.multiple_of(block * slim, LANES), slim)]
                spun[slot, 0:slim, page * rows : (page + 1) * rows] = slab.T
            for copy in slab_copies(block, slot, pair, far):
                copy.start()
            return carry

        lax.fori_loop(0, count, one, 0)
        for block in (count - 2, count - 1):
            for copy in slab_copies(block, block % 2, pair, far):
                copy.wait()

    def right_copies(page):
        found, at = [], 0
        for slot, piece in enumerate((d_proj, d_att, d_before, d_branch.at[page])):
            cols = piece.shape[-1]
            found.append(pltpu.make_async_copy(
                piece, right_hbm.at[page_rows(page), pl.ds(at, cols)], right_sem.at[page if slot == 3 else pages + slot]))
            at += cols
        found.append(pltpu.make_async_copy(cross, cross_hbm.at[page_rows(page)], right_sem.at[pages + 4]))
        return found

    lane = lax.broadcasted_iota(jnp.int32, (rows, LANES), 1)
    side = lane < size

    tall = rows // 2

    def result_copy(page, part):
        here = pl.ds(pl.multiple_of(page * rows + part * tall, tall), tall)
        return peer_copy(result.at[here], arrive.at[page, pl.ds(part * tall, tall)], 2 * page + part)

    def grad_copy(page, part):
        here = pl.ds(part * tall, tall)
        return peer_copy(sent_grad.at[page, here], arrive_grad.at[page, here], 2 * pages + 2 * page + part)

    def forward(page, carry):
        @pl.when(first)
        def _():
            own_copy(page).wait()

        @pl.when(section == 1)
        def _():
            for part in range(2):
                result_copy(page, part).wait_recv()

        @pl.when(page == 0)
        def _():
            loads[0].wait()

        layer_in = arrive[page]
        for part in range(3):
            cols = slice(part * width, (part + 1) * width)
            found = dot_nn(layer_in, w_in[:, cols])
            if part != 1:
                found = found + offsets[part // 2]
            qkv[page, :, cols] = found.astype(low)
        mark = onehot[page_rows(page), :]
        for head in range(heads):
            picked[:, head * LANES : (head + 1) * LANES] = dot_nn(mark, spread[head]).astype(low)
        live = lax.broadcasted_iota(jnp.int32, (1, rows), 1) < lengths[page]
        zero = jnp.zeros((rows, LANES), low)

        def scores_of(pair):
            cols = slice(pair * LANES, (pair + 1) * LANES)
            query = qkv[page, :, cols] * jnp.asarray(size**-0.5, low)
            keyed = jnp.concatenate([qkv[page, :, width + pair * LANES : width + (pair + 1) * LANES], mark], axis=1)
            parts = []
            for half in range(2):
                head = 2 * pair + half
                mine = jnp.where(side if half == 0 else ~side, query, zero)
                parts.append(jnp.concatenate([mine, picked[:, head * LANES : (head + 1) * LANES]], axis=1))
            square[pair % 2] = dot_nt(jnp.concatenate(parts, axis=0), keyed)

        def attend(pair):
            cols = slice(pair * LANES, (pair + 1) * LANES)
            valued = qkv[page, :, 2 * width + pair * LANES : 2 * width + (pair + 1) * LANES]
            got = dot_nn(square_low[pair % 2], valued)
            context[page, :, cols] = jnp.where(side, got[:rows], got[rows:]).astype(low)

        scores_of(0)
        for pair in range(pairs):
            if pair + 1 < pairs:
                scores_of(pair + 1)
            for at in range(0, 2 * rows, block):
                scores = jnp.where(live, square[pair % 2, at : at + block], masked_score)
                raised = jnp.exp(scores - jnp.max(scores, axis=-1, keepdims=True))
                share = raised * (1.0 / jnp.sum(raised, axis=-1, keepdims=True))
                chance[page, 2 * pair + at // rows, at % rows : at % rows + block] = share
                square_low[pair % 2, at : at + block] = share.astype(low)
            if pair > 0:
                attend(pair - 1)
        attend(pairs - 1)

        @pl.when(page == 0)
        def _():
            loads[1].wait()

        work[...] = dot_nn(context[page], w_out[...])

        for at in range(0, rows, block):
            here = slice(at, at + block)
            summed = arrive[page, here].astype(high) + (work[here] + offsets[2])
            normal, scale = norm_rows(summed)
            normal_one[page, here] = normal
            scale_one[page, here] = scale
            shifted = normal * gains[0:1] + offsets[3]
            normed[here] = shifted
            normed_low[page, here] = shifted.astype(low)

        @pl.when(page == 0)
        def _():
            loads[2].wait()
            loads[3].wait()

        def feed_forward(parts):
            high_rows = rows // parts
            for part in range(parts):
                mine = slice(part * high_rows, (part + 1) * high_rows)
                for at in range(0, ff, chunk):
                    cols = slice(at, at + chunk)
                    before = dot_nn(normed_low[page, mine], w_up[:, cols]) + bias[:, cols]
                    below, density = normal_terms(before)
                    hidden[page, mine, cols] = (before * below).astype(low)
                    slope[page, mine, cols] = (below + density).astype(slope.dtype)
                work[mine] = dot_nn(hidden[page, mine], w_down[...])
                for at in range(part * high_rows, (part + 1) * high_rows, block):
                    here = slice(at, at + block)
                    normal, scale = norm_rows(normed[here] + (work[here] + offsets[4]))
                    normal_two[page, here] = normal
                    scale_two[page, here] = scale
                    result[pl.ds(pl.multiple_of(page * rows + at, block), block), :] = (
                        normal * gains[1:2] + offsets[5]).astype(low)
                if parts == 2:
                    result_copy(page, part).start()

        @pl.when(first)
        def _():
            feed_forward(2)

        @pl.when(section == 1)
        def _():
            feed_forward(1)

        if exchange:
            @pl.when(first)
            def _():
                for copy in near_copies(page)[:-1]:
                    copy.start()

        return carry

    lax.fori_loop(0, pages, forward, 0)

    @pl.when(first)
    def _():
        turn_plain()
        if exchange:
            turn_slabs(ff // width, True, 0)
            for page in range(pages):
                for copy in near_copies(page)[:-1]:
                    copy.wait()
            turn_slabs(ff // width, True, 1)
        else:
            turn_slabs(2 * ff // width, False, 0)

    def backward(page, carry):
        @pl.when(first)
        def _():
            for part in range(2):
                grad_copy(page, part).wait_recv()

        @pl.when(section == 1)
        def _():
            own_grad_copy(page).wait()

        sums = [jnp.zeros((1, width), high) for _ in range(8)]
        for at in range(0, rows, block):
            here = slice(at, at + block)
            upstream = arrive_grad[page, here].astype(high)
            normal = normal_two[page, here]
            sums[1] += column_sum(upstream * normal)
            sums[7] += column_sum(upstream)
            d_second = norm_back(upstream, gains[1:2], normal, scale_two[page, here])
            d_first[here] = d_second
            branch = d_second.astype(low)
            sums[6] += column_sum(branch)
            d_branch[page, here] = branch
        right_copies(page)[3].start()
        if exchange:
            @pl.when(first)
            def _():
                near_copies(page)[-1].start()


        @pl.when(page > 0)
        def _():
            right_copies(page - 1)[2].wait()

        for at in range(0, ff, chunk):
            cols = slice(at, at + chunk)
            d_hidden = dot_nt(d_branch[page], w_down[cols, :])
            d_chunk = (d_hidden * slope[page, :, cols].astype(high)).astype(low)
            d_before[:, cols] = d_chunk
            bias_grad[:, cols] += column_sum(d_chunk)
        right_copies(page)[2].start()
        work[...] = dot_nt(d_before[...], w_up[...])

        @pl.when(page > 0)
        def _():
            right_copies(page - 1)[1].wait()

        for at in range(0, rows, block):
            here = slice(at, at + block)
            d_normed = d_first[here] + work[here]
            normal = normal_one[page, here]
            sums[0] += column_sum(d_normed * normal)
            sums[5] += column_sum(d_normed)
            found = norm_back(d_normed, gains[0:1], normal, scale_one[page, here])
            d_first[here] = found
            attended = found.astype(low)
            sums[4] += column_sum(attended)
            d_att[here] = attended
        right_copies(page)[1].start()
        d_context[...] = dot_nt(d_att[...], w_out[...]).astype(low)
        turned[...] = qkv[page, :, 0:width].T
        turned_grad[...] = d_context[...].T
        mark = onehot[page_rows(page), :]
        zero = jnp.zeros((rows, LANES), low)
        scaling = size**-0.5

        @pl.when(page > 0)
        def _():
            right_copies(page - 1)[0].wait()

        @pl.when(page > 0)
        def _():
            right_copies(page - 1)[4].wait()

        def upstream_of(pair):
            valued = qkv[page, :, 2 * width + pair * LANES : 2 * width + (pair + 1) * LANES]
            given = d_context[:, pair * LANES : (pair + 1) * LANES]
            parts = [jnp.where(side, given, zero), jnp.where(side, zero, given)]
            square[pair % 2] = dot_nt(jnp.concatenate(parts, axis=0), valued)

        def consume(pair):
            cols = slice(pair * LANES, (pair + 1) * LANES)
            keyed = jnp.concatenate([qkv[page, :, width + pair * LANES : width + (pair + 1) * LANES], mark], axis=1)
            found = []
            joined = dot_nn(square_low[pair % 2], keyed)
            for half in range(2):
                head = 2 * pair + half
                slim_rows = slice(head * size, (head + 1) * size)
                both = joined[half * rows : (half + 1) * rows]
                found.append(both[:, :LANES])
                rest = both[:, LANES:]
                upper = rest.astype(low)
                lower = (rest - upper.astype(high)).astype(low)
                cross[:, 2 * head * LANES : (2 * head + 1) * LANES] = upper
                cross[:, (2 * head + 1) * LANES : (2 * head + 2) * LANES] = lower
                back[slim_rows, :] = dot_nn(turned[slim_rows, :], square_low[pair % 2, half * rows : (half + 1) * rows]) * scaling
                back[slice(width + head * size, width + (head + 1) * size), :] = dot_nn(
                    turned_grad[slim_rows, :], chance[page, head].astype(low))
            d_proj[:, cols] = (jnp.where(side, found[0], found[1]) * scaling).astype(low)

        upstream_of(0)
        for pair in range(pairs):
            if pair + 1 < pairs:
                upstream_of(pair + 1)
            for half in range(2):
                head = 2 * pair + half
                for at in range(0, rows, block):
                    here = slice(half * rows + at, half * rows + at + block)
                    share = chance[page, head, at : at + block]
                    both = share * square[pair % 2, here]
                    d_scores = both - share * jnp.sum(both, axis=-1, keepdims=True)
                    square_low[pair % 2, here] = d_scores.astype(low)
            if pair > 0:
                consume(pair - 1)
        consume(pairs - 1)
        d_proj[:, width:] = back[...].astype(low).T
        sums[2] += column_sum(d_proj[:, 0:width])
        sums[3] += column_sum(d_proj[:, 2 * width :])
        for row, value in enumerate(sums):
            vectors[row : row + 1, :] += value
        right_copies(page)[0].start()
        right_copies(page)[4].start()
        def input_grad(parts):
            high_rows = rows // parts
            for part in range(parts):
                mine = slice(part * high_rows, (part + 1) * high_rows)
                work[mine] = dot_nt(d_proj[mine], w_in[...])
                for at in range(part * high_rows, (part + 1) * high_rows, block):
                    here = slice(at, at + block)
                    d_in = d_first[here] + work[here]
                    narrow = d_in.astype(low)
                    if parts == 2:
                        sent_grad[page, here] = narrow
                        d_in = narrow.astype(high)
                    input_grads[pl.ds(pl.multiple_of(page * rows + at, block), block), :] = d_in
                if parts == 2:
                    grad_copy(page, part).start()

        @pl.when(first)
        def _():
            input_grad(1)

        @pl.when(section == 1)
        def _():
            input_grad(2)

        return carry

    lax.fori_loop(0, pages, backward, 0)

    @pl.when(section == 1)
    def _():
        turn_plain()
        turn_slabs(2 * ff // width, False, 0)

    for page in range(pages):
        right_copies(page)[3].wait()
        if exchange:
            @pl.when(first)
            def _():
                near_copies(page)[-1].wait()

    for slot in (0, 1, 2, 4):
        right_copies(pages - 1)[slot].wait()
    for page in range(pages):
        @pl.when(first)
        def _():
            for part in range(2):
                result_copy(page, part).wait_send()

        @pl.when(section == 1)
        def _():
            for part in range(2):
                grad_copy(page, part).wait_send()


def both_passes(tokens, cotangent, lengths, buckets, layout, params, exchange):
    in_proj, out_proj, up_proj, down_proj, gains, offsets, bias, heads = params
    pages = lengths.shape[0]
    rows = tokens.shape[0] // pages
    width, ff = up_proj.shape
    sizes = (rows, width, heads, ff, pages)
    VM = pltpu.VMEM
    here, there = pl.BlockSpec(memory_space=pltpu.VMEM), pl.BlockSpec(memory_space=pl.ANY)
    scratch = [
        VM(in_proj.shape, low), VM(out_proj.shape, low), VM(up_proj.shape, low), VM(down_proj.shape, low),
        VM((pages, rows, width), low), VM((pages, rows, width), low), VM((pages, rows, width), low),
        VM((pages, rows, 3 * width), low),
        VM((pages, heads, rows, rows), high),
        VM((pages, rows, width), low),
        VM((pages, rows, width), high), VM((pages, rows, 1), high),
        VM((rows, width), high), VM((pages, rows, width), low),
        VM((pages, rows, ff), high),
        VM((pages, rows, ff), low),
        VM((pages, rows, width), high), VM((pages, rows, 1), high),
        VM((rows, heads * LANES), low),
        VM((rows, width), high),
        VM((2, 2 * rows, rows), high), VM((2, 2 * rows, rows), low),
        VM((rows, 2 * heads * LANES), low),
        VM((rows, 3 * width), low), VM((rows, width), low), VM((rows, ff), low), VM((pages, rows, width), low),
        VM((width, rows), low), VM((width, rows), low), VM((2 * width, rows), high),
        VM((rows, width), low), VM((rows, width), high),
        VM((pages * rows, LANES), low), VM((heads, LANES, LANES), low),
        VM((pages, rows, ff // 2), low), VM((2, width, pages * rows), low),
        pltpu.SemaphoreType.DMA((4,)), pltpu.SemaphoreType.DMA((pages,)), pltpu.SemaphoreType.DMA((2, 2 * ff // width)),
        pltpu.SemaphoreType.DMA((pages + 5,)), pltpu.SemaphoreType.DMA((4 * pages,)), pltpu.SemaphoreType.DMA((4 * pages,)),
        pltpu.SemaphoreType.DMA((pages, ff // width + 1)), pltpu.SemaphoreType.DMA((pages, ff // width + 1)),
    ]
    return pl.pallas_call(
        functools.partial(main_kernel, sizes, exchange),
        out_shape=(
            jax.ShapeDtypeStruct(tokens.shape, low),
            jax.ShapeDtypeStruct(tokens.shape, high),
            jax.ShapeDtypeStruct((3 * width, pages * rows), low),
            jax.ShapeDtypeStruct((ff // width, width // 2, 2 * pages * rows), low),
            jax.ShapeDtypeStruct((ff // width, width, pages * rows), low),
            jax.ShapeDtypeStruct((pages * rows, 5 * width + ff), low),
            jax.ShapeDtypeStruct((pages * rows, 2 * heads * LANES), low),
            jax.ShapeDtypeStruct((8, width), high),
            jax.ShapeDtypeStruct((1, ff), high),
            jax.ShapeDtypeStruct((pages * rows, width), low),
        ),
        in_specs=[pl.BlockSpec(memory_space=pltpu.SMEM), there, there, here, here, here, here, here] + [there] * 4,
        out_specs=(here, here, there, there, there, there, there, here, here, there),
        scratch_shapes=scratch,
        compiler_params=pltpu.CompilerParams(
            collective_id=0, has_side_effects=True, vmem_limit_bytes=63 * 2**20),
    )(lengths, tokens, cotangent, buckets, layout, gains, offsets, bias, in_proj, out_proj, up_proj, down_proj)


def marks_of(buckets):
    tokens = buckets.shape[1]
    level = lax.broadcasted_iota(jnp.int32, (BUCKETS, tokens), 0)
    rows = [jnp.where(buckets[axis : axis + 1, :] == level, 1.0, 0.0) for axis in range(3)]
    return jnp.concatenate(rows + [jnp.zeros((BUCKETS, tokens), high)], axis=0).astype(low)


def spread_tables(layout, spread):
    cells = BUCKETS * BUCKETS
    row = lax.broadcasted_iota(jnp.int32, (BUCKETS, cells), 0)
    own = lax.broadcasted_iota(jnp.int32, (BUCKETS, cells), 1) // BUCKETS == row
    cell = lax.broadcasted_iota(jnp.int32, (cells, LANES), 0) % BUCKETS
    place = lax.broadcasted_iota(jnp.int32, (cells, LANES), 1)
    heads = layout.shape[1]
    for axis in range(3):
        cellwise = layout[axis].astype(high)
        target = jnp.where(cell + axis * BUCKETS == place, 1.0, 0.0).astype(low)
        for head in range(heads):
            grid = jnp.where(own, cellwise[head : head + 1], 0.0).astype(low)
            spread[head, axis * BUCKETS : (axis + 1) * BUCKETS] = dot_nn(grid, target).astype(low)
    spread[:, 3 * BUCKETS :] = jnp.zeros((heads, LANES - 3 * BUCKETS, LANES), low)


def cross_tables(turned, cross):
    found = dot_nn(turned, cross)
    found = found[:, :LANES] + found[:, LANES:]
    place = lax.broadcasted_iota(jnp.int32, (BUCKETS, LANES), 1)
    return jnp.where(
        place < BUCKETS, found[:BUCKETS],
        jnp.where(place < 2 * BUCKETS, found[BUCKETS : 2 * BUCKETS], found[2 * BUCKETS : 3 * BUCKETS]))


LAGS = ((0, 3, 9, 13, 18), (0, 1, 3, 6, 11))


def down_turn(turn):
    return jnp.where(turn < 12, turn % 2 == 0, turn % 4 == 0)


def down_of(turn):
    return jnp.where(turn < 12, turn // 2, 3 + turn // 4)


def place_of(turn):
    other = jnp.where(turn < 12, turn // 2, turn - 6 - (turn - 9) // 4)
    other = jnp.where(other < 12, other + 12, jnp.where(other < 15, other - 3, other - 15))
    return jnp.where(down_turn(turn), 24 + down_of(turn), other)


def left_of(at):
    return jnp.where(at < 9, 0, jnp.where(at < 12, 1, 2))


def rs_kernel(
    count, levels, rows, cols, lags,
    plain_hbm, pair_hbm, full_hbm, right_hbm, cross_hbm, near_branch, buckets, vectors, bias_grad,
    out_in, out_out, out_up, out_down, out_tables, out_gains, out_offsets, out_bias,
    left, left_pair, left_full, right, right_down, cross, tables, dw, k1, k2, k3, s0, s1, s2, s3, r0, r1, r2, r3, ssem, rsem, left_sem, right_sem, left_down_sem, right_down_sem, cross_sem,
    ks, ks0, ks1, ks2, ss0, ss1, ss2, ss3, sr0, sr1, sr2, sr3, sssem, srsem,
):
    me = lax.axis_index("wide")
    keeps, sends, recvs = (dw, k1, k2, k3), (s0, s1, s2, s3), (r0, r1, r2, r3)
    skeeps, ssends, srecvs = (ks, ks0, ks1, ks2), (ss0, ss1, ss2, ss3), (sr0, sr1, sr2, sr3)
    bits = [(me // 2**level) % 2 for level in range(levels)]
    partners = [me + 2**level * (1 - 2 * bits[level]) for level in range(levels)]
    width = rows * 2**levels

    section = lax.axis_index("section")
    first = section == 0
    depth = right.shape[1]

    def left_load(block):
        return pltpu.make_async_copy(
            plain_hbm.at[pl.ds(pl.multiple_of(block * width, width), width)], left.at[block], left_sem.at[block])

    def right_load(block):
        return pltpu.make_async_copy(
            right_hbm.at[:, pl.ds(pl.multiple_of(block * cols, cols), cols)], right.at[block], right_sem.at[block])

    def pair_load(piece):
        return pltpu.make_async_copy(pair_hbm.at[piece], left_pair.at[piece], left_down_sem.at[piece])

    def full_load(piece):
        return pltpu.make_async_copy(full_hbm.at[piece], left_full.at[piece], left_down_sem.at[piece])

    def right_down_load(col):
        here = pl.ds(pl.multiple_of((right.shape[0] + col) * cols, cols), cols)
        return pltpu.make_async_copy(right_hbm.at[:, here], right_down.at[col, pl.ds(0, depth)], right_down_sem.at[0, col])

    def near_load(col):
        there = pl.ds(pl.multiple_of(col * cols, cols), cols)
        return pltpu.make_async_copy(near_branch.at[:, there], right_down.at[col, pl.ds(depth, depth)], right_down_sem.at[1, col])

    cross_load = pltpu.make_async_copy(cross_hbm, cross, cross_sem)
    barrier = pltpu.get_barrier_semaphore()
    for partner in partners:
        pl.semaphore_signal(barrier, inc=1, device_id={"wide": partner}, device_id_type=MESH)

    @pl.when(first)
    def _():
        pair_load(0).start()
        near_load(0).start()

    @pl.when(section == 1)
    def _():
        full_load(0).start()

    right_down_load(0).start()
    left_load(2).start()
    for block in range(12, 16):
        right_load(block).start()
    for col in (1, 2):
        right_down_load(col).start()

    @pl.when(first)
    def _():
        for col in (1, 2):
            near_load(col).start()
        for piece in (1, 2, 3):
            pair_load(piece).start()

    @pl.when(section == 1)
    def _():
        for piece in (1, 2, 3):
            full_load(piece).start()

    for block in range(16, 24):
        right_load(block).start()
    cross_load.start()
    for block in (1, 0):
        left_load(block).start()
    for block in range(0, 12):
        right_load(block).start()
    pl.semaphore_wait(barrier, levels)

    def copy(step, at, partner):
        return pltpu.make_async_remote_copy(
            src_ref=sends[step].at[at], dst_ref=recvs[step].at[at],
            send_sem=ssem.at[step, at], recv_sem=rsem.at[step, at],
            device_id={"wide": partners[partner]}, device_id_type=MESH)

    def small_copy(step):
        return pltpu.make_async_remote_copy(
            src_ref=ssends[step], dst_ref=srecvs[step],
            send_sem=sssem.at[step], recv_sem=srsem.at[step],
            device_id={"wide": partners[step]}, device_id_type=MESH)

    def cross_head(head):
        here = pl.ds(pl.multiple_of(head * 2 * LANES, 2 * LANES), 2 * LANES)
        tables[head] = cross_tables(marks_of(buckets), cross[:, here])

    def paired(turn):
        return jnp.logical_and(first, down_turn(turn))

    def far_first(turn):
        return jnp.logical_and(section == 1, turn % 6 == 2)

    def start(turn):
        at = place_of(turn)
        slot = turn % dw.shape[0]
        down = down_of(turn)
        piece, col = down // 3, down % 3

        def take(value):
            dw[slot] = value.reshape(dw.shape[1:])
            for j in range(2 ** (levels - 1)):
                s0[turn, j] = dw[slot, 2 * j + 1 - bits[0]].astype(low)
            copy(0, turn, 0).start()

        @pl.when(jnp.logical_and(down_turn(turn), down < 3))
        def _():
            right_down_load(down).wait()

        @pl.when(paired(turn))
        def _():
            @pl.when(down < 3)
            def _():
                near_load(down).wait()

            @pl.when(col == 0)
            def _():
                pair_load(piece).wait()

            found = dot_nn(left_pair[piece], right_down[col])
            dw[slot, 0 : 2 ** (levels - 1)] = found.reshape((2 ** (levels - 1),) + dw.shape[2:])

        @pl.when(jnp.logical_and(section == 1, down_turn(turn)))
        def _():
            @pl.when(col == 0)
            def _():
                full_load(piece).wait()

            take(dot_nn(left_full[piece], right_down[col, 0:depth]))

        @pl.when(jnp.logical_not(down_turn(turn)))
        def _():
            right_load(at).wait()

            @pl.when(jnp.logical_or(at == 12, jnp.logical_or(at == 9, at == 0)))
            def _():
                left_load(left_of(at)).wait()

            take(dot_nn(left[left_of(at)], right[at]))

    def pass_on(step, at, partner, place, total):
        half = 2 ** (levels - 1 - step)
        new = at % keeps[step].shape[0]
        bit = bits[partner]

        def pick(j, value):
            return (j >> place << (place + 1)) + (j & (2**place - 1)) + value * 2**place

        for j in range(half):
            sends[step][at, j] = total(pick(j, 1 - bit)).astype(low)
        copy(step, at, partner).start()
        for j in range(half):
            keeps[step][new, j] = total(pick(j, bit))

    def second(at, kind):
        old = at % dw.shape[0]
        if kind == "paired":
            pass_on(1, at, 0, 0, lambda pick: dw[old, pick])
            return
        copy(0, at, 0).wait_recv()
        partner, place = (2, 1) if kind == "far" else (1, 0)
        pass_on(1, at, partner, place, lambda pick: dw[old, 2 * pick + bits[0]] + r0[at, pick].astype(high))

    def later(step, at, kind):
        copy(step - 1, at, 0).wait_recv()
        old = at % keeps[step - 1].shape[0]
        partner, place = ((3, 1) if step == 2 else (1, 0)) if kind == "far" else (step, 0)
        pass_on(step, at, partner, place, lambda pick: keeps[step - 1][old, pick] + recvs[step - 1][at, pick].astype(high))

    def finish(turn):
        copy(levels - 1, turn, levels - 1).wait_recv()
        old = turn % keeps[levels - 1].shape[0]
        value = keeps[levels - 1][old, 0] + recvs[levels - 1][turn, 0].astype(high)
        at = place_of(turn)

        def columns(first):
            return pl.ds(pl.multiple_of((at - first) * cols, cols), cols)

        @pl.when(at < 9)
        def _():
            out_in[0, :, columns(0)] = value

        @pl.when(jnp.logical_and(at >= 9, at < 12))
        def _():
            out_out[0, :, columns(9)] = value

        @pl.when(jnp.logical_and(at >= 12, at < 24))
        def _():
            out_up[0, :, columns(12)] = value

        @pl.when(at >= 24)
        def _():
            part, col = (at - 24) // 3, at % 3
            out_down[0, pl.ds(pl.multiple_of(part * rows, rows), rows), pl.ds(pl.multiple_of(col * cols, cols), cols)] = value

    def small_fill():
        heads = tables.shape[0]
        for part in range(2**levels):
            for head in range(heads):
                ks[part, 2 * head : 2 * head + 2] = tables[head, 2 * part : 2 * part + 2]
            ks[part, 2 * heads : 2 * heads + 8, 0:rows] = vectors[:, part * rows : (part + 1) * rows]
            for piece in range(4):
                at = (4 * part + piece) * rows
                ks[part, 2 * heads + piece : 2 * heads + piece + 1, rows : 2 * rows] = bias_grad[:, at : at + rows]

    def small_stage(step):
        if step:
            small_copy(step - 1).wait_recv()
        if step == levels:
            heads = tables.shape[0]
            ks[0] = skeeps[levels - 1][0] + srecvs[levels - 1][0]
            for axis in range(3):
                for i in range(2):
                    got = ks[0, pl.ds(i, heads, 2), :]
                    out_tables[axis, :, 0, i * BUCKETS : (i + 1) * BUCKETS] = got[:, axis * BUCKETS : (axis + 1) * BUCKETS]
            out_gains[0] = ks[0, 2 * heads : 2 * heads + 2, 0:rows]
            out_offsets[:, 0] = ks[0, 2 * heads + 2 : 2 * heads + 8, 0:rows]
            for piece in range(4):
                out_bias[:, piece * rows : (piece + 1) * rows] = ks[0, 2 * heads + piece : 2 * heads + piece + 1, rows : 2 * rows]
            return
        half = 2 ** (levels - 1 - step)

        def total(pick):
            if step == 0:
                return ks[pick]
            return skeeps[step - 1][2 * pick + bits[0] if step == 1 else pick] + srecvs[step - 1][pick]

        for j in range(half):
            ssends[step][j] = total(2 * j + 1 - bits[step])
        small_copy(step).start()
        if step:
            for j in range(half):
                skeeps[step][j] = total(2 * j + bits[step])

    def step_at(moment, carry):
        @pl.when(moment == 5)
        def _():
            cross_load.wait()

        @pl.when(jnp.logical_and(moment >= 5, moment < 5 + tables.shape[0]))
        def _():
            cross_head(moment - 5)

        def due(at):
            return jnp.logical_and(at >= 0, at < count)

        @pl.when(due(moment))
        def _():
            start(moment)

        for step in range(1, levels + 1):
            near_at, pair_at = moment - lags[0][step], moment - lags[1][step]
            plain_due = jnp.logical_and(due(near_at), jnp.logical_not(paired(near_at)))
            pair_due = jnp.logical_and(due(pair_at), paired(pair_at))
            if step == 1:
                @pl.when(pair_due)
                def _():
                    second(pair_at, "paired")
            elif step < levels:
                @pl.when(pair_due)
                def _():
                    later(step, pair_at, "paired")
            else:
                @pl.when(pair_due)
                def _():
                    finish(pair_at)

                @pl.when(plain_due)
                def _():
                    finish(near_at)
                continue
            for kind in ("plain", "far"):
                chosen = far_first(near_at) if kind == "far" else jnp.logical_not(far_first(near_at))

                @pl.when(jnp.logical_and(plain_due, chosen))
                def _():
                    second(near_at, kind) if step == 1 else later(step, near_at, kind)
        return carry

    ks[...] = jnp.zeros_like(ks)
    lax.fori_loop(0, 19, step_at, 0)
    small_fill()
    small_stage(0)
    lax.fori_loop(19, 22, step_at, 0)
    small_stage(1)
    lax.fori_loop(22, count, step_at, 0)
    small_stage(2)
    small_stage(3)
    small_stage(4)
    lax.fori_loop(count, count + lags[0][levels], step_at, 0)

    def drain(at, carry):
        @pl.when(jnp.logical_not(paired(at)))
        def _():
            copy(0, at, 0).wait_send()

        for step in range(1, levels):
            copy(step, at, step).wait_send()
        return carry

    lax.fori_loop(0, count, drain, 0)
    for step in range(levels):
        small_copy(step).wait_send()


def reduce_grads(plain, pair, full, right, cross, near_branch, buckets, vectors, bias_grad, count=36, levels=4, lags=LAGS):
    n = 2**levels
    depth, total = right.shape
    width = vectors.shape[1]
    cols, rows = 256, width // n
    heads = cross.shape[1] // (2 * LANES)
    ff = bias_grad.shape[1]
    others = total // cols - width // cols

    def ring(step):
        return max(lag[step + 1] for lag in lags) - min(lag[step] for lag in lags) + 1

    VM = pltpu.VMEM
    scratch = [VM((3, width, depth), low), VM(pair.shape, low), VM(full.shape, low)]
    scratch += [VM((others, depth, cols), low), VM((width // cols, 2 * depth, cols), low)]
    scratch += [VM(cross.shape, low), VM((heads, BUCKETS, LANES), high)]
    scratch += [VM((ring(0), n, rows, cols), high)]
    scratch += [VM((ring(step), n >> (step + 1), rows, cols), high) for step in (1, 2, 3)]
    scratch += [VM((count, n >> (step + 1), rows, cols), low) for step in range(4)] * 2
    scratch += [pltpu.SemaphoreType.DMA((levels, count))] * 2
    scratch += [pltpu.SemaphoreType.DMA((3,)), pltpu.SemaphoreType.DMA((others,))]
    scratch += [pltpu.SemaphoreType.DMA((ff // width,)), pltpu.SemaphoreType.DMA((2, width // cols)), pltpu.SemaphoreType.DMA]
    few = (2 * heads + 8, LANES)
    scratch += [VM((n,) + few, high)]
    scratch += [VM((n >> (step + 1),) + few, high) for step in (1, 2, 3)]
    scratch += [VM((n >> (step + 1),) + few, high) for step in range(4)] * 2
    scratch += [pltpu.SemaphoreType.DMA((levels,))] * 2
    here, there = pl.BlockSpec(memory_space=pltpu.VMEM), pl.BlockSpec(memory_space=pl.ANY)
    shapes = (
        (1, rows, 3 * width), (1, rows, width), (1, rows, ff), (1, ff // n, width),
        (3, heads, 1, 2 * BUCKETS), (1, 2, rows), (6, 1, rows), (1, ff // n),
    )
    return pl.pallas_call(
        functools.partial(rs_kernel, count, levels, rows, cols, lags),
        out_shape=tuple(jax.ShapeDtypeStruct(shape, high) for shape in shapes),
        in_specs=[there] * 6 + [here] * 3,
        out_specs=(here,) * len(shapes),
        scratch_shapes=scratch,
        compiler_params=pltpu.CompilerParams(
            collective_id=1, has_side_effects=True, vmem_limit_bytes=63 * 2**20),
    )(plain, pair, full, right, cross, near_branch, buckets, vectors, bias_grad)


def settle_kernel(count, *refs):
    sources, targets, held, sem = refs[:count], refs[count : 2 * count], refs[2 * count : 3 * count], refs[3 * count]
    copies = [
        (pltpu.make_async_copy(sources[at], held[at], sem.at[0, at]), pltpu.make_async_copy(held[at], targets[at], sem.at[1, at]))
        for at in range(count)
    ]
    for fetch, _ in copies:
        fetch.start()
    for fetch, put in copies:
        fetch.wait()
        put.start()
    for _, put in copies:
        put.wait()


def settle(arrays):
    there = pl.BlockSpec(memory_space=pl.ANY)
    return pl.pallas_call(
        functools.partial(settle_kernel, len(arrays)),
        out_shape=tuple(jax.ShapeDtypeStruct(array.shape, array.dtype) for array in arrays),
        in_specs=[there] * len(arrays),
        out_specs=(there,) * len(arrays),
        scratch_shapes=[pltpu.VMEM(array.shape, array.dtype) for array in arrays] + [pltpu.SemaphoreType.DMA((2, len(arrays)))],
        compiler_params=pltpu.CompilerParams(vmem_limit_bytes=63 * 2**20),
    )(*arrays)


def local(tokens, cotangent, lengths, buckets, in_proj, out_proj, up_proj, down_proj, layout_tables, norm_gains, offsets, hidden_bias):
    heads = layout_tables.shape[2]
    width, ff = up_proj.shape[1:]
    shifts = jnp.transpose(offsets, (1, 0, 2))
    params = (in_proj[0], out_proj[0], up_proj[0], down_proj[0], norm_gains[0], shifts, hidden_bias, heads)
    wide_count = lax.axis_size("wide")
    result, input_grads, plain, pair, full, right, cross, vectors, bias_grad, near_branch = both_passes(
        tokens, cotangent, lengths, buckets, layout_tables[0], params, wide_count == 16)
    share = width // wide_count
    if wide_count == 16 and share % 16 == 0:
        found = reduce_grads(plain, pair, full, right, cross, near_branch, buckets, vectors, bias_grad)
        found = settle((result[None], input_grads[None]) + found)
        return found[:6] + (jnp.transpose(found[6], (2, 0, 1, 3)), found[7], jnp.transpose(found[8], (1, 0, 2)), found[9])
    else:

        def scattered(value, dim):
            return lax.psum_scatter(value[None], "wide", scatter_dimension=dim, tiled=True)

        def product(rows_from, cols_from, cols):
            return dot_nn(plain[rows_from : rows_from + width], right[:, cols_from : cols_from + cols])

        grad_in = scattered(product(0, 0, 3 * width), 1)
        grad_out = scattered(product(width, 3 * width, width), 1)
        grad_up = scattered(product(2 * width, 4 * width, ff), 1)
        grad_down = dot_nn(full.reshape(ff, -1), right[:, 4 * width + ff :])
        grad_down = grad_down.reshape(ff // width, 16, -1, width).transpose(1, 0, 2, 3).reshape(ff, width)
        grad_down = scattered(grad_down, 1)
        grad_hidden = scattered(bias_grad[0], 1)
        turned = marks_of(buckets)
        tables = jnp.stack([
            cross_tables(turned, cross[:, 2 * head * LANES : 2 * (head + 1) * LANES]) for head in range(heads)])
        tables = tables[:, :, : 3 * BUCKETS].reshape(heads, BUCKETS, 3, BUCKETS).transpose(2, 0, 1, 3)
        grad_tables = scattered(tables.reshape(3, heads, -1), 3)
        vectors = scattered(vectors, 2)
        grad_gains, grad_offsets = vectors[:, :2], vectors[:, 2:]
    return (
        result[None],
        input_grads[None],
        grad_in,
        grad_out,
        grad_up,
        grad_down,
        grad_tables,
        grad_gains,
        grad_offsets,
        grad_hidden,
    )


def solution(mesh):
    placed = (
        P("wide", None),
        P("wide", None),
        P("wide"),
        P(None, "wide"),
        P("section", None, None),
        P("section", None, None),
        P("section", None, None),
        P("section", None, None),
        P("section", None, None, None),
        P("section", None, None),
        P("section", None, None),
        P("section", None),
    )
    return jax.shard_map(
        local,
        mesh=mesh,
        in_specs=placed,
        out_specs=(
            P("section", "wide", None),
            P("section", "wide", None),
            P("section", "wide", None),
            P("section", "wide", None),
            P("section", "wide", None),
            P("section", "wide", None),
            P("section", None, None, "wide"),
            P("section", None, "wide"),
            P("section", None, "wide"),
            P("section", "wide"),
        ),
        check_vma=False,
    )
```

```python
import functools

import jax
import jax.numpy as jnp
from jax import lax
from jax.experimental import pallas as pl
from jax.experimental.pallas import tpu as pltpu
from jax.sharding import PartitionSpec as P

MESH = pl.DeviceIdType.MESH
BUCKETS = 32
LANES = 128
epsilon = 1e-05
masked_score = -1000000000.0
low = jnp.bfloat16
high = jnp.float32


def dot_nn(left, right):
    return jnp.dot(left, right, preferred_element_type=high)


def dot_nt(left, right):
    return lax.dot_general(left, right, (((1,), (1,)), ((), ())), preferred_element_type=high)


def normal_terms(values):
    below = 0.5 + 0.5 * lax.erf(values * 0.7071067811865476)
    return below, values * (0.3989422804014327 * jnp.exp(-0.5 * values * values))


def norm_rows(values):
    centered = values - jnp.mean(values, axis=-1, keepdims=True)
    spread = jnp.mean(centered * centered, axis=-1, keepdims=True)
    scale = lax.rsqrt(spread + epsilon)
    return centered * scale, scale


def norm_back(upstream, gain, normal, scale):
    scaled = upstream * gain
    middle = jnp.mean(scaled, axis=-1, keepdims=True)
    along = jnp.mean(scaled * normal, axis=-1, keepdims=True)
    return scale * (scaled - middle - normal * along)


def column_sum(values):
    return jnp.sum(values.astype(high), axis=0, keepdims=True)


def main_kernel(
    sizes, exchange,
    lengths, tokens, cotangent, buckets, layout, gains, offsets, bias,
    in_hbm, out_hbm, up_hbm, down_hbm,
    result_hbm, input_grads_hbm, plain_hbm, pair_hbm, full_hbm, right_hbm, cross_hbm, vectors, bias_grad, near_branch,
    w_in, w_out, w_up, w_down, arrive, arrive_grad, sent_grad,
    qkv, chance, context, normal_one, scale_one, normed, normed_low, slope, hidden,
    normal_two, scale_two, picked, work, square, square_low, cross, d_proj, d_att, d_before, d_branch,
    turned, turned_grad, back, d_context, d_first, onehot, spread, near_hidden, spun, result, input_grads,
    load_sem, page_sem, spun_sem, right_sem, send_sem, recv_sem, near_send, near_recv, final_sem,
):
    rows, width, heads, ff, pages = sizes
    size = width // heads
    pairs = heads // 2
    section = lax.axis_index("section")
    first = section == 0
    block = 64
    chunk = 512
    me = lax.axis_index("wide")
    side_bit = (me // 2) % 2
    near = me + 2 - 4 * side_bit
    slim = width // 2

    def near_copies(page):
        found = []
        for slot in range(ff // width):
            at = pl.multiple_of(slot * width + (1 - side_bit) * slim, LANES)
            found.append((hidden.at[page, :, pl.ds(at, slim)], near_hidden.at[page, :, pl.ds(slot * slim, slim)]))
        found.append((d_branch.at[page], near_branch.at[page_rows(page)]))
        return [
            pltpu.make_async_remote_copy(
                src_ref=src, dst_ref=dst, send_sem=near_send.at[page, slot], recv_sem=near_recv.at[page, slot],
                device_id={"wide": near}, device_id_type=MESH)
            for slot, (src, dst) in enumerate(found)
        ]

    def peer_copy(src, dst, slot):
        return pltpu.make_async_remote_copy(
            src_ref=src, dst_ref=dst, send_sem=send_sem.at[slot], recv_sem=recv_sem.at[slot],
            device_id={"section": 1 - section}, device_id_type=MESH)

    def page_rows(page):
        return pl.ds(pl.multiple_of(page * rows, rows), rows)

    loads = [pltpu.make_async_copy(src, dst, load_sem.at[at]) for at, (src, dst) in enumerate(
        ((in_hbm, w_in), (out_hbm, w_out), (up_hbm, w_up), (down_hbm, w_down)))]

    def own_copy(page):
        return pltpu.make_async_copy(tokens.at[page_rows(page)], arrive.at[page], page_sem.at[page])

    def own_grad_copy(page):
        return pltpu.make_async_copy(cotangent.at[page_rows(page)], arrive_grad.at[page], page_sem.at[page])

    @pl.when(first)
    def _():
        for page in range(pages):
            own_copy(page).start()

    for load in loads:
        load.start()

    @pl.when(section == 1)
    def _():
        for page in range(pages):
            own_grad_copy(page).start()

    barrier = pltpu.get_barrier_semaphore()
    pl.semaphore_signal(barrier, inc=1, device_id={"section": 1 - section}, device_id_type=MESH)
    if exchange:
        pl.semaphore_signal(barrier, inc=1, device_id={"wide": near}, device_id_type=MESH)
    pl.semaphore_wait(barrier, 2 if exchange else 1)

    onehot[...] = marks_of(buckets).T
    spread_tables(layout, spread)
    vectors[...] = jnp.zeros_like(vectors)
    bias_grad[...] = jnp.zeros_like(bias_grad)

    share = width // 16
    pieces = ff // width
    both = pages * rows

    def plain_copy(block):
        return pltpu.make_async_copy(
            spun.at[block % 2], plain_hbm.at[pl.ds(block * width, width)], spun_sem.at[block % 2, 0])

    def turn_plain():
        for block, source in enumerate((arrive, context, normed_low)):
            if block > 1:
                plain_copy(block - 2).wait()
            for page in range(pages):
                spun[block % 2, :, page * rows : (page + 1) * rows] = source[page].T
            plain_copy(block).start()
        for block in (1, 2):
            plain_copy(block).wait()

    def slab_copies(block, slot, pair, far):
        found = []
        for core in range(2):
            for piece in range(pieces):
                source = spun.at[slot, pl.ds((core * pieces + piece) * share, share)]
                row = pl.multiple_of((2 * block + core) * share, share)
                if pair:
                    target = pair_hbm.at[piece, pl.ds(row, share), pl.ds(far * both, both)]
                else:
                    target = full_hbm.at[piece, pl.ds(row, share)]
                found.append(pltpu.make_async_copy(source, target, spun_sem.at[slot, core * pieces + piece]))
        return found

    def turn_slabs(count, pair, far):
        def one(block, carry):
            slot = block % 2

            @pl.when(block > 1)
            def _():
                for copy in slab_copies(block - 2, slot, pair, far):
                    copy.wait()

            for page in range(pages):
                if far:
                    slab = near_hidden[page, :, pl.ds(pl.multiple_of(block * slim, LANES), slim)]
                elif pair:
                    slab = hidden[page, :, pl.ds(pl.multiple_of(block * width + side_bit * slim, LANES), slim)]
                else:
                    slab = hidden[page, :, pl.ds(pl.multiple_of(block * slim, LANES), slim)]
                spun[slot, 0:slim, page * rows : (page + 1) * rows] = slab.T
            for copy in slab_copies(block, slot, pair, far):
                copy.start()
            return carry

        lax.fori_loop(0, count, one, 0)
        for block in (count - 2, count - 1):
            for copy in slab_copies(block, block % 2, pair, far):
                copy.wait()

    def right_copies(page):
        found, at = [], 0
        for slot, piece in enumerate((d_proj, d_att, d_before, d_branch.at[page])):
            cols = piece.shape[-1]
            found.append(pltpu.make_async_copy(
                piece, right_hbm.at[page_rows(page), pl.ds(at, cols)], right_sem.at[page if slot == 3 else pages + slot]))
            at += cols
        found.append(pltpu.make_async_copy(cross, cross_hbm.at[page_rows(page)], right_sem.at[pages + 4]))
        return found

    lane = lax.broadcasted_iota(jnp.int32, (rows, LANES), 1)
    side = lane < size

    tall = rows // 2

    def final_copies(page):
        return [
            pltpu.make_async_copy(source.at[page_rows(page)], target.at[page_rows(page)], final_sem.at[slot, page])
            for slot, (source, target) in enumerate(((result, result_hbm), (input_grads, input_grads_hbm)))
        ]

    def result_copy(page, part):
        here = pl.ds(pl.multiple_of(page * rows + part * tall, tall), tall)
        return peer_copy(result.at[here], arrive.at[page, pl.ds(part * tall, tall)], 2 * page + part)

    def grad_copy(page, part):
        here = pl.ds(part * tall, tall)
        return peer_copy(sent_grad.at[page, here], arrive_grad.at[page, here], 2 * pages + 2 * page + part)

    def forward(page, carry):
        @pl.when(first)
        def _():
            own_copy(page).wait()

        @pl.when(section == 1)
        def _():
            for part in range(2):
                result_copy(page, part).wait_recv()

        @pl.when(page == 0)
        def _():
            loads[0].wait()

        layer_in = arrive[page]
        for part in range(3):
            cols = slice(part * width, (part + 1) * width)
            found = dot_nn(layer_in, w_in[:, cols])
            if part != 1:
                found = found + offsets[part // 2]
            qkv[page, :, cols] = found.astype(low)
        mark = onehot[page_rows(page), :]
        for head in range(heads):
            picked[:, head * LANES : (head + 1) * LANES] = dot_nn(mark, spread[head]).astype(low)
        live = lax.broadcasted_iota(jnp.int32, (1, rows), 1) < lengths[page]
        zero = jnp.zeros((rows, LANES), low)

        def scores_of(pair):
            cols = slice(pair * LANES, (pair + 1) * LANES)
            query = qkv[page, :, cols] * jnp.asarray(size**-0.5, low)
            keyed = jnp.concatenate([qkv[page, :, width + pair * LANES : width + (pair + 1) * LANES], mark], axis=1)
            parts = []
            for half in range(2):
                head = 2 * pair + half
                mine = jnp.where(side if half == 0 else ~side, query, zero)
                parts.append(jnp.concatenate([mine, picked[:, head * LANES : (head + 1) * LANES]], axis=1))
            square[pair % 2] = dot_nt(jnp.concatenate(parts, axis=0), keyed)

        def attend(pair):
            cols = slice(pair * LANES, (pair + 1) * LANES)
            valued = qkv[page, :, 2 * width + pair * LANES : 2 * width + (pair + 1) * LANES]
            got = dot_nn(square_low[pair % 2], valued)
            context[page, :, cols] = jnp.where(side, got[:rows], got[rows:]).astype(low)

        scores_of(0)
        for pair in range(pairs):
            if pair + 1 < pairs:
                scores_of(pair + 1)
            for at in range(0, 2 * rows, block):
                scores = jnp.where(live, square[pair % 2, at : at + block], masked_score)
                raised = jnp.exp(scores - jnp.max(scores, axis=-1, keepdims=True))
                share = raised * (1.0 / jnp.sum(raised, axis=-1, keepdims=True))
                chance[page, 2 * pair + at // rows, at % rows : at % rows + block] = share
                square_low[pair % 2, at : at + block] = share.astype(low)
            if pair > 0:
                attend(pair - 1)
        attend(pairs - 1)

        @pl.when(page == 0)
        def _():
            loads[1].wait()

        work[...] = dot_nn(context[page], w_out[...])

        for at in range(0, rows, block):
            here = slice(at, at + block)
            summed = arrive[page, here].astype(high) + (work[here] + offsets[2])
            normal, scale = norm_rows(summed)
            normal_one[page, here] = normal
            scale_one[page, here] = scale
            shifted = normal * gains[0:1] + offsets[3]
            normed[here] = shifted
            normed_low[page, here] = shifted.astype(low)

        @pl.when(page == 0)
        def _():
            loads[2].wait()
            loads[3].wait()

        def feed_forward(parts):
            high_rows = rows // parts
            for part in range(parts):
                mine = slice(part * high_rows, (part + 1) * high_rows)
                for at in range(0, ff, chunk):
                    cols = slice(at, at + chunk)
                    before = dot_nn(normed_low[page, mine], w_up[:, cols]) + bias[:, cols]
                    below, density = normal_terms(before)
                    hidden[page, mine, cols] = (before * below).astype(low)
                    slope[page, mine, cols] = (below + density).astype(slope.dtype)
                work[mine] = dot_nn(hidden[page, mine], w_down[...])
                for at in range(part * high_rows, (part + 1) * high_rows, block):
                    here = slice(at, at + block)
                    normal, scale = norm_rows(normed[here] + (work[here] + offsets[4]))
                    normal_two[page, here] = normal
                    scale_two[page, here] = scale
                    result[pl.ds(pl.multiple_of(page * rows + at, block), block), :] = (
                        normal * gains[1:2] + offsets[5]).astype(low)
                if parts == 2:
                    result_copy(page, part).start()

        @pl.when(first)
        def _():
            feed_forward(2)

        @pl.when(section == 1)
        def _():
            feed_forward(1)

        final_copies(page)[0].start()
        if exchange:
            @pl.when(first)
            def _():
                for copy in near_copies(page)[:-1]:
                    copy.start()

        return carry

    lax.fori_loop(0, pages, forward, 0)

    @pl.when(first)
    def _():
        turn_plain()
        if exchange:
            turn_slabs(ff // width, True, 0)
            for page in range(pages):
                for copy in near_copies(page)[:-1]:
                    copy.wait()
            turn_slabs(ff // width, True, 1)
        else:
            turn_slabs(2 * ff // width, False, 0)

    def backward(page, carry):
        @pl.when(section == 1)
        def _():
            own_grad_copy(page).wait()

        sums = [jnp.zeros((1, width), high) for _ in range(8)]

        @pl.when(page > 0)
        def _():
            right_copies(page - 1)[2].wait()

        def feed_back(parts):
            high_rows = rows // parts
            totals = {1: 0.0, 6: 0.0, 7: 0.0}
            for part in range(parts):
                if parts == 2:
                    grad_copy(page, part).wait_recv()
                mine = slice(part * high_rows, (part + 1) * high_rows)
                for at in range(part * high_rows, (part + 1) * high_rows, block):
                    here = slice(at, at + block)
                    upstream = arrive_grad[page, here].astype(high)
                    normal = normal_two[page, here]
                    totals[1] += column_sum(upstream * normal)
                    totals[7] += column_sum(upstream)
                    d_second = norm_back(upstream, gains[1:2], normal, scale_two[page, here])
                    d_first[here] = d_second
                    branch = d_second.astype(low)
                    totals[6] += column_sum(branch)
                    d_branch[page, here] = branch
                if part == parts - 1:
                    right_copies(page)[3].start()
                    if exchange and parts == 2:
                        near_copies(page)[-1].start()
                for at in range(0, ff, chunk):
                    cols = slice(at, at + chunk)
                    d_hidden = dot_nt(d_branch[page, mine], w_down[cols, :])
                    d_chunk = (d_hidden * slope[page, mine, cols].astype(high)).astype(low)
                    d_before[mine, cols] = d_chunk
                    bias_grad[:, cols] += column_sum(d_chunk)
                work[mine] = dot_nt(d_before[mine], w_up[...])
            for row, value in totals.items():
                vectors[row : row + 1, :] += value

        @pl.when(first)
        def _():
            feed_back(2)

        @pl.when(section == 1)
        def _():
            feed_back(1)

        right_copies(page)[2].start()

        @pl.when(page > 0)
        def _():
            right_copies(page - 1)[1].wait()

        for at in range(0, rows, block):
            here = slice(at, at + block)
            d_normed = d_first[here] + work[here]
            normal = normal_one[page, here]
            sums[0] += column_sum(d_normed * normal)
            sums[5] += column_sum(d_normed)
            found = norm_back(d_normed, gains[0:1], normal, scale_one[page, here])
            d_first[here] = found
            attended = found.astype(low)
            sums[4] += column_sum(attended)
            d_att[here] = attended
        right_copies(page)[1].start()
        d_context[...] = dot_nt(d_att[...], w_out[...]).astype(low)
        turned[...] = qkv[page, :, 0:width].T
        turned_grad[...] = d_context[...].T
        mark = onehot[page_rows(page), :]
        zero = jnp.zeros((rows, LANES), low)
        scaling = size**-0.5

        @pl.when(page > 0)
        def _():
            right_copies(page - 1)[0].wait()

        @pl.when(page > 0)
        def _():
            right_copies(page - 1)[4].wait()

        def upstream_of(pair):
            valued = qkv[page, :, 2 * width + pair * LANES : 2 * width + (pair + 1) * LANES]
            given = d_context[:, pair * LANES : (pair + 1) * LANES]
            parts = [jnp.where(side, given, zero), jnp.where(side, zero, given)]
            square[pair % 2] = dot_nt(jnp.concatenate(parts, axis=0), valued)

        def consume(pair):
            cols = slice(pair * LANES, (pair + 1) * LANES)
            keyed = jnp.concatenate([qkv[page, :, width + pair * LANES : width + (pair + 1) * LANES], mark], axis=1)
            found = []
            joined = dot_nn(square_low[pair % 2], keyed)
            for half in range(2):
                head = 2 * pair + half
                slim_rows = slice(head * size, (head + 1) * size)
                both = joined[half * rows : (half + 1) * rows]
                found.append(both[:, :LANES])
                rest = both[:, LANES:]
                upper = rest.astype(low)
                lower = (rest - upper.astype(high)).astype(low)
                cross[:, 2 * head * LANES : (2 * head + 1) * LANES] = upper
                cross[:, (2 * head + 1) * LANES : (2 * head + 2) * LANES] = lower
                back[slim_rows, :] = dot_nn(turned[slim_rows, :], square_low[pair % 2, half * rows : (half + 1) * rows]) * scaling
                back[slice(width + head * size, width + (head + 1) * size), :] = dot_nn(
                    turned_grad[slim_rows, :], chance[page, head].astype(low))
            d_proj[:, cols] = (jnp.where(side, found[0], found[1]) * scaling).astype(low)

        upstream_of(0)
        for pair in range(pairs):
            if pair + 1 < pairs:
                upstream_of(pair + 1)
            for half in range(2):
                head = 2 * pair + half
                for at in range(0, rows, block):
                    here = slice(half * rows + at, half * rows + at + block)
                    share = chance[page, head, at : at + block]
                    both = share * square[pair % 2, here]
                    d_scores = both - share * jnp.sum(both, axis=-1, keepdims=True)
                    square_low[pair % 2, here] = d_scores.astype(low)
            if pair > 0:
                consume(pair - 1)
        consume(pairs - 1)
        d_proj[:, width:] = back[...].astype(low).T
        sums[2] += column_sum(d_proj[:, 0:width])
        sums[3] += column_sum(d_proj[:, 2 * width :])
        for row, value in enumerate(sums):
            vectors[row : row + 1, :] += value
        right_copies(page)[0].start()
        right_copies(page)[4].start()
        def input_grad(parts):
            high_rows = rows // parts
            for part in range(parts):
                mine = slice(part * high_rows, (part + 1) * high_rows)
                work[mine] = dot_nt(d_proj[mine], w_in[...])
                for at in range(part * high_rows, (part + 1) * high_rows, block):
                    here = slice(at, at + block)
                    d_in = d_first[here] + work[here]
                    narrow = d_in.astype(low)
                    if parts == 2:
                        sent_grad[page, here] = narrow
                        d_in = narrow.astype(high)
                    input_grads[pl.ds(pl.multiple_of(page * rows + at, block), block), :] = d_in
                if parts == 2:
                    grad_copy(page, part).start()

        @pl.when(first)
        def _():
            input_grad(1)

        @pl.when(section == 1)
        def _():
            input_grad(2)

        final_copies(page)[1].start()
        return carry

    lax.fori_loop(0, pages, backward, 0)

    @pl.when(section == 1)
    def _():
        turn_plain()
        turn_slabs(2 * ff // width, False, 0)

    for page in range(pages):
        right_copies(page)[3].wait()
        for copy in final_copies(page):
            copy.wait()
        if exchange:
            @pl.when(first)
            def _():
                near_copies(page)[-1].wait()

    for slot in (0, 1, 2, 4):
        right_copies(pages - 1)[slot].wait()
    for page in range(pages):
        @pl.when(first)
        def _():
            for part in range(2):
                result_copy(page, part).wait_send()

        @pl.when(section == 1)
        def _():
            for part in range(2):
                grad_copy(page, part).wait_send()


def both_passes(tokens, cotangent, lengths, buckets, layout, params, exchange):
    in_proj, out_proj, up_proj, down_proj, gains, offsets, bias, heads = params
    pages = lengths.shape[0]
    rows = tokens.shape[0] // pages
    width, ff = up_proj.shape
    sizes = (rows, width, heads, ff, pages)
    VM = pltpu.VMEM
    here, there = pl.BlockSpec(memory_space=pltpu.VMEM), pl.BlockSpec(memory_space=pl.ANY)
    scratch = [
        VM(in_proj.shape, low), VM(out_proj.shape, low), VM(up_proj.shape, low), VM(down_proj.shape, low),
        VM((pages, rows, width), low), VM((pages, rows, width), low), VM((pages, rows, width), low),
        VM((pages, rows, 3 * width), low),
        VM((pages, heads, rows, rows), high),
        VM((pages, rows, width), low),
        VM((pages, rows, width), high), VM((pages, rows, 1), high),
        VM((rows, width), high), VM((pages, rows, width), low),
        VM((pages, rows, ff), high),
        VM((pages, rows, ff), low),
        VM((pages, rows, width), high), VM((pages, rows, 1), high),
        VM((rows, heads * LANES), low),
        VM((rows, width), high),
        VM((2, 2 * rows, rows), high), VM((2, 2 * rows, rows), low),
        VM((rows, 2 * heads * LANES), low),
        VM((rows, 3 * width), low), VM((rows, width), low), VM((rows, ff), low), VM((pages, rows, width), low),
        VM((width, rows), low), VM((width, rows), low), VM((2 * width, rows), high),
        VM((rows, width), low), VM((rows, width), high),
        VM((pages * rows, LANES), low), VM((heads, LANES, LANES), low),
        VM((pages, rows, ff // 2), low), VM((2, width, pages * rows), low),
        VM(tokens.shape, low), VM(tokens.shape, high),
        pltpu.SemaphoreType.DMA((4,)), pltpu.SemaphoreType.DMA((pages,)), pltpu.SemaphoreType.DMA((2, 2 * ff // width)),
        pltpu.SemaphoreType.DMA((pages + 5,)), pltpu.SemaphoreType.DMA((4 * pages,)), pltpu.SemaphoreType.DMA((4 * pages,)),
        pltpu.SemaphoreType.DMA((pages, ff // width + 1)), pltpu.SemaphoreType.DMA((pages, ff // width + 1)),
        pltpu.SemaphoreType.DMA((2, pages)),
    ]
    return pl.pallas_call(
        functools.partial(main_kernel, sizes, exchange),
        out_shape=(
            jax.ShapeDtypeStruct(tokens.shape, low),
            jax.ShapeDtypeStruct(tokens.shape, high),
            jax.ShapeDtypeStruct((3 * width, pages * rows), low),
            jax.ShapeDtypeStruct((ff // width, width // 2, 2 * pages * rows), low),
            jax.ShapeDtypeStruct((ff // width, width, pages * rows), low),
            jax.ShapeDtypeStruct((pages * rows, 5 * width + ff), low),
            jax.ShapeDtypeStruct((pages * rows, 2 * heads * LANES), low),
            jax.ShapeDtypeStruct((8, width), high),
            jax.ShapeDtypeStruct((1, ff), high),
            jax.ShapeDtypeStruct((pages * rows, width), low),
        ),
        in_specs=[pl.BlockSpec(memory_space=pltpu.SMEM), there, there, here, here, here, here, here] + [there] * 4,
        out_specs=(there,) * 7 + (here, here, there),
        scratch_shapes=scratch,
        compiler_params=pltpu.CompilerParams(
            collective_id=0, has_side_effects=True, vmem_limit_bytes=63 * 2**20),
    )(lengths, tokens, cotangent, buckets, layout, gains, offsets, bias, in_proj, out_proj, up_proj, down_proj)


def marks_of(buckets):
    tokens = buckets.shape[1]
    level = lax.broadcasted_iota(jnp.int32, (BUCKETS, tokens), 0)
    rows = [jnp.where(buckets[axis : axis + 1, :] == level, 1.0, 0.0) for axis in range(3)]
    return jnp.concatenate(rows + [jnp.zeros((BUCKETS, tokens), high)], axis=0).astype(low)


def spread_tables(layout, spread):
    cells = BUCKETS * BUCKETS
    row = lax.broadcasted_iota(jnp.int32, (BUCKETS, cells), 0)
    own = lax.broadcasted_iota(jnp.int32, (BUCKETS, cells), 1) // BUCKETS == row
    cell = lax.broadcasted_iota(jnp.int32, (cells, LANES), 0) % BUCKETS
    place = lax.broadcasted_iota(jnp.int32, (cells, LANES), 1)
    heads = layout.shape[1]
    for axis in range(3):
        cellwise = layout[axis].astype(high)
        target = jnp.where(cell + axis * BUCKETS == place, 1.0, 0.0).astype(low)
        for head in range(heads):
            grid = jnp.where(own, cellwise[head : head + 1], 0.0).astype(low)
            spread[head, axis * BUCKETS : (axis + 1) * BUCKETS] = dot_nn(grid, target).astype(low)
    spread[:, 3 * BUCKETS :] = jnp.zeros((heads, LANES - 3 * BUCKETS, LANES), low)


def cross_tables(turned, cross):
    found = dot_nn(turned, cross)
    found = found[:, :LANES] + found[:, LANES:]
    place = lax.broadcasted_iota(jnp.int32, (BUCKETS, LANES), 1)
    return jnp.where(
        place < BUCKETS, found[:BUCKETS],
        jnp.where(place < 2 * BUCKETS, found[BUCKETS : 2 * BUCKETS], found[2 * BUCKETS : 3 * BUCKETS]))


LAGS = ((0, 3, 9, 13, 18), (0, 1, 3, 6, 11))


def down_turn(turn):
    return jnp.where(turn < 12, turn % 2 == 0, turn % 4 == 0)


def down_of(turn):
    return jnp.where(turn < 12, turn // 2, 3 + turn // 4)


def place_of(turn):
    other = jnp.where(turn < 12, turn // 2, turn - 6 - (turn - 9) // 4)
    other = jnp.where(other < 12, other + 12, jnp.where(other < 15, other - 3, other - 15))
    return jnp.where(down_turn(turn), 24 + down_of(turn), other)


def left_of(at):
    return jnp.where(at < 9, 0, jnp.where(at < 12, 1, 2))


def rs_kernel(
    count, levels, rows, cols, lags,
    plain_hbm, pair_hbm, full_hbm, right_hbm, cross_hbm, near_branch, buckets, vectors, bias_grad,
    out_in, out_out, out_up, out_down, out_tables, out_gains, out_offsets, out_bias,
    left, left_pair, left_full, right, right_down, cross, tables, dw, k1, k2, k3, s0, s1, s2, s3, r0, r1, r2, r3, ssem, rsem, left_sem, right_sem, left_down_sem, right_down_sem, cross_sem,
    ks, ks0, ks1, ks2, ss0, ss1, ss2, ss3, sr0, sr1, sr2, sr3, sssem, srsem,
):
    me = lax.axis_index("wide")
    keeps, sends, recvs = (dw, k1, k2, k3), (s0, s1, s2, s3), (r0, r1, r2, r3)
    skeeps, ssends, srecvs = (ks, ks0, ks1, ks2), (ss0, ss1, ss2, ss3), (sr0, sr1, sr2, sr3)
    bits = [(me // 2**level) % 2 for level in range(levels)]
    partners = [me + 2**level * (1 - 2 * bits[level]) for level in range(levels)]
    width = rows * 2**levels

    section = lax.axis_index("section")
    first = section == 0
    depth = right.shape[1]

    def left_load(block):
        return pltpu.make_async_copy(
            plain_hbm.at[pl.ds(pl.multiple_of(block * width, width), width)], left.at[block], left_sem.at[block])

    def right_load(block):
        return pltpu.make_async_copy(
            right_hbm.at[:, pl.ds(pl.multiple_of(block * cols, cols), cols)], right.at[block], right_sem.at[block])

    def pair_load(piece):
        return pltpu.make_async_copy(pair_hbm.at[piece], left_pair.at[piece], left_down_sem.at[piece])

    def full_load(piece):
        return pltpu.make_async_copy(full_hbm.at[piece], left_full.at[piece], left_down_sem.at[piece])

    def right_down_load(col):
        here = pl.ds(pl.multiple_of((right.shape[0] + col) * cols, cols), cols)
        return pltpu.make_async_copy(right_hbm.at[:, here], right_down.at[col, pl.ds(0, depth)], right_down_sem.at[0, col])

    def near_load(col):
        there = pl.ds(pl.multiple_of(col * cols, cols), cols)
        return pltpu.make_async_copy(near_branch.at[:, there], right_down.at[col, pl.ds(depth, depth)], right_down_sem.at[1, col])

    cross_load = pltpu.make_async_copy(cross_hbm, cross, cross_sem)
    barrier = pltpu.get_barrier_semaphore()
    for partner in partners:
        pl.semaphore_signal(barrier, inc=1, device_id={"wide": partner}, device_id_type=MESH)

    @pl.when(first)
    def _():
        pair_load(0).start()
        near_load(0).start()

    @pl.when(section == 1)
    def _():
        full_load(0).start()

    right_down_load(0).start()
    left_load(2).start()
    for block in range(12, 16):
        right_load(block).start()
    for col in (1, 2):
        right_down_load(col).start()

    @pl.when(first)
    def _():
        for col in (1, 2):
            near_load(col).start()
        for piece in (1, 2, 3):
            pair_load(piece).start()

    @pl.when(section == 1)
    def _():
        for piece in (1, 2, 3):
            full_load(piece).start()

    for block in range(16, 24):
        right_load(block).start()
    cross_load.start()
    for block in (1, 0):
        left_load(block).start()
    for block in range(0, 12):
        right_load(block).start()
    pl.semaphore_wait(barrier, levels)

    def copy(step, at, partner):
        return pltpu.make_async_remote_copy(
            src_ref=sends[step].at[at], dst_ref=recvs[step].at[at],
            send_sem=ssem.at[step, at], recv_sem=rsem.at[step, at],
            device_id={"wide": partners[partner]}, device_id_type=MESH)

    def small_copy(step):
        return pltpu.make_async_remote_copy(
            src_ref=ssends[step], dst_ref=srecvs[step],
            send_sem=sssem.at[step], recv_sem=srsem.at[step],
            device_id={"wide": partners[step]}, device_id_type=MESH)

    def cross_head(head):
        here = pl.ds(pl.multiple_of(head * 2 * LANES, 2 * LANES), 2 * LANES)
        tables[head] = cross_tables(marks_of(buckets), cross[:, here])

    def paired(turn):
        return jnp.logical_and(first, down_turn(turn))

    def far_first(turn):
        return jnp.logical_and(section == 1, turn % 6 == 2)

    def start(turn):
        at = place_of(turn)
        slot = turn % dw.shape[0]
        down = down_of(turn)
        piece, col = down // 3, down % 3

        def take(value):
            dw[slot] = value.reshape(dw.shape[1:])
            for j in range(2 ** (levels - 1)):
                s0[turn, j] = dw[slot, 2 * j + 1 - bits[0]].astype(low)
            copy(0, turn, 0).start()

        @pl.when(jnp.logical_and(down_turn(turn), down < 3))
        def _():
            right_down_load(down).wait()

        @pl.when(paired(turn))
        def _():
            @pl.when(down < 3)
            def _():
                near_load(down).wait()

            @pl.when(col == 0)
            def _():
                pair_load(piece).wait()

            found = dot_nn(left_pair[piece], right_down[col])
            dw[slot, 0 : 2 ** (levels - 1)] = found.reshape((2 ** (levels - 1),) + dw.shape[2:])

        @pl.when(jnp.logical_and(section == 1, down_turn(turn)))
        def _():
            @pl.when(col == 0)
            def _():
                full_load(piece).wait()

            take(dot_nn(left_full[piece], right_down[col, 0:depth]))

        @pl.when(jnp.logical_not(down_turn(turn)))
        def _():
            right_load(at).wait()

            @pl.when(jnp.logical_or(at == 12, jnp.logical_or(at == 9, at == 0)))
            def _():
                left_load(left_of(at)).wait()

            take(dot_nn(left[left_of(at)], right[at]))

    def pass_on(step, at, partner, place, total):
        half = 2 ** (levels - 1 - step)
        new = at % keeps[step].shape[0]
        bit = bits[partner]

        def pick(j, value):
            return (j >> place << (place + 1)) + (j & (2**place - 1)) + value * 2**place

        for j in range(half):
            sends[step][at, j] = total(pick(j, 1 - bit)).astype(low)
        copy(step, at, partner).start()
        for j in range(half):
            keeps[step][new, j] = total(pick(j, bit))

    def second(at, kind):
        old = at % dw.shape[0]
        if kind == "paired":
            pass_on(1, at, 0, 0, lambda pick: dw[old, pick])
            return
        copy(0, at, 0).wait_recv()
        partner, place = (2, 1) if kind == "far" else (1, 0)
        pass_on(1, at, partner, place, lambda pick: dw[old, 2 * pick + bits[0]] + r0[at, pick].astype(high))

    def later(step, at, kind):
        copy(step - 1, at, 0).wait_recv()
        old = at % keeps[step - 1].shape[0]
        partner, place = ((3, 1) if step == 2 else (1, 0)) if kind == "far" else (step, 0)
        pass_on(step, at, partner, place, lambda pick: keeps[step - 1][old, pick] + recvs[step - 1][at, pick].astype(high))

    def finish(turn):
        copy(levels - 1, turn, levels - 1).wait_recv()
        old = turn % keeps[levels - 1].shape[0]
        value = keeps[levels - 1][old, 0] + recvs[levels - 1][turn, 0].astype(high)
        at = place_of(turn)

        def columns(first):
            return pl.ds(pl.multiple_of((at - first) * cols, cols), cols)

        @pl.when(at < 9)
        def _():
            out_in[0, :, columns(0)] = value

        @pl.when(jnp.logical_and(at >= 9, at < 12))
        def _():
            out_out[0, :, columns(9)] = value

        @pl.when(jnp.logical_and(at >= 12, at < 24))
        def _():
            out_up[0, :, columns(12)] = value

        @pl.when(at >= 24)
        def _():
            part, col = (at - 24) // 3, at % 3
            out_down[0, pl.ds(pl.multiple_of(part * rows, rows), rows), pl.ds(pl.multiple_of(col * cols, cols), cols)] = value

    def small_fill():
        heads = tables.shape[0]
        for part in range(2**levels):
            for head in range(heads):
                ks[part, 2 * head : 2 * head + 2] = tables[head, 2 * part : 2 * part + 2]
            ks[part, 2 * heads : 2 * heads + 8, 0:rows] = vectors[:, part * rows : (part + 1) * rows]
            for piece in range(4):
                at = (4 * part + piece) * rows
                ks[part, 2 * heads + piece : 2 * heads + piece + 1, rows : 2 * rows] = bias_grad[:, at : at + rows]

    def small_stage(step):
        if step:
            small_copy(step - 1).wait_recv()
        if step == levels:
            heads = tables.shape[0]
            ks[0] = skeeps[levels - 1][0] + srecvs[levels - 1][0]
            for axis in range(3):
                for i in range(2):
                    got = ks[0, pl.ds(i, heads, 2), :]
                    out_tables[axis, :, 0, i * BUCKETS : (i + 1) * BUCKETS] = got[:, axis * BUCKETS : (axis + 1) * BUCKETS]
            out_gains[0] = ks[0, 2 * heads : 2 * heads + 2, 0:rows]
            out_offsets[:, 0] = ks[0, 2 * heads + 2 : 2 * heads + 8, 0:rows]
            for piece in range(4):
                out_bias[:, piece * rows : (piece + 1) * rows] = ks[0, 2 * heads + piece : 2 * heads + piece + 1, rows : 2 * rows]
            return
        half = 2 ** (levels - 1 - step)

        def total(pick):
            if step == 0:
                return ks[pick]
            return skeeps[step - 1][2 * pick + bits[0] if step == 1 else pick] + srecvs[step - 1][pick]

        for j in range(half):
            ssends[step][j] = total(2 * j + 1 - bits[step])
        small_copy(step).start()
        if step:
            for j in range(half):
                skeeps[step][j] = total(2 * j + bits[step])

    def step_at(moment, carry):
        @pl.when(moment == 5)
        def _():
            cross_load.wait()

        @pl.when(jnp.logical_and(moment >= 5, moment < 5 + tables.shape[0]))
        def _():
            cross_head(moment - 5)

        def due(at):
            return jnp.logical_and(at >= 0, at < count)

        @pl.when(due(moment))
        def _():
            start(moment)

        for step in range(1, levels + 1):
            near_at, pair_at = moment - lags[0][step], moment - lags[1][step]
            plain_due = jnp.logical_and(due(near_at), jnp.logical_not(paired(near_at)))
            pair_due = jnp.logical_and(due(pair_at), paired(pair_at))
            if step == 1:
                @pl.when(pair_due)
                def _():
                    second(pair_at, "paired")
            elif step < levels:
                @pl.when(pair_due)
                def _():
                    later(step, pair_at, "paired")
            else:
                @pl.when(pair_due)
                def _():
                    finish(pair_at)

                @pl.when(plain_due)
                def _():
                    finish(near_at)
                continue
            for kind in ("plain", "far"):
                chosen = far_first(near_at) if kind == "far" else jnp.logical_not(far_first(near_at))

                @pl.when(jnp.logical_and(plain_due, chosen))
                def _():
                    second(near_at, kind) if step == 1 else later(step, near_at, kind)
        return carry

    ks[...] = jnp.zeros_like(ks)
    lax.fori_loop(0, 19, step_at, 0)
    small_fill()
    small_stage(0)
    lax.fori_loop(19, 22, step_at, 0)
    small_stage(1)
    lax.fori_loop(22, count, step_at, 0)
    small_stage(2)
    small_stage(3)
    small_stage(4)
    lax.fori_loop(count, count + lags[0][levels], step_at, 0)

    def drain(at, carry):
        @pl.when(jnp.logical_not(paired(at)))
        def _():
            copy(0, at, 0).wait_send()

        for step in range(1, levels):
            copy(step, at, step).wait_send()
        return carry

    lax.fori_loop(0, count, drain, 0)
    for step in range(levels):
        small_copy(step).wait_send()


def reduce_grads(plain, pair, full, right, cross, near_branch, buckets, vectors, bias_grad, count=36, levels=4, lags=LAGS):
    n = 2**levels
    depth, total = right.shape
    width = vectors.shape[1]
    cols, rows = 256, width // n
    heads = cross.shape[1] // (2 * LANES)
    ff = bias_grad.shape[1]
    others = total // cols - width // cols

    def ring(step):
        return max(lag[step + 1] for lag in lags) - min(lag[step] for lag in lags) + 1

    VM = pltpu.VMEM
    scratch = [VM((3, width, depth), low), VM(pair.shape, low), VM(full.shape, low)]
    scratch += [VM((others, depth, cols), low), VM((width // cols, 2 * depth, cols), low)]
    scratch += [VM(cross.shape, low), VM((heads, BUCKETS, LANES), high)]
    scratch += [VM((ring(0), n, rows, cols), high)]
    scratch += [VM((ring(step), n >> (step + 1), rows, cols), high) for step in (1, 2, 3)]
    scratch += [VM((count, n >> (step + 1), rows, cols), low) for step in range(4)] * 2
    scratch += [pltpu.SemaphoreType.DMA((levels, count))] * 2
    scratch += [pltpu.SemaphoreType.DMA((3,)), pltpu.SemaphoreType.DMA((others,))]
    scratch += [pltpu.SemaphoreType.DMA((ff // width,)), pltpu.SemaphoreType.DMA((2, width // cols)), pltpu.SemaphoreType.DMA]
    few = (2 * heads + 8, LANES)
    scratch += [VM((n,) + few, high)]
    scratch += [VM((n >> (step + 1),) + few, high) for step in (1, 2, 3)]
    scratch += [VM((n >> (step + 1),) + few, high) for step in range(4)] * 2
    scratch += [pltpu.SemaphoreType.DMA((levels,))] * 2
    here, there = pl.BlockSpec(memory_space=pltpu.VMEM), pl.BlockSpec(memory_space=pl.ANY)
    shapes = (
        (1, rows, 3 * width), (1, rows, width), (1, rows, ff), (1, ff // n, width),
        (3, heads, 1, 2 * BUCKETS), (1, 2, rows), (6, 1, rows), (1, ff // n),
    )
    return pl.pallas_call(
        functools.partial(rs_kernel, count, levels, rows, cols, lags),
        out_shape=tuple(jax.ShapeDtypeStruct(shape, high) for shape in shapes),
        in_specs=[there] * 6 + [here] * 3,
        out_specs=(here,) * len(shapes),
        scratch_shapes=scratch,
        compiler_params=pltpu.CompilerParams(
            collective_id=1, has_side_effects=True, vmem_limit_bytes=63 * 2**20),
    )(plain, pair, full, right, cross, near_branch, buckets, vectors, bias_grad)


def settle_kernel(count, *refs):
    sources, targets, held, sem = refs[:count], refs[count : 2 * count], refs[2 * count : 3 * count], refs[3 * count]
    copies = [
        (pltpu.make_async_copy(sources[at], held[at], sem.at[0, at]), pltpu.make_async_copy(held[at], targets[at], sem.at[1, at]))
        for at in range(count)
    ]
    for fetch, _ in copies:
        fetch.start()
    for fetch, put in copies:
        fetch.wait()
        put.start()
    for _, put in copies:
        put.wait()


def settle(arrays):
    there = pl.BlockSpec(memory_space=pl.ANY)
    return pl.pallas_call(
        functools.partial(settle_kernel, len(arrays)),
        out_shape=tuple(jax.ShapeDtypeStruct(array.shape, array.dtype) for array in arrays),
        in_specs=[there] * len(arrays),
        out_specs=(there,) * len(arrays),
        scratch_shapes=[pltpu.VMEM(array.shape, array.dtype) for array in arrays] + [pltpu.SemaphoreType.DMA((2, len(arrays)))],
        compiler_params=pltpu.CompilerParams(vmem_limit_bytes=63 * 2**20),
    )(*arrays)


def local(tokens, cotangent, lengths, buckets, in_proj, out_proj, up_proj, down_proj, layout_tables, norm_gains, offsets, hidden_bias):
    heads = layout_tables.shape[2]
    width, ff = up_proj.shape[1:]
    shifts = jnp.transpose(offsets, (1, 0, 2))
    params = (in_proj[0], out_proj[0], up_proj[0], down_proj[0], norm_gains[0], shifts, hidden_bias, heads)
    wide_count = lax.axis_size("wide")
    result, input_grads, plain, pair, full, right, cross, vectors, bias_grad, near_branch = both_passes(
        tokens, cotangent, lengths, buckets, layout_tables[0], params, wide_count == 16)
    share = width // wide_count
    if wide_count == 16 and share % 16 == 0:
        found = reduce_grads(plain, pair, full, right, cross, near_branch, buckets, vectors, bias_grad)
        found = settle((result[None], input_grads[None]) + found)
        return found[:6] + (jnp.transpose(found[6], (2, 0, 1, 3)), found[7], jnp.transpose(found[8], (1, 0, 2)), found[9])
    else:

        def scattered(value, dim):
            return lax.psum_scatter(value[None], "wide", scatter_dimension=dim, tiled=True)

        def product(rows_from, cols_from, cols):
            return dot_nn(plain[rows_from : rows_from + width], right[:, cols_from : cols_from + cols])

        grad_in = scattered(product(0, 0, 3 * width), 1)
        grad_out = scattered(product(width, 3 * width, width), 1)
        grad_up = scattered(product(2 * width, 4 * width, ff), 1)
        grad_down = dot_nn(full.reshape(ff, -1), right[:, 4 * width + ff :])
        grad_down = grad_down.reshape(ff // width, 16, -1, width).transpose(1, 0, 2, 3).reshape(ff, width)
        grad_down = scattered(grad_down, 1)
        grad_hidden = scattered(bias_grad[0], 1)
        turned = marks_of(buckets)
        tables = jnp.stack([
            cross_tables(turned, cross[:, 2 * head * LANES : 2 * (head + 1) * LANES]) for head in range(heads)])
        tables = tables[:, :, : 3 * BUCKETS].reshape(heads, BUCKETS, 3, BUCKETS).transpose(2, 0, 1, 3)
        grad_tables = scattered(tables.reshape(3, heads, -1), 3)
        vectors = scattered(vectors, 2)
        grad_gains, grad_offsets = vectors[:, :2], vectors[:, 2:]
    return (
        result[None],
        input_grads[None],
        grad_in,
        grad_out,
        grad_up,
        grad_down,
        grad_tables,
        grad_gains,
        grad_offsets,
        grad_hidden,
    )


def solution(mesh):
    placed = (
        P("wide", None),
        P("wide", None),
        P("wide"),
        P(None, "wide"),
        P("section", None, None),
        P("section", None, None),
        P("section", None, None),
        P("section", None, None),
        P("section", None, None, None),
        P("section", None, None),
        P("section", None, None),
        P("section", None),
    )
    return jax.shard_map(
        local,
        mesh=mesh,
        in_specs=placed,
        out_specs=(
            P("section", "wide", None),
            P("section", "wide", None),
            P("section", "wide", None),
            P("section", "wide", None),
            P("section", "wide", None),
            P("section", "wide", None),
            P("section", None, None, "wide"),
            P("section", None, "wide"),
            P("section", None, "wide"),
            P("section", "wide"),
        ),
        check_vma=False,
    )
```
